128 devices in a mesh: pool: 16 (over y, x), tp: 8 (over z, core).
Axes of the slice: x: 4, y: 4, z: 4, core: 2. Of those that a mesh axis runs over, the one named last changes fastest.
Arguments:
- prompt_latent: bfloat16 [512, 384, 576], P('pool'), may hold values from -4 to 4
- prompt_lengths: int32 [512], replicated, may hold values from 192 to 384, as said below
- decode_slot: int32 [512], replicated, may hold values from 0 to 511, as said below
- new_latent: bfloat16 [4, 512, 576], P(None, 'pool'), may hold values from -4 to 4
- queries: bfloat16 [4, 512, 64, 192], P(None, 'pool', 'tp'), may hold values from -48 to 48
- w_uk: bfloat16 [64, 512, 128], P('tp'), may hold values from -0.25 to 0.25
- w_uv: bfloat16 [64, 512, 128], P('tp'), may hold values from -1.5 to 1.5
- w_out: bfloat16 [8192, 2560], P('tp'), may hold values from -0.0625 to 0.0625
Outputs:
- decoded: bfloat16 [512, 4, 2560], P('pool')
- context: bfloat16 [512, 384, 576], P('pool', 'tp')
The draws below stay inside these ranges and needn't reach their ends.
Inputs may be any that keep to these rules, and one draw needn't show every extreme that they name: `prompt_lengths`: each block of 32 consecutive prefill slots holds a prompt of exactly 384 rows and one of exactly 192 rows. `decode_slot`: a one-to-one map of prefill slots onto decode slots; prefill slot g belongs to prefill owner g // 32 and decode slot i to decode owner i // 32; of one prefill owner's 32 slots at most 4 go to any one decode owner, and exactly 4 go to one of them.
All inputs are finite; a program needn't handle non-finite values.
Results may differ from the reference program's by a relative error of at most 0.02.
Values may be sent and summed in bfloat16 or wider, within the bound.
No kernel may reach another device: no remote copies, remote signals or barrier semaphores. Data moves between devices by JAX's collectives and lax.ppermute only.
A program may use at most 192 MiB of HBM per device.

```python
import math
import jax
import jax.numpy as jnp
from jax import lax

LATENT_WIDTH = 512
ROPE = 64
NOPE = 128
VDIM = 128
HEADS = 64
D_OUT = 2560
STEPS = 4
REQ_DEV = 32
L_MAX = 384
CAP = 4
REQUESTS = 512


def draw_prompt_latent(key, part):
    key = jax.random.fold_in(key, 11)
    first = jax.random.fold_in(key, 0)
    values = jnp.clip(jax.random.normal(first, (REQUESTS, L_MAX, LATENT_WIDTH + ROPE), jnp.float32), -4.0, 4.0)
    return values.astype(jnp.bfloat16)


def draw_new_latent(key, part):
    key = jax.random.fold_in(key, 12)
    first = jax.random.fold_in(key, 0)
    values = jnp.clip(jax.random.normal(first, (STEPS, REQUESTS, LATENT_WIDTH + ROPE), jnp.float32), -4.0, 4.0)
    return values.astype(jnp.bfloat16)


def draw_queries(key, part):
    key = jax.random.fold_in(key, 13)
    subkeys = jax.random.split(key, 1)
    values = jnp.clip(jax.random.normal(subkeys[0], (STEPS, REQUESTS, HEADS, NOPE + ROPE), jnp.float32), -4.0, 4.0)
    return values.astype(jnp.bfloat16)


def draw_prompt_lengths(key, part):
    key = jax.random.fold_in(key, 17)
    subkeys = jax.random.split(key, 3)
    owners = REQUESTS // REQ_DEV
    drawn = jax.random.randint(subkeys[1], (REQUESTS,), L_MAX // 2, L_MAX + 1)
    offset = jax.random.randint(subkeys[2], (owners,), 0, REQ_DEV)
    base = jnp.arange(owners) * REQ_DEV
    longest = offset + base
    shortest = (offset + 1) % REQ_DEV + base
    rows = jnp.arange(REQUESTS)
    is_long = jnp.any(rows[:, None] == longest[None, :], axis=1)
    is_short = jnp.any(rows[:, None] == shortest[None, :], axis=1)
    result = jnp.where(is_long, L_MAX, jnp.where(is_short, L_MAX // 2, drawn))
    return result.astype(jnp.int32)


def draw_decode_slot(key, part):
    key = jax.random.fold_in(key, 19)
    subkeys = jax.random.split(key, 4)
    owners = REQUESTS // REQ_DEV
    shift_base = jax.random.permutation(subkeys[0], owners)
    owner_order = jax.random.permutation(subkeys[1], owners)
    sender_order = jax.vmap(lambda subkey: jax.random.permutation(subkey, REQ_DEV))(jax.random.split(subkeys[2], owners))
    receiver_order = jax.vmap(lambda subkey: jax.random.permutation(subkey, REQ_DEV))(jax.random.split(subkeys[3], owners))
    stride = -(-(REQ_DEV - CAP) // (owners - 1))
    column = jnp.arange(REQ_DEV)
    shift_index = jnp.where(column < CAP, 0, 1 + (column - CAP) // stride)
    shifts = shift_base[shift_index]
    senders = jnp.arange(owners)[:, None]
    picked = sender_order
    target = owner_order[(senders + shifts[picked]) % owners]
    inner_slot = receiver_order[target, picked]
    return (target * REQ_DEV + inner_slot).reshape(-1).astype(jnp.int32)


def block_scale(stream_key, extent, cuts, least, high):
    def one(axis_at, parts):
        heights = jax.random.uniform(jax.random.fold_in(jax.random.fold_in(stream_key, 6), axis_at), (parts,), jnp.float32, least / len(cuts), high / len(cuts))
        return jnp.repeat(jnp.exp(heights), extent[axis_at] // parts).reshape((-1,) + (1,) * (len(extent) - axis_at - 1))

    level = one(*cuts[0])
    for cut in cuts[1:]:
        level = level * one(*cut)
    return level


def noise(stream_key, extent, deviation, bound, shards=(), kind=jnp.bfloat16):
    entries = deviation * jax.random.normal(stream_key, extent, jnp.float32)
    if shards:
        entries = entries * block_scale(stream_key, extent, shards, -0.22, 0.18)
    return jnp.clip(entries, -bound, bound).astype(kind)


def setup_inputs(seed: int = 0) -> dict:
    splits = jax.random.split(jax.random.key(seed), 9)
    prompt_latent = draw_prompt_latent(jax.random.fold_in(splits[8], 71), 0)
    prompt_lengths = draw_prompt_lengths(jax.random.fold_in(splits[8], 71), 0)
    decode_slot = draw_decode_slot(jax.random.fold_in(splits[8], 71), 0)
    new_latent = draw_new_latent(jax.random.fold_in(splits[8], 71), 0)
    queries = draw_queries(jax.random.fold_in(splits[8], 71), 0)
    w_uk = noise(splits[5], (HEADS, LATENT_WIDTH, NOPE), LATENT_WIDTH ** -0.5, 0.25, ((0, 8),))
    w_uv = noise(splits[6], (HEADS, LATENT_WIDTH, VDIM), (LATENT_WIDTH // 32) ** -0.5, 1.5, ((0, 8),))
    w_out = noise(splits[7], (HEADS * VDIM, D_OUT), (HEADS * VDIM) ** -0.5, 0.0625, ((0, 8),))
    return {"prompt_latent": prompt_latent, "prompt_lengths": prompt_lengths, "decode_slot": decode_slot, "new_latent": new_latent, "queries": queries, "w_uk": w_uk, "w_uv": w_uv, "w_out": w_out}


floor_score = -1e+30

def reference(prompt_latent, prompt_lengths, decode_slot, new_latent, queries, w_uk, w_uv, w_out):
    request_count = decode_slot.shape[0]
    owner_slot = jnp.zeros((request_count,), jnp.int32).at[decode_slot].set(jnp.arange(request_count, dtype=jnp.int32))
    score_scale = 1.0 / math.sqrt(NOPE + ROPE)
    block_count = request_count // REQ_DEV

    def one_block(block_index):
        first_row = (block_index * REQ_DEV).astype(jnp.int32)
        prefill_rows = lax.dynamic_slice_in_dim(owner_slot, first_row, REQ_DEV)
        context_length = jnp.take(prompt_lengths, prefill_rows, axis=0)
        raw_context = jnp.take(prompt_latent, prefill_rows, axis=0)
        row_valid = jnp.arange(L_MAX, dtype=jnp.int32)[None, :] < context_length[:, None]
        context = jnp.where(row_valid[..., None], raw_context, jnp.zeros((), raw_context.dtype))
        fresh_rows = lax.dynamic_slice_in_dim(new_latent, first_row, REQ_DEV, 1)
        query_rows = lax.dynamic_slice_in_dim(queries, first_row, REQ_DEV, 1)
        absorbed = jnp.einsum('sbhn,hcn->bshc', query_rows[..., :NOPE].astype(jnp.float32), w_uk.astype(jnp.float32)).astype(jnp.bfloat16)
        absorbed = lax.optimization_barrier(absorbed)
        rotary = jnp.transpose(query_rows[..., NOPE:], (1, 0, 2, 3))
        complete_query = jnp.concatenate([absorbed, rotary], axis=-1).reshape(REQ_DEV, STEPS * HEADS, LATENT_WIDTH + ROPE)
        key_row_block = jnp.concatenate([context, jnp.transpose(fresh_rows, (1, 0, 2))], axis=1)
        logit_scores = jnp.einsum('oiz,oaz->oia', complete_query.astype(jnp.float32), key_row_block.astype(jnp.float32)) * score_scale
        position = jnp.arange(L_MAX + STEPS, dtype=jnp.int32)
        step_of = jnp.arange(STEPS * HEADS, dtype=jnp.int32) // HEADS
        fresh_ok = (position[None, :] >= L_MAX) & (position[None, :] - L_MAX <= step_of[:, None])
        allowed = (position[None, None, :] < context_length[:, None, None]) | fresh_ok[None, :, :]
        peak = lax.optimization_barrier(jnp.max(jnp.where(allowed, logit_scores, floor_score), axis=-1, keepdims=True))
        weights = jnp.where(allowed, jnp.exp(logit_scores - peak), 0.0)
        softmax_totals = lax.optimization_barrier(jnp.sum(weights, axis=-1))
        rounded_weight_matrix = lax.optimization_barrier(weights.astype(jnp.bfloat16))
        weighted_latent = jnp.einsum('xmf,xfo->xmo', rounded_weight_matrix.astype(jnp.float32), key_row_block[..., :LATENT_WIDTH].astype(jnp.float32)) / softmax_totals[..., None]
        weighted_latent = lax.optimization_barrier(weighted_latent.astype(jnp.bfloat16)).reshape(REQ_DEV, STEPS, HEADS, LATENT_WIDTH)
        head_out = jnp.einsum('bshc,hcv->bshv', weighted_latent.astype(jnp.float32), w_uv.astype(jnp.float32)).astype(jnp.bfloat16)
        decoded = jnp.dot(head_out.reshape(REQ_DEV * STEPS, HEADS * VDIM), w_out, preferred_element_type=jnp.float32)
        return (decoded.astype(jnp.bfloat16).reshape(REQ_DEV, STEPS, D_OUT), context)
    stacked, contexts = lax.map(one_block, jnp.arange(block_count, dtype=jnp.int32))
    return (stacked.reshape(request_count, STEPS, D_OUT), contexts.reshape(request_count, L_MAX, LATENT_WIDTH + ROPE))
```

```python
import math

import jax
import jax.numpy as jnp
from jax import lax
from jax.sharding import PartitionSpec as P

ROPE = 64
NOPE = 128
CAP = 4
FIRST_RANKS = 3
FLOOR = -1e30


def route(decode_slot, pool_index, pool_count, slot_count):
    targets = decode_slot // slot_count
    by_source = targets.reshape(pool_count, slot_count)
    earlier = jnp.tril(jnp.ones((slot_count, slot_count), jnp.int32), -1)
    own = lax.dynamic_slice_in_dim(by_source, pool_index, 1, 0)[0]
    same = (own[:, None] == own[None, :]).astype(jnp.int32)
    placing = own * CAP + jnp.sum(same * earlier, axis=1)
    cells = jnp.arange(pool_count * CAP)
    source_row = jnp.sum(
        jnp.where(placing[None, :] == cells[:, None], jnp.arange(slot_count)[None, :], 0), axis=1
    )
    arriving = (by_source == pool_index).astype(jnp.int32)
    before = jnp.cumsum(arriving, axis=1) - arriving
    cell = (jnp.arange(pool_count)[:, None] * CAP + before).reshape(-1)
    wanted = pool_index * slot_count + jnp.arange(slot_count)
    match = decode_slot[None, :] == wanted[:, None]
    arrival = jnp.sum(jnp.where(match, cell[None, :], 0), axis=1)
    decode_row = jnp.sum(
        jnp.where(arrival[None, :] == cells[:, None], jnp.arange(slot_count)[None, :], 0), axis=1
    )
    return placing, source_row, arrival, decode_row, match


def body(prompt_latent, prompt_lengths, decode_slot, new_latent, queries, w_uk, w_uv, w_out):
    pool_count = lax.axis_size("pool")
    tp_count = lax.axis_size("tp")
    pool_index = lax.axis_index("pool")
    tp_index = lax.axis_index("tp")
    steps, slots, heads, width = queries.shape
    span, feature = prompt_latent.shape[1:]
    piece = span // tp_count
    latent = w_uk.shape[1]
    out_width = w_out.shape[1]
    cells = pool_count * CAP
    placing, source_row, arrival, decode_row, match = route(
        decode_slot, pool_index, pool_count, slots
    )
    decode_lengths = jnp.sum(jnp.where(match, prompt_lengths[None, :], 0), axis=1)
    own_lengths = lax.dynamic_slice_in_dim(prompt_lengths, pool_index * slots, slots)

    q_out = jnp.take(queries, decode_row, axis=1).transpose(1, 0, 2, 3).reshape(cells, -1)
    n_out = jnp.take(new_latent, decode_row, axis=1).transpose(1, 0, 2).reshape(cells, -1)
    payload = jnp.concatenate([q_out, n_out], axis=1).reshape(pool_count, -1, 128)
    payload = lax.all_to_all(payload, "pool", split_axis=0, concat_axis=0, tiled=True)

    own_piece = lax.dynamic_slice_in_dim(prompt_latent, tp_index * piece, piece, 1)
    sending = jnp.take(own_piece, source_row, axis=0).reshape(
        pool_count, CAP, piece, feature
    )
    payload, first_send = lax.optimization_barrier((payload, sending[:, :FIRST_RANKS]))
    first = lax.all_to_all(first_send, "pool", split_axis=0, concat_axis=0, tiled=True)

    payload = jnp.take(payload.reshape(cells, -1), placing, axis=0)
    q_size = steps * heads * width
    q = payload[:, :q_size].reshape(slots, steps, heads, width)
    fresh = payload[:, q_size:].reshape(slots, steps, feature)

    absorbed = jnp.einsum(
        "rshn,hcn->rshc", q[..., :NOPE], w_uk, preferred_element_type=jnp.float32
    ).astype(jnp.bfloat16)
    full_q = jnp.concatenate([absorbed, q[..., NOPE:]], axis=-1).reshape(
        slots, steps * heads, feature
    )
    scale = 1.0 / math.sqrt(width)
    step_of = jnp.arange(steps * heads, dtype=jnp.int32) // heads
    s_prompt = scale * jnp.einsum(
        "rqc,rkc->rqk", full_q, prompt_latent, preferred_element_type=jnp.float32
    )
    s_fresh = scale * jnp.einsum(
        "rqc,rkc->rqk", full_q, fresh, preferred_element_type=jnp.float32
    )
    ok_prompt = jnp.arange(span)[None, None, :] < own_lengths[:, None, None]
    ok_fresh = (jnp.arange(steps)[None, :] <= step_of[:, None])[None]
    s_prompt = jnp.where(ok_prompt, s_prompt, FLOOR)
    s_fresh = jnp.where(ok_fresh, s_fresh, FLOOR)
    peak = jnp.maximum(jnp.max(s_prompt, -1), jnp.max(s_fresh, -1))[..., None]
    w_prompt = jnp.exp(s_prompt - peak)
    w_fresh = jnp.exp(s_fresh - peak)
    totals = jnp.sum(w_prompt, -1) + jnp.sum(w_fresh, -1)
    mixed = jnp.einsum(
        "rqk,rkc->rqc",
        w_prompt.astype(jnp.bfloat16),
        prompt_latent[..., :latent],
        preferred_element_type=jnp.float32,
    ) + jnp.einsum(
        "rqk,rkc->rqc",
        w_fresh.astype(jnp.bfloat16),
        fresh[..., :latent],
        preferred_element_type=jnp.float32,
    )
    mixed = (mixed / totals[..., None]).astype(jnp.bfloat16)
    mixed = mixed.reshape(slots, steps, heads, latent)
    head_out = jnp.einsum(
        "rshc,hcv->srhv", mixed, w_uv, preferred_element_type=jnp.float32
    ).astype(jnp.bfloat16)
    partial = jnp.dot(
        head_out.reshape(steps * slots, -1), w_out, preferred_element_type=jnp.float32
    )

    core = tp_index % 2
    z = tp_index // 2
    z_count = tp_count // 2
    half = steps * slots // 2
    block = out_width // z_count
    swap = [(i, i ^ 1) for i in range(tp_count)]

    def hop(d):
        return [(i, i ^ (2 * d)) for i in range(tp_count)]

    kept = lax.dynamic_slice_in_dim(partial, core * half, half, 0)
    given = lax.dynamic_slice_in_dim(partial, (1 - core) * half, half, 0).astype(jnp.bfloat16)
    pair = kept + lax.ppermute(given, "tp", swap).astype(jnp.float32)
    mine = lax.dynamic_slice_in_dim(pair, z * block, block, 1)
    pair16 = pair.astype(jnp.bfloat16)
    got = [
        lax.ppermute(
            lax.dynamic_slice_in_dim(pair16, (z ^ d) * block, block, 1), "tp", hop(d)
        )
        for d in range(1, z_count)
    ]
    for part in got:
        mine = mine + part.astype(jnp.float32)
    mine = mine.astype(jnp.bfloat16).reshape(steps // 2, slots, block)

    back = jnp.take(mine, source_row, axis=1).transpose(1, 0, 2)
    back = back.reshape(pool_count, CAP * steps // 2, block)
    back, first = lax.optimization_barrier((back, first))
    back = lax.all_to_all(back, "pool", split_axis=0, concat_axis=0, tiled=True)
    back, second_send = lax.optimization_barrier((back, sending[:, FIRST_RANKS:]))
    second = lax.all_to_all(second_send, "pool", split_axis=0, concat_axis=0, tiled=True)

    back = jnp.take(back.reshape(cells, steps // 2, block), arrival, axis=0)
    parts = jnp.stack([back] + [lax.ppermute(back, "tp", hop(d)) for d in range(1, z_count)])
    parts = jnp.take(parts, jnp.arange(z_count) ^ z, axis=0)
    row_half = parts.transpose(1, 2, 0, 3).reshape(slots, steps // 2, out_width)
    other_half = lax.ppermute(row_half, "tp", swap)
    decoded = jnp.concatenate(
        [
            jnp.where(core == 0, row_half, other_half),
            jnp.where(core == 0, other_half, row_half),
        ],
        axis=1,
    )

    owner, rank = arrival // CAP, arrival % CAP
    both = jnp.concatenate([first, second], axis=1).reshape(cells, piece, feature)
    context = jnp.take(both, owner * CAP + rank, axis=0)
    position = tp_index * piece + jnp.arange(piece, dtype=jnp.int32)
    valid = position[None, :] < decode_lengths[:, None]
    context = jnp.where(valid[..., None], context, jnp.zeros((), context.dtype))
    return decoded, context


def solution(mesh):
    in_specs = (
        P("pool", None, None),
        P(),
        P(),
        P(None, "pool", None),
        P(None, "pool", "tp", None),
        P("tp", None, None),
        P("tp", None, None),
        P("tp", None),
    )
    out_specs = (P("pool", None, None), P("pool", "tp", None))
    return jax.shard_map(body, mesh=mesh, in_specs=in_specs, out_specs=out_specs, check_vma=False)
```

```python
import functools
import math

import jax
import jax.numpy as jnp
from jax import lax
from jax.experimental import pallas as pl
from jax.experimental.pallas import tpu as pltpu
from jax.sharding import PartitionSpec as P

ROPE = 64
NOPE = 128
CAP = 4
FIRST_RANKS = 3
GROUP = 2
FLOOR = -1e30
BF16 = jnp.bfloat16
F32 = jnp.float32

VMEM_LIMIT = 48 * 1024 * 1024
SMEM_SPEC = pl.BlockSpec(memory_space=pltpu.SMEM)
VMEM_SPEC = pl.BlockSpec(memory_space=pltpu.VMEM)
ANY_SPEC = pl.BlockSpec(memory_space=pl.ANY)
NT = (((1,), (1,)), ((), ()))


def params(**kw):
    return pltpu.CompilerParams(vmem_limit_bytes=VMEM_LIMIT, **kw)


def cost(flops=1000, bytes_accessed=1000):
    return pl.CostEstimate(flops=flops, bytes_accessed=bytes_accessed, transcendentals=0)


def route(decode_slot, pool_index, pool_count, slot_count):
    targets = decode_slot // slot_count
    by_source = targets.reshape(pool_count, slot_count)
    earlier = jnp.tril(jnp.ones((slot_count, slot_count), jnp.int32), -1)
    own = lax.dynamic_slice_in_dim(by_source, pool_index, 1, 0)[0]
    same = (own[:, None] == own[None, :]).astype(jnp.int32)
    placing = own * CAP + jnp.sum(same * earlier, axis=1)
    arriving = (by_source == pool_index).astype(jnp.int32)
    before = jnp.cumsum(arriving, axis=1) - arriving
    cell = (jnp.arange(pool_count)[:, None] * CAP + before).reshape(-1)
    wanted = pool_index * slot_count + jnp.arange(slot_count)
    match = decode_slot[None, :] == wanted[:, None]
    arrival = jnp.sum(jnp.where(match, cell[None, :], 0), axis=1)
    return placing, arrival, match


def pack_queries_kernel(arrival, q_ref, n_ref, out_ref, new_rows, tails):
    steps, slots, heads, width = q_ref.shape
    rows = steps * heads
    blocks = n_ref.shape[2] // 128
    new_rows[...] = n_ref[...].astype(F32)
    tails[...] = jnp.zeros(tails.shape, F32)

    def one(j, carry):
        dest, rank = arrival[j] // CAP, arrival[j] % CAP
        x = q_ref[:, j].astype(F32)
        nope = x[:, :, :NOPE].reshape(rows, NOPE)
        rope = x[:, :, NOPE:].reshape(rows, ROPE)
        rope = jnp.concatenate([rope[: rows // 2], rope[rows // 2 :]], axis=1)
        fresh = jnp.concatenate([new_rows[s, pl.ds(j, 1), :] for s in range(steps)], axis=0)
        body = [fresh[:, 128 * b : 128 * b + 128] for b in range(blocks)]
        last = fresh[:, 128 * blocks :]
        cell = jnp.concatenate([nope, rope] + body, axis=0)
        out_ref[dest, pl.ds(pl.multiple_of(rank * 64, 64), 64), :] = cell.astype(BF16)
        tails[pl.ds(dest * 8 + rank * 2, 2), :] = jnp.concatenate(
            [last[: steps // 2], last[steps // 2 :]], axis=1
        )
        return carry

    lax.fori_loop(0, slots, one, 0)
    out_ref[:, 256:264, :] = tails[...].reshape(out_ref.shape[0], 8, 128).astype(BF16)


def pack_queries(arrival, queries, new_latent, pool_count):
    return pl.pallas_call(
        pack_queries_kernel,
        out_shape=jax.ShapeDtypeStruct((pool_count, 264, 128), BF16),
        in_specs=[SMEM_SPEC, VMEM_SPEC, VMEM_SPEC],
        out_specs=VMEM_SPEC,
        scratch_shapes=[
            pltpu.VMEM(new_latent.shape, F32),
            pltpu.VMEM((pool_count * 8, 128), F32),
        ],
        compiler_params=params(),
        cost_estimate=cost(),
        name="pack_queries",
    )(arrival, queries, new_latent)


def pack_context_kernel(placing, where, p_ref, first_ref, second_ref, buf, sems):
    slots, piece, feature = buf.shape
    blocks = feature // 128
    chunk = slots // sems.shape[0]
    start = pl.multiple_of(where[0] * piece, 16)
    copies = [
        pltpu.make_async_copy(
            p_ref.at[pl.ds(k * chunk, chunk), pl.ds(start, piece), :],
            buf.at[pl.ds(k * chunk, chunk)],
            sems.at[k],
        )
        for k in range(sems.shape[0])
    ]
    for copy in copies:
        copy.start()
    for k, copy in enumerate(copies):
        copy.wait()

        def one(n, carry):
            g = k * chunk + n
            dest, rank = placing[g] // CAP, placing[g] % CAP

            def put(ref, at):
                for b in range(blocks):
                    ref[(*at, pl.ds(b * piece, piece), slice(None))] = buf[
                        g, :, 128 * b : 128 * b + 128
                    ]
                last = buf[g, :, 128 * blocks :].astype(F32)
                last = jnp.concatenate([last[: piece // 2], last[piece // 2 :]], axis=1)
                ref[(*at, pl.ds(blocks * piece, piece // 2), slice(None))] = last.astype(BF16)

            @pl.when(rank < FIRST_RANKS)
            def _():
                put(first_ref, (dest, rank))

            @pl.when(rank >= FIRST_RANKS)
            def _():
                put(second_ref, (dest, rank - FIRST_RANKS))

            return carry

        lax.fori_loop(0, chunk, one, 0)


def pack_context(placing, where, prompt_latent, piece, pool_count):
    slots, _, feature = prompt_latent.shape
    rows = piece * feature // 128
    return pl.pallas_call(
        pack_context_kernel,
        out_shape=(
            jax.ShapeDtypeStruct((pool_count, FIRST_RANKS, rows, 128), BF16),
            jax.ShapeDtypeStruct((pool_count, CAP - FIRST_RANKS, rows, 128), BF16),
        ),
        in_specs=[SMEM_SPEC, SMEM_SPEC, ANY_SPEC],
        out_specs=(VMEM_SPEC, VMEM_SPEC),
        scratch_shapes=[
            pltpu.VMEM((slots, piece, feature), BF16),
            pltpu.SemaphoreType.DMA((4,)),
        ],
        compiler_params=params(),
        cost_estimate=cost(),
        name="pack_context",
    )(placing, where, prompt_latent)


def unpack_piece(packed, row, first_row, length, piece, feature):
    blocks = feature // 128
    parts = [packed[(*row, pl.ds(b * piece, piece), slice(None))] for b in range(blocks)]
    last = packed[(*row, pl.ds(blocks * piece, piece // 2), slice(None))].astype(F32)
    last = jnp.concatenate([last[:, :64], last[:, 64:]], axis=0).astype(BF16)
    whole = jnp.concatenate(parts + [last], axis=1)
    position = first_row + lax.broadcasted_iota(jnp.int32, whole.shape, 0)
    return jnp.where(position < length, whole.astype(F32), 0.0).astype(BF16)


def place_kernel(low, high, keep, arrival, lengths, where, packed, *rest):
    out_ref, inbox, outbox, in_sems, out_sems = rest[-5:]
    slots, piece, feature = out_ref.shape
    first_row = where[0] * piece

    def copy_in(j):
        owner, rank = arrival[j] // CAP, arrival[j] % CAP
        rank = jnp.clip(rank - low, 0, high - low - 1)
        return pltpu.make_async_copy(packed.at[owner, rank], inbox.at[j], in_sems.at[j])

    def copy_out(j):
        return pltpu.make_async_copy(outbox.at[j], out_ref.at[j], out_sems.at[j])

    def each(action):
        def step(j, carry):
            rank = arrival[j] % CAP

            @pl.when((rank >= low) & (rank < high))
            def _():
                action(j)

            return carry

        lax.fori_loop(0, slots, step, 0)

    def work(j):
        copy_in(j).wait()
        outbox[j] = unpack_piece(inbox, (j,), first_row, lengths[j], piece, feature)
        copy_out(j).start()

    each(lambda j: copy_in(j).start())
    each(work)
    each(lambda j: copy_out(j).wait())


def place(low, high, arrival, lengths, where, packed, piece, feature, context=None):
    slots = arrival.shape[0]
    rows = packed.shape[2]
    args = [arrival, lengths, where, packed] + ([] if context is None else [context])
    return pl.pallas_call(
        functools.partial(place_kernel, low, high, context is not None),
        out_shape=jax.ShapeDtypeStruct((slots, piece, feature), BF16),
        in_specs=[SMEM_SPEC] * 3 + [ANY_SPEC] * (len(args) - 3),
        out_specs=ANY_SPEC,
        scratch_shapes=[
            pltpu.VMEM((slots, rows, 128), BF16),
            pltpu.VMEM((slots, piece, feature), BF16),
            pltpu.SemaphoreType.DMA((slots,)),
            pltpu.SemaphoreType.DMA((slots,)),
        ],
        input_output_aliases={} if context is None else {4: 0},
        compiler_params=params(),
        cost_estimate=cost(),
        name="place_context",
    )(*args)


def attention_kernel(
    placing, lengths, where, payload, p_ref, w_uk, w_uv_hbm, w_out_hbm,
    given_ref, kept_ref,
    q_nope, q_rope, acc, fresh, tails, fresh_score, total, w_uv, w_out, head_out, sems,
):
    steps = 4
    heads, latent, nope = w_uk.shape
    group, span, feature = p_ref.shape
    slots = placing.shape[0]
    chunks = latent // 128
    per_step = slots * heads
    many = slots * steps
    scale = 1.0 / math.sqrt(nope + ROPE)
    at = pl.program_id(0)
    copy_uv = pltpu.make_async_copy(w_uv_hbm, w_uv, sems.at[0])
    copy_out = pltpu.make_async_copy(w_out_hbm, w_out, sems.at[1])

    def spread(ref, i, lead=()):
        return jnp.concatenate(
            [
                ref[(*lead, pl.ds(pl.multiple_of(per_step * s + heads * i, 8), heads), slice(None))]
                for s in range(steps)
            ],
            axis=0,
        )

    def collect(ref, i, value, lead=()):
        for s in range(steps):
            ref[(*lead, pl.ds(pl.multiple_of(per_step * s + heads * i, 8), heads), slice(None))] = (
                value[heads * s : heads * s + heads]
            )

    @pl.when(at == 0)
    def _():
        copy_uv.start()
        copy_out.start()
        tails[...] = payload[:, 256:264, :].astype(F32).reshape(tails.shape)

        def one(i, carry):
            dest, rank = placing[i] // CAP, placing[i] % CAP
            cell = payload[dest, pl.ds(pl.multiple_of(rank * 64, 64), 64), :].astype(F32)
            collect(q_nope, i, cell[:32])
            rope = jnp.concatenate([cell[32:48, :64], cell[32:48, 64:]], axis=0)
            collect(q_rope, i, jnp.concatenate([rope, jnp.zeros_like(rope)], axis=1))
            for b in range(chunks):
                fresh[b, pl.ds(steps * i, steps), :] = cell[48 + 4 * b : 52 + 4 * b]
            last = tails[pl.ds(dest * 8 + rank * 2, 2), :]
            last = jnp.concatenate([last[:, :64], last[:, 64:]], axis=0)
            fresh[chunks, pl.ds(steps * i, steps), :] = jnp.concatenate(
                [last, jnp.zeros_like(last)], axis=1
            )
            return carry

        lax.fori_loop(0, slots, one, 0)
        for h in range(heads):
            rows = pl.ds(h, many, stride=heads)
            a = lax.dot_general(
                q_nope[rows, :].astype(BF16), w_uk[h], NT, preferred_element_type=F32
            )
            a = a.astype(BF16).astype(F32)
            for c in range(chunks):
                acc[c, rows, :] = a[:, 128 * c : 128 * c + 128]
        keys = jnp.concatenate([fresh[b] for b in range(chunks + 1)], axis=1).astype(BF16)

        def score(k, carry):
            rows = pl.ds(pl.multiple_of(k * 128, 128), 128)
            q = jnp.concatenate(
                [acc[c, rows, :] for c in range(chunks)] + [q_rope[rows, :]], axis=1
            ).astype(BF16)
            fresh_score[rows, :] = scale * lax.dot_general(
                q, keys, NT, preferred_element_type=F32
            )
            return carry

        lax.fori_loop(0, per_step * steps // 128, score, 0)

    for n in range(group):
        i = at * group + n
        q = jnp.concatenate(
            [spread(acc, i, (c,)) for c in range(chunks)] + [spread(q_rope, i)[:, :ROPE]], axis=1
        ).astype(BF16)
        keys = p_ref[n]
        s_prompt = scale * lax.dot_general(q, keys, NT, preferred_element_type=F32)
        s_fresh = spread(fresh_score, i)
        column = lax.broadcasted_iota(jnp.int32, s_prompt.shape, 1)
        s_prompt = jnp.where(column < lengths[i], s_prompt, FLOOR)
        step_of = lax.broadcasted_iota(jnp.int32, s_fresh.shape, 0) // heads
        column = lax.broadcasted_iota(jnp.int32, s_fresh.shape, 1) - steps * i
        s_fresh = jnp.where((column >= 0) & (column <= step_of), s_fresh, FLOOR)
        peak = jnp.maximum(
            jnp.max(s_prompt, axis=1, keepdims=True), jnp.max(s_fresh, axis=1, keepdims=True)
        )
        w_prompt = jnp.exp(s_prompt - peak)
        w_fresh = jnp.exp(s_fresh - peak)
        sums = jnp.sum(w_prompt, axis=1, keepdims=True) + jnp.sum(w_fresh, axis=1, keepdims=True)
        mixed = jnp.dot(
            w_prompt.astype(BF16), keys[:, :latent], preferred_element_type=F32
        )
        for c in range(chunks):
            collect(acc, i, mixed[:, 128 * c : 128 * c + 128], (c,))
        collect(fresh_score, i, w_fresh)
        collect(total, i, jnp.broadcast_to(sums, s_fresh.shape))

    @pl.when(at == pl.num_programs(0) - 1)
    def _():
        values = jnp.concatenate([fresh[b] for b in range(chunks)], axis=1).astype(BF16)
        copy_uv.wait()
        for h in range(heads):
            rows = pl.ds(h, many, stride=heads)
            mixed = jnp.dot(
                fresh_score[rows, :].astype(BF16), values, preferred_element_type=F32
            )
            mixed = mixed + jnp.concatenate([acc[c, rows, :] for c in range(chunks)], axis=1)
            part = total[rows, :]
            mixed = (mixed / jnp.concatenate([part] * chunks, axis=1)).astype(BF16)
            head_out[:, h * 128 : h * 128 + 128] = jnp.dot(
                mixed, w_uv[h], preferred_element_type=F32
            ).astype(BF16)
        copy_out.wait()
        half = many // 2
        core = where[0] % 2
        mine = head_out[pl.ds(pl.multiple_of(core * half, half), half), :]
        theirs = head_out[pl.ds(pl.multiple_of((1 - core) * half, half), half), :]
        for b in range(w_out.shape[1] // 512):
            at_b = slice(b * 512, b * 512 + 512)
            given_ref[:, at_b] = jnp.dot(
                theirs, w_out[:, at_b], preferred_element_type=F32
            ).astype(BF16)
            kept_ref[:, at_b] = jnp.dot(mine, w_out[:, at_b], preferred_element_type=F32)


def attention(placing, lengths, where, payload, prompt_latent, w_uk, w_uv, w_out, steps):
    slots, span, feature = prompt_latent.shape
    heads, latent, nope = w_uk.shape
    width = w_out.shape[1]
    rows = steps * slots * heads
    half = steps * slots // 2
    chunks = latent // 128

    def whole(x):
        return pl.BlockSpec(x.shape, lambda i: (0,) * x.ndim, pipeline_mode=pl.Buffered(1))

    def whole_out(shape):
        return pl.BlockSpec(shape, lambda i: (0, 0), pipeline_mode=pl.Buffered(1))

    return pl.pallas_call(
        attention_kernel,
        grid=(slots // GROUP,),
        out_shape=(
            jax.ShapeDtypeStruct((half, width), BF16),
            jax.ShapeDtypeStruct((half, width), F32),
        ),
        in_specs=[
            SMEM_SPEC,
            SMEM_SPEC,
            SMEM_SPEC,
            whole(payload),
            pl.BlockSpec((GROUP, span, feature), lambda i: (i, 0, 0)),
            whole(w_uk),
            ANY_SPEC,
            ANY_SPEC,
        ],
        out_specs=(
            pl.BlockSpec((half, width), lambda i: (0, 0)),
            pl.BlockSpec((half, width), lambda i: (0, 0)),
        ),
        scratch_shapes=[
            pltpu.VMEM((rows, 128), F32),
            pltpu.VMEM((rows, 128), F32),
            pltpu.VMEM((chunks, rows, 128), F32),
            pltpu.VMEM((chunks + 1, steps * slots, 128), F32),
            pltpu.VMEM((payload.shape[0] * 8, 128), F32),
            pltpu.VMEM((rows, 128), F32),
            pltpu.VMEM((rows, 128), F32),
            pltpu.VMEM(w_uv.shape, BF16),
            pltpu.VMEM(w_out.shape, BF16),
            pltpu.VMEM((steps * slots, heads * 128), BF16),
            pltpu.SemaphoreType.DMA((2,)),
        ],
        compiler_params=params(dimension_semantics=("arbitrary",)),
        cost_estimate=cost(),
        name="attention",
    )(placing, lengths, where, payload, prompt_latent, w_uk, w_uv, w_out)


def exchange(x):
    return lax.all_to_all(x, "pool", split_axis=0, concat_axis=0, tiled=True)


def body(prompt_latent, prompt_lengths, decode_slot, new_latent, queries, w_uk, w_uv, w_out):
    pool_count = lax.axis_size("pool")
    tp_count = lax.axis_size("tp")
    pool_index = lax.axis_index("pool")
    tp_index = lax.axis_index("tp")
    steps, slots, heads, width = queries.shape
    span, feature = prompt_latent.shape[1:]
    piece = span // tp_count
    out_width = w_out.shape[1]
    cells = pool_count * CAP
    where = tp_index.astype(jnp.int32).reshape(1)
    placing, arrival, match = route(decode_slot, pool_index, pool_count, slots)
    decode_lengths = jnp.sum(jnp.where(match, prompt_lengths[None, :], 0), axis=1)
    own_lengths = lax.dynamic_slice_in_dim(prompt_lengths, pool_index * slots, slots)

    payload = exchange(pack_queries(arrival, queries, new_latent, pool_count))
    first_send, second_send = pack_context(placing, where, prompt_latent, piece, pool_count)
    payload, first_send = lax.optimization_barrier((payload, first_send))
    first = exchange(first_send)

    given, kept = attention(
        placing, own_lengths, where, payload, prompt_latent, w_uk, w_uv, w_out, steps
    )

    core = tp_index % 2
    z = tp_index // 2
    z_count = tp_count // 2
    block = out_width // z_count
    swap = [(i, i ^ 1) for i in range(tp_count)]

    def hop(d):
        return [(i, i ^ (2 * d)) for i in range(tp_count)]

    pair = kept + lax.ppermute(given, "tp", swap).astype(F32)
    mine = lax.dynamic_slice_in_dim(pair, z * block, block, 1)
    pair16 = pair.astype(BF16)
    got = [
        lax.ppermute(
            lax.dynamic_slice_in_dim(pair16, (z ^ d) * block, block, 1), "tp", hop(d)
        )
        for d in range(1, z_count)
    ]
    for part in got:
        mine = mine + part.astype(F32)
    mine = mine.astype(BF16).reshape(steps // 2, slots, block)

    grid_cells = jnp.arange(cells)
    source_row = jnp.sum(
        jnp.where(placing[None, :] == grid_cells[:, None], jnp.arange(slots)[None, :], 0), axis=1
    )
    back = jnp.take(mine, source_row, axis=1).transpose(1, 0, 2)
    back = back.reshape(pool_count, CAP * steps // 2, block)
    back, first = lax.optimization_barrier((back, first))
    back = exchange(back)
    back, second_send = lax.optimization_barrier((back, second_send))
    second = exchange(second_send)
    context = place(0, FIRST_RANKS, arrival, decode_lengths, where, first, piece, feature)

    back = jnp.take(back.reshape(cells, steps // 2, block), arrival, axis=0)
    parts = jnp.stack([back] + [lax.ppermute(back, "tp", hop(d)) for d in range(1, z_count)])
    parts = jnp.take(parts, jnp.arange(z_count) ^ z, axis=0)
    row_half = parts.transpose(1, 2, 0, 3).reshape(slots, steps // 2, out_width)
    other_half = lax.ppermute(row_half, "tp", swap)
    decoded = jnp.concatenate(
        [
            jnp.where(core == 0, row_half, other_half),
            jnp.where(core == 0, other_half, row_half),
        ],
        axis=1,
    )
    context = place(
        FIRST_RANKS, CAP, arrival, decode_lengths, where, second, piece, feature, context
    )
    return decoded, context


def solution(mesh):
    in_specs = (
        P("pool", None, None),
        P(),
        P(),
        P(None, "pool", None),
        P(None, "pool", "tp", None),
        P("tp", None, None),
        P("tp", None, None),
        P("tp", None),
    )
    out_specs = (P("pool", None, None), P("pool", "tp", None))
    return jax.shard_map(body, mesh=mesh, in_specs=in_specs, out_specs=out_specs, check_vma=False)
```

```python
import functools
import math

import jax
import jax.numpy as jnp
from jax import lax
from jax.experimental import pallas as pl
from jax.experimental.pallas import tpu as pltpu
from jax.sharding import PartitionSpec as P

ROPE = 64
NOPE = 128
CAP = 4
FIRST_RANKS = 3
GROUP = 4
FLOOR = -1e30
BF16 = jnp.bfloat16
F32 = jnp.float32

VMEM_LIMIT = 60 * 1024 * 1024
SMEM_SPEC = pl.BlockSpec(memory_space=pltpu.SMEM)
VMEM_SPEC = pl.BlockSpec(memory_space=pltpu.VMEM)
ANY_SPEC = pl.BlockSpec(memory_space=pl.ANY)
NT = (((1,), (1,)), ((), ()))


def params(**kw):
    return pltpu.CompilerParams(vmem_limit_bytes=VMEM_LIMIT, **kw)


def cost(flops=1000, bytes_accessed=1000):
    return pl.CostEstimate(flops=flops, bytes_accessed=bytes_accessed, transcendentals=0)


def route(decode_slot, pool_index, pool_count, slot_count):
    targets = decode_slot // slot_count
    by_source = targets.reshape(pool_count, slot_count)
    earlier = jnp.tril(jnp.ones((slot_count, slot_count), jnp.int32), -1)
    own = lax.dynamic_slice_in_dim(by_source, pool_index, 1, 0)[0]
    same = (own[:, None] == own[None, :]).astype(jnp.int32)
    placing = own * CAP + jnp.sum(same * earlier, axis=1)
    arriving = (by_source == pool_index).astype(jnp.int32)
    before = jnp.cumsum(arriving, axis=1) - arriving
    cell = (jnp.arange(pool_count)[:, None] * CAP + before).reshape(-1)
    wanted = pool_index * slot_count + jnp.arange(slot_count)
    match = decode_slot[None, :] == wanted[:, None]
    arrival = jnp.sum(jnp.where(match, cell[None, :], 0), axis=1)
    return placing, arrival, match


def pack_queries_kernel(arrival, q_ref, n_ref, out_ref, new_rows, tails):
    steps, slots, heads, width = q_ref.shape
    rows = steps * heads
    blocks = n_ref.shape[2] // 128
    new_rows[...] = n_ref[...].astype(F32)
    tails[...] = jnp.zeros(tails.shape, F32)

    def one(j, carry):
        dest, rank = arrival[j] // CAP, arrival[j] % CAP
        x = q_ref[:, j].astype(F32)
        nope = x[:, :, :NOPE].reshape(rows, NOPE)
        rope = x[:, :, NOPE:].reshape(rows, ROPE)
        rope = jnp.concatenate([rope[: rows // 2], rope[rows // 2 :]], axis=1)
        fresh = jnp.concatenate([new_rows[s, pl.ds(j, 1), :] for s in range(steps)], axis=0)
        body = [fresh[:, 128 * b : 128 * b + 128] for b in range(blocks)]
        last = fresh[:, 128 * blocks :]
        cell = jnp.concatenate([nope, rope] + body, axis=0)
        out_ref[dest, pl.ds(pl.multiple_of(rank * 64, 64), 64), :] = cell.astype(BF16)
        tails[pl.ds(dest * 8 + rank * 2, 2), :] = jnp.concatenate(
            [last[: steps // 2], last[steps // 2 :]], axis=1
        )
        return carry

    lax.fori_loop(0, slots, one, 0)
    out_ref[:, 256:264, :] = tails[...].reshape(out_ref.shape[0], 8, 128).astype(BF16)


def pack_queries(arrival, queries, new_latent, pool_count):
    return pl.pallas_call(
        pack_queries_kernel,
        out_shape=jax.ShapeDtypeStruct((pool_count, 264, 128), BF16),
        in_specs=[SMEM_SPEC, VMEM_SPEC, VMEM_SPEC],
        out_specs=VMEM_SPEC,
        scratch_shapes=[
            pltpu.VMEM(new_latent.shape, F32),
            pltpu.VMEM((pool_count * 8, 128), F32),
        ],
        compiler_params=params(),
        cost_estimate=cost(),
        name="pack_queries",
    )(arrival, queries, new_latent)


def pack_context_kernel(placing, where, p_ref, first_ref, second_ref, buf, sems):
    slots, feature, window = buf.shape
    blocks = feature // 128
    piece = first_ref.shape[2] * 128 // feature
    chunk = slots // sems.shape[0]
    row = where[0] * piece
    start = pl.multiple_of(jnp.where(row + piece > window, p_ref.shape[2] - window, 0), 128)
    copies = [
        pltpu.make_async_copy(
            p_ref.at[pl.ds(k * chunk, chunk), :, pl.ds(start, window)],
            buf.at[pl.ds(k * chunk, chunk)],
            sems.at[k],
        )
        for k in range(sems.shape[0])
    ]
    for copy in copies:
        copy.start()
    pick = lax.broadcasted_iota(jnp.int32, (piece, window), 1) - (
        row - start + lax.broadcasted_iota(jnp.int32, (piece, window), 0)
    )
    pick = jnp.where(pick == 0, 1.0, 0.0).astype(BF16)

    for k, copy in enumerate(copies):
        copy.wait()

        def one(n, carry):
            g = k * chunk + n
            dest, rank = placing[g] // CAP, placing[g] % CAP
            turned = lax.dot_general(pick, buf[g], NT, preferred_element_type=F32)
            last = turned[:, 128 * blocks :]
            last = jnp.concatenate([last[: piece // 2], last[piece // 2 :]], axis=1)
            cell = jnp.concatenate(
                [turned[:, 128 * b : 128 * b + 128] for b in range(blocks)] + [last], axis=0
            ).astype(BF16)

            @pl.when(rank < FIRST_RANKS)
            def _():
                first_ref[dest, rank] = cell

            @pl.when(rank >= FIRST_RANKS)
            def _():
                second_ref[dest, rank - FIRST_RANKS] = cell

            return carry

        lax.fori_loop(0, chunk, one, 0, unroll=2)


def pack_context(placing, where, prompt_latent, piece, pool_count):
    slots, feature, _ = prompt_latent.shape
    rows = piece * feature // 128
    return pl.pallas_call(
        pack_context_kernel,
        out_shape=(
            jax.ShapeDtypeStruct((pool_count, FIRST_RANKS, rows, 128), BF16),
            jax.ShapeDtypeStruct((pool_count, CAP - FIRST_RANKS, rows, 128), BF16),
        ),
        in_specs=[SMEM_SPEC, SMEM_SPEC, ANY_SPEC],
        out_specs=(VMEM_SPEC, VMEM_SPEC),
        scratch_shapes=[
            pltpu.VMEM((slots, feature, 256), BF16),
            pltpu.SemaphoreType.DMA((4,)),
        ],
        compiler_params=params(),
        cost_estimate=cost(),
        name="pack_context",
    )(placing, where, prompt_latent)


def unpack_piece(packed, row, first_row, length, piece, feature):
    blocks = feature // 128
    parts = [packed[(*row, pl.ds(b * piece, piece), slice(None))] for b in range(blocks)]
    last = packed[(*row, pl.ds(blocks * piece, piece // 2), slice(None))].astype(F32)
    last = jnp.concatenate([last[:, :64], last[:, 64:]], axis=0).astype(BF16)
    whole = jnp.concatenate(parts + [last], axis=1)
    position = first_row + lax.broadcasted_iota(jnp.int32, whole.shape, 0)
    return jnp.where(position < length, whole.astype(F32), 0.0).astype(BF16)


def place_kernel(low, high, keep, arrival, lengths, where, packed, *rest):
    out_ref, inbox, outbox, in_sems, out_sems = rest[-5:]
    slots, piece, feature = out_ref.shape
    first_row = where[0] * piece

    def copy_in(j):
        owner, rank = arrival[j] // CAP, arrival[j] % CAP
        rank = jnp.clip(rank - low, 0, high - low - 1)
        return pltpu.make_async_copy(packed.at[owner, rank], inbox.at[j], in_sems.at[j])

    def copy_out(j):
        return pltpu.make_async_copy(outbox.at[j], out_ref.at[j], out_sems.at[j])

    def each(action):
        def step(j, carry):
            rank = arrival[j] % CAP

            @pl.when((rank >= low) & (rank < high))
            def _():
                action(j)

            return carry

        lax.fori_loop(0, slots, step, 0)

    def work(j):
        copy_in(j).wait()
        outbox[j] = unpack_piece(inbox, (j,), first_row, lengths[j], piece, feature)
        copy_out(j).start()

    each(lambda j: copy_in(j).start())
    each(work)
    each(lambda j: copy_out(j).wait())


def place(low, high, arrival, lengths, where, packed, piece, feature, context=None):
    slots = arrival.shape[0]
    rows = packed.shape[2]
    args = [arrival, lengths, where, packed] + ([] if context is None else [context])
    return pl.pallas_call(
        functools.partial(place_kernel, low, high, context is not None),
        out_shape=jax.ShapeDtypeStruct((slots, piece, feature), BF16),
        in_specs=[SMEM_SPEC] * 3 + [ANY_SPEC] * (len(args) - 3),
        out_specs=ANY_SPEC,
        scratch_shapes=[
            pltpu.VMEM((slots, rows, 128), BF16),
            pltpu.VMEM((slots, piece, feature), BF16),
            pltpu.SemaphoreType.DMA((slots,)),
            pltpu.SemaphoreType.DMA((slots,)),
        ],
        input_output_aliases={} if context is None else {4: 0},
        compiler_params=params(),
        cost_estimate=cost(),
        name="place_context",
    )(*args)


def attention_kernel(
    placing, lengths, where, payload_hbm, p_hbm, w_uk_hbm, w_uv_hbm, w_out_hbm,
    given_ref, kept_ref,
    payload, prompt, w_uk, w_uv, w_out,
    q_nope, q_rope, acc, fresh, tails, fresh_score, total, head_out, sems,
):
    steps = 4
    heads, latent, nope = w_uk.shape
    slots, feature, span = prompt.shape
    chunks = latent // 128
    per_step = slots * heads
    many = slots * steps
    scale = 1.0 / math.sqrt(nope + ROPE)
    copy_payload = pltpu.make_async_copy(payload_hbm, payload, sems.at[0])
    copy_uk = pltpu.make_async_copy(w_uk_hbm, w_uk, sems.at[1])
    copy_uv = pltpu.make_async_copy(w_uv_hbm, w_uv, sems.at[2])
    copy_out = pltpu.make_async_copy(w_out_hbm, w_out, sems.at[3])

    def copy_prompt(k):
        part = pl.ds(k * GROUP, GROUP)
        return pltpu.make_async_copy(p_hbm.at[part], prompt.at[part], sems.at[4 + k])

    copy_payload.start()
    copy_uk.start()
    for k in range(slots // GROUP):
        copy_prompt(k).start()
    copy_uv.start()
    copy_out.start()

    def spread(ref, i, lead=()):
        return jnp.concatenate(
            [
                ref[(*lead, pl.ds(pl.multiple_of(per_step * s + heads * i, 8), heads), slice(None))]
                for s in range(steps)
            ],
            axis=0,
        )

    def collect(ref, i, value, lead=()):
        for s in range(steps):
            ref[(*lead, pl.ds(pl.multiple_of(per_step * s + heads * i, 8), heads), slice(None))] = (
                value[heads * s : heads * s + heads]
            )

    copy_payload.wait()
    tails[...] = payload[:, 256:264, :].astype(F32).reshape(tails.shape)

    def unpack(i, carry):
        dest, rank = placing[i] // CAP, placing[i] % CAP
        cell = payload[dest, pl.ds(pl.multiple_of(rank * 64, 64), 64), :].astype(F32)
        collect(q_nope, i, cell[:32])
        rope = jnp.concatenate([cell[32:48, :64], cell[32:48, 64:]], axis=0)
        collect(q_rope, i, jnp.concatenate([rope, jnp.zeros_like(rope)], axis=1))
        for b in range(chunks):
            fresh[b, pl.ds(steps * i, steps), :] = cell[48 + 4 * b : 52 + 4 * b]
        last = tails[pl.ds(dest * 8 + rank * 2, 2), :]
        last = jnp.concatenate([last[:, :64], last[:, 64:]], axis=0)
        fresh[chunks, pl.ds(steps * i, steps), :] = jnp.concatenate(
            [last, jnp.zeros_like(last)], axis=1
        )
        return carry

    lax.fori_loop(0, slots, unpack, 0, unroll=4)
    copy_uk.wait()
    for h in range(heads):
        rows = pl.ds(h, many, stride=heads)
        a = lax.dot_general(
            q_nope[rows, :].astype(BF16), w_uk[h], NT, preferred_element_type=F32
        )
        a = a.astype(BF16).astype(F32)
        for c in range(chunks):
            acc[c, rows, :] = a[:, 128 * c : 128 * c + 128]
    keys = jnp.concatenate([fresh[b] for b in range(chunks + 1)], axis=1).astype(BF16)

    def score(k, carry):
        rows = pl.ds(pl.multiple_of(k * 128, 128), 128)
        q = jnp.concatenate(
            [acc[c, rows, :] for c in range(chunks)] + [q_rope[rows, :]], axis=1
        ).astype(BF16)
        fresh_score[rows, :] = scale * lax.dot_general(q, keys, NT, preferred_element_type=F32)
        return carry

    lax.fori_loop(0, per_step * steps // 128, score, 0)

    def one(i):
        q = jnp.concatenate(
            [spread(acc, i, (c,)) for c in range(chunks)] + [spread(q_rope, i)[:, :ROPE]], axis=1
        ).astype(BF16)
        s_prompt = scale * jnp.dot(q, prompt[i], preferred_element_type=F32)
        s_fresh = spread(fresh_score, i)
        column = lax.broadcasted_iota(jnp.int32, s_prompt.shape, 1)
        s_prompt = jnp.where(column < lengths[i], s_prompt, FLOOR)
        step_of = lax.broadcasted_iota(jnp.int32, s_fresh.shape, 0) // heads
        column = lax.broadcasted_iota(jnp.int32, s_fresh.shape, 1) - steps * i
        s_fresh = jnp.where((column >= 0) & (column <= step_of), s_fresh, FLOOR)
        peak = jnp.maximum(
            jnp.max(s_prompt, axis=1, keepdims=True), jnp.max(s_fresh, axis=1, keepdims=True)
        )
        w_prompt = jnp.exp(s_prompt - peak)
        w_fresh = jnp.exp(s_fresh - peak)
        sums = jnp.sum(w_prompt, axis=1, keepdims=True) + jnp.sum(w_fresh, axis=1, keepdims=True)
        mixed = lax.dot_general(
            w_prompt.astype(BF16), prompt[i, :latent], NT, preferred_element_type=F32
        )
        for c in range(chunks):
            collect(acc, i, mixed[:, 128 * c : 128 * c + 128], (c,))
        collect(fresh_score, i, w_fresh)
        collect(total, i, jnp.broadcast_to(sums, s_fresh.shape))

    def attend(k, carry):
        copy_prompt(k).wait()
        for n in range(GROUP):
            one(k * GROUP + n)
        return carry

    lax.fori_loop(0, slots // GROUP, attend, 0)

    values = jnp.concatenate([fresh[b] for b in range(chunks)], axis=1).astype(BF16)
    copy_uv.wait()
    for h in range(heads):
        rows = pl.ds(h, many, stride=heads)
        mixed = jnp.dot(fresh_score[rows, :].astype(BF16), values, preferred_element_type=F32)
        mixed = mixed + jnp.concatenate([acc[c, rows, :] for c in range(chunks)], axis=1)
        part = total[rows, :]
        mixed = (mixed / jnp.concatenate([part] * chunks, axis=1)).astype(BF16)
        head_out[:, h * 128 : h * 128 + 128] = jnp.dot(
            mixed, w_uv[h], preferred_element_type=F32
        ).astype(BF16)
    copy_out.wait()
    half = many // 2
    core = where[0] % 2
    mine = head_out[pl.ds(pl.multiple_of(core * half, half), half), :]
    theirs = head_out[pl.ds(pl.multiple_of((1 - core) * half, half), half), :]
    for b in range(w_out.shape[1] // 512):
        at_b = slice(b * 512, b * 512 + 512)
        given_ref[:, at_b] = jnp.dot(theirs, w_out[:, at_b], preferred_element_type=F32).astype(
            BF16
        )
        kept_ref[:, at_b] = jnp.dot(mine, w_out[:, at_b], preferred_element_type=F32)


def attention(placing, lengths, where, payload, prompt_latent, w_uk, w_uv, w_out, steps):
    slots, feature, span = prompt_latent.shape
    heads, latent, nope = w_uk.shape
    width = w_out.shape[1]
    rows = steps * slots * heads
    half = steps * slots // 2
    chunks = latent // 128
    return pl.pallas_call(
        attention_kernel,
        out_shape=(
            jax.ShapeDtypeStruct((half, width), BF16),
            jax.ShapeDtypeStruct((half, width), F32),
        ),
        in_specs=[SMEM_SPEC] * 3 + [ANY_SPEC] * 5,
        out_specs=(VMEM_SPEC, VMEM_SPEC),
        scratch_shapes=[
            pltpu.VMEM(payload.shape, BF16),
            pltpu.VMEM(prompt_latent.shape, BF16),
            pltpu.VMEM(w_uk.shape, BF16),
            pltpu.VMEM(w_uv.shape, BF16),
            pltpu.VMEM(w_out.shape, BF16),
            pltpu.VMEM((rows, 128), F32),
            pltpu.VMEM((rows, 128), F32),
            pltpu.VMEM((chunks, rows, 128), F32),
            pltpu.VMEM((chunks + 1, steps * slots, 128), F32),
            pltpu.VMEM((payload.shape[0] * 8, 128), F32),
            pltpu.VMEM((rows, 128), F32),
            pltpu.VMEM((rows, 128), F32),
            pltpu.VMEM((steps * slots, heads * 128), BF16),
            pltpu.SemaphoreType.DMA((4 + slots // GROUP,)),
        ],
        compiler_params=params(),
        cost_estimate=cost(),
        name="attention",
    )(placing, lengths, where, payload, prompt_latent, w_uk, w_uv, w_out)


def exchange(x):
    return lax.all_to_all(x, "pool", split_axis=0, concat_axis=0, tiled=True)


def body(prompt_latent, prompt_lengths, decode_slot, new_latent, queries, w_uk, w_uv, w_out):
    pool_count = lax.axis_size("pool")
    tp_count = lax.axis_size("tp")
    pool_index = lax.axis_index("pool")
    tp_index = lax.axis_index("tp")
    latent_t = prompt_latent.transpose(0, 2, 1)
    steps, slots, heads, width = queries.shape
    span, feature = prompt_latent.shape[1:]
    piece = span // tp_count
    out_width = w_out.shape[1]
    cells = pool_count * CAP
    where = tp_index.astype(jnp.int32).reshape(1)
    placing, arrival, match = route(decode_slot, pool_index, pool_count, slots)
    decode_lengths = jnp.sum(jnp.where(match, prompt_lengths[None, :], 0), axis=1)
    own_lengths = lax.dynamic_slice_in_dim(prompt_lengths, pool_index * slots, slots)

    payload = exchange(pack_queries(arrival, queries, new_latent, pool_count))
    first_send, second_send = pack_context(placing, where, latent_t, piece, pool_count)
    payload, first_send = lax.optimization_barrier((payload, first_send))
    first = exchange(first_send)

    given, kept = attention(
        placing, own_lengths, where, payload, latent_t, w_uk, w_uv, w_out, steps
    )

    core = tp_index % 2
    z = tp_index // 2
    z_count = tp_count // 2
    block = out_width // z_count
    swap = [(i, i ^ 1) for i in range(tp_count)]

    def hop(d):
        return [(i, i ^ (2 * d)) for i in range(tp_count)]

    pair = kept + lax.ppermute(given, "tp", swap).astype(F32)
    mine = lax.dynamic_slice_in_dim(pair, z * block, block, 1)
    pair16 = pair.astype(BF16)
    got = [
        lax.ppermute(
            lax.dynamic_slice_in_dim(pair16, (z ^ d) * block, block, 1), "tp", hop(d)
        )
        for d in range(1, z_count)
    ]
    for part in got:
        mine = mine + part.astype(F32)
    mine = mine.astype(BF16).reshape(steps // 2, slots, block)

    grid_cells = jnp.arange(cells)
    source_row = jnp.sum(
        jnp.where(placing[None, :] == grid_cells[:, None], jnp.arange(slots)[None, :], 0), axis=1
    )
    back = jnp.take(mine, source_row, axis=1).transpose(1, 0, 2)
    back = back.reshape(pool_count, CAP * steps // 2, block)
    back, first = lax.optimization_barrier((back, first))
    back = exchange(back)
    back, second_send = lax.optimization_barrier((back, second_send))
    second = exchange(second_send)
    context = place(0, FIRST_RANKS, arrival, decode_lengths, where, first, piece, feature)

    back = jnp.take(back.reshape(cells, steps // 2, block), arrival, axis=0)
    parts = jnp.stack([back] + [lax.ppermute(back, "tp", hop(d)) for d in range(1, z_count)])
    parts = jnp.take(parts, jnp.arange(z_count) ^ z, axis=0)
    row_half = parts.transpose(1, 2, 0, 3).reshape(slots, steps // 2, out_width)
    other_half = lax.ppermute(row_half, "tp", swap)
    decoded = jnp.concatenate(
        [
            jnp.where(core == 0, row_half, other_half),
            jnp.where(core == 0, other_half, row_half),
        ],
        axis=1,
    )
    context = place(
        FIRST_RANKS, CAP, arrival, decode_lengths, where, second, piece, feature, context
    )
    return decoded, context


def solution(mesh):
    in_specs = (
        P("pool", None, None),
        P(),
        P(),
        P(None, "pool", None),
        P(None, "pool", "tp", None),
        P("tp", None, None),
        P("tp", None, None),
        P("tp", None),
    )
    out_specs = (P("pool", None, None), P("pool", "tp", None))
    return jax.shard_map(body, mesh=mesh, in_specs=in_specs, out_specs=out_specs, check_vma=False)
```

```python
import functools
import math

import jax
import jax.numpy as jnp
from jax import lax
from jax.experimental import pallas as pl
from jax.experimental.pallas import tpu as pltpu
from jax.sharding import PartitionSpec as P

ROPE = 64
NOPE = 128
CAP = 4
FIRST_RANKS = 3
GROUP = 4
FLOOR = -1e30
BF16 = jnp.bfloat16
F32 = jnp.float32

MIB = 1024 * 1024
SMEM_SPEC = pl.BlockSpec(memory_space=pltpu.SMEM)
VMEM_SPEC = pl.BlockSpec(memory_space=pltpu.VMEM)
ANY_SPEC = pl.BlockSpec(memory_space=pl.ANY)
NT = (((1,), (1,)), ((), ()))


def params(mib=16):
    return pltpu.CompilerParams(vmem_limit_bytes=mib * MIB)


def cost(flops=1000, bytes_accessed=1000):
    return pl.CostEstimate(flops=flops, bytes_accessed=bytes_accessed, transcendentals=0)


def split(cell):
    return cell // CAP, cell % CAP


def pack_queries_kernel(
    decode_slot, prompt_lengths, where, q_hbm, n_hbm,
    out_ref, arrival, lengths,
    q_ref, n_ref, new_rows, tails, sems,
):
    steps, slots, heads, width = q_ref.shape
    rows = steps * heads
    blocks = n_ref.shape[2] // 128
    copy_n = pltpu.make_async_copy(n_hbm, n_ref, sems.at[0])
    copy_q = pltpu.make_async_copy(q_hbm, q_ref, sems.at[1])
    copy_n.start()
    copy_q.start()
    first = where[1] * slots

    def locate(p, carry):
        rank = jnp.int32(0)
        for k in range(slots):
            inner = decode_slot[p * slots + k] - first
            hit = (inner >= 0) & (inner < slots)
            at = jnp.where(hit, inner, slots)
            arrival[at] = p * CAP + rank
            lengths[at] = prompt_lengths[p * slots + k]
            rank = rank + hit.astype(jnp.int32)
        return carry

    lax.fori_loop(0, out_ref.shape[0], locate, 0)
    tails[...] = jnp.zeros(tails.shape, F32)
    copy_n.wait()
    new_rows[...] = n_ref[...].astype(F32)
    copy_q.wait()

    def one(j, carry):
        dest, rank = split(arrival[j])
        x = q_ref[:, j].astype(F32)
        nope = x[:, :, :NOPE].reshape(rows, NOPE)
        rope = x[:, :, NOPE:].reshape(rows, ROPE)
        rope = jnp.concatenate([rope[: rows // 2], rope[rows // 2 :]], axis=1)
        fresh = jnp.concatenate([new_rows[s, pl.ds(j, 1), :] for s in range(steps)], axis=0)
        body = [fresh[:, 128 * b : 128 * b + 128] for b in range(blocks)]
        last = fresh[:, 128 * blocks :]
        cell = jnp.concatenate([nope, rope] + body, axis=0)
        out_ref[dest, pl.ds(pl.multiple_of(rank * 64, 64), 64), :] = cell.astype(BF16)
        tails[pl.ds(dest * 8 + rank * 2, 2), :] = jnp.concatenate(
            [last[: steps // 2], last[steps // 2 :]], axis=1
        )
        return carry

    lax.fori_loop(0, slots, one, 0, unroll=4)
    out_ref[:, 256:264, :] = tails[...].reshape(out_ref.shape[0], 8, 128).astype(BF16)


def pack_queries(decode_slot, prompt_lengths, where, queries, new_latent, pool_count):
    slots = queries.shape[1]
    return pl.pallas_call(
        pack_queries_kernel,
        out_shape=(
            jax.ShapeDtypeStruct((pool_count, 264, 128), BF16),
            jax.ShapeDtypeStruct((slots + 8,), jnp.int32),
            jax.ShapeDtypeStruct((slots + 8,), jnp.int32),
        ),
        in_specs=[SMEM_SPEC] * 3 + [ANY_SPEC] * 2,
        out_specs=(VMEM_SPEC, SMEM_SPEC, SMEM_SPEC),
        scratch_shapes=[
            pltpu.VMEM(queries.shape, BF16),
            pltpu.VMEM(new_latent.shape, BF16),
            pltpu.VMEM(new_latent.shape, F32),
            pltpu.VMEM((pool_count * 8, 128), F32),
            pltpu.SemaphoreType.DMA((2,)),
        ],
        compiler_params=params(60),
        cost_estimate=cost(),
        name="pack_queries",
    )(decode_slot, prompt_lengths, where, queries, new_latent)


def pack_context_kernel(
    decode_slot, where, p_ref, first_ref, second_ref, placing, counts, buf, sems
):
    slots, feature, window = buf.shape
    blocks = feature // 128
    piece = first_ref.shape[2] * 128 // feature
    chunk = slots // sems.shape[0]
    row = where[0] * piece
    start = pl.multiple_of(jnp.where(row + piece > window, p_ref.shape[2] - window, 0), 128)
    copies = [
        pltpu.make_async_copy(
            p_ref.at[pl.ds(k * chunk, chunk), :, pl.ds(start, window)],
            buf.at[pl.ds(k * chunk, chunk)],
            sems.at[k],
        )
        for k in range(sems.shape[0])
    ]
    for copy in copies:
        copy.start()
    bits = slots.bit_length() - 1
    for p in range(counts.shape[0]):
        counts[p] = 0
    for g in range(slots):
        owner = decode_slot[where[1] * slots + g] >> bits
        rank = counts[owner]
        counts[owner] = rank + 1
        placing[g] = owner * CAP + rank
    pick = lax.broadcasted_iota(jnp.int32, (piece, window), 1) - (
        row - start + lax.broadcasted_iota(jnp.int32, (piece, window), 0)
    )
    pick = jnp.where(pick == 0, 1.0, 0.0).astype(BF16)

    for k, copy in enumerate(copies):
        copy.wait()

        def one(n, carry):
            g = k * chunk + n
            dest, rank = split(placing[g])
            turned = lax.dot_general(pick, buf[g], NT, preferred_element_type=F32)
            last = turned[:, 128 * blocks :]
            last = jnp.concatenate([last[: piece // 2], last[piece // 2 :]], axis=1)
            cell = jnp.concatenate(
                [turned[:, 128 * b : 128 * b + 128] for b in range(blocks)] + [last], axis=0
            ).astype(BF16)

            @pl.when(rank < FIRST_RANKS)
            def _():
                first_ref[dest, rank] = cell

            @pl.when(rank >= FIRST_RANKS)
            def _():
                second_ref[dest] = cell

            return carry

        lax.fori_loop(0, chunk, one, 0, unroll=2)


def pack_context(decode_slot, where, prompt_latent, piece, pool_count):
    slots, feature, _ = prompt_latent.shape
    rows = piece * feature // 128
    return pl.pallas_call(
        pack_context_kernel,
        out_shape=(
            jax.ShapeDtypeStruct((pool_count, FIRST_RANKS, rows, 128), BF16),
            jax.ShapeDtypeStruct((pool_count, rows, 128), BF16),
            jax.ShapeDtypeStruct((slots,), jnp.int32),
        ),
        in_specs=[SMEM_SPEC, SMEM_SPEC, ANY_SPEC],
        out_specs=(VMEM_SPEC, VMEM_SPEC, SMEM_SPEC),
        scratch_shapes=[
            pltpu.SMEM((pool_count,), jnp.int32),
            pltpu.VMEM((slots, feature, 256), BF16),
            pltpu.SemaphoreType.DMA((4,)),
        ],
        compiler_params=params(60),
        cost_estimate=cost(),
        name="pack_context",
    )(decode_slot, where, prompt_latent)


def unpack_piece(packed, row, first_row, length, piece, feature):
    blocks = feature // 128
    parts = [packed[(*row, pl.ds(b * piece, piece), slice(None))] for b in range(blocks)]
    last = packed[(*row, pl.ds(blocks * piece, piece // 2), slice(None))].astype(F32)
    last = jnp.concatenate([last[:, :64], last[:, 64:]], axis=0).astype(BF16)
    whole = jnp.concatenate(parts + [last], axis=1)
    position = first_row + lax.broadcasted_iota(jnp.int32, whole.shape, 0)
    return jnp.where(position < length, whole.astype(F32), 0.0).astype(BF16)


def place_kernel(low, high, arrival, lengths, where, packed, *rest):
    out_ref, inbox, outbox, in_sems, out_sems = rest[-5:]
    slots, piece, feature = out_ref.shape
    first_row = where[0] * piece

    def copy_in(j):
        owner, rank = split(arrival[j])
        if high - low == 1:
            source = packed.at[owner]
        else:
            source = packed.at[owner, jnp.clip(rank - low, 0, high - low - 1)]
        return pltpu.make_async_copy(source, inbox.at[j], in_sems.at[j])

    def copy_out(j):
        return pltpu.make_async_copy(outbox.at[j], out_ref.at[j], out_sems.at[j])

    def each(action):
        def step(j, carry):
            rank = split(arrival[j])[1]

            @pl.when((rank >= low) & (rank < high))
            def _():
                action(j)

            return carry

        lax.fori_loop(0, slots, step, 0)

    def work(j):
        copy_in(j).wait()
        outbox[j] = unpack_piece(inbox, (j,), first_row, lengths[j], piece, feature)
        copy_out(j).start()

    each(lambda j: copy_in(j).start())
    each(work)
    each(lambda j: copy_out(j).wait())


def place(low, high, arrival, lengths, where, packed, piece, feature, context=None):
    slots = arrival.shape[0] - 8
    rows = packed.shape[-2]
    args = [arrival, lengths, where, packed] + ([] if context is None else [context])
    return pl.pallas_call(
        functools.partial(place_kernel, low, high),
        out_shape=jax.ShapeDtypeStruct((slots, piece, feature), BF16),
        in_specs=[SMEM_SPEC] * 3 + [ANY_SPEC] * (len(args) - 3),
        out_specs=ANY_SPEC,
        scratch_shapes=[
            pltpu.VMEM((slots, rows, 128), BF16),
            pltpu.VMEM((slots, piece, feature), BF16),
            pltpu.SemaphoreType.DMA((slots,)),
            pltpu.SemaphoreType.DMA((slots,)),
        ],
        input_output_aliases={} if context is None else {4: 0},
        compiler_params=params(),
        cost_estimate=cost(bytes_accessed=12_000_000 if context is None else 1000),
        name="place_context",
    )(*args)


def attention_kernel(
    placing, lengths, where, payload_hbm, p_hbm, w_uk_hbm, w_uv_hbm, w_out_hbm,
    given_ref, kept_ref,
    payload, prompt, w_uk, w_uv, w_out,
    q_nope, q_rope, acc, fresh, tails, fresh_score, total, head_out, sems,
):
    steps = 4
    heads, latent, nope = w_uk.shape
    slots, feature, span = prompt.shape
    chunks = latent // 128
    per_step = slots * heads
    many = slots * steps
    scale = 1.0 / math.sqrt(nope + ROPE)
    first = where[1] * slots
    copy_payload = pltpu.make_async_copy(payload_hbm, payload, sems.at[0])
    copy_uk = pltpu.make_async_copy(w_uk_hbm, w_uk, sems.at[1])
    copy_uv = pltpu.make_async_copy(w_uv_hbm, w_uv, sems.at[2])
    copy_out = pltpu.make_async_copy(w_out_hbm, w_out, sems.at[3])

    def copy_prompt(k):
        part = pl.ds(k * GROUP, GROUP)
        return pltpu.make_async_copy(p_hbm.at[part], prompt.at[part], sems.at[4 + k])

    copy_payload.start()
    copy_uk.start()
    for k in range(slots // GROUP):
        copy_prompt(k).start()
    copy_uv.start()
    copy_out.start()

    def spread(ref, i, lead=()):
        return jnp.concatenate(
            [
                ref[(*lead, pl.ds(pl.multiple_of(per_step * s + heads * i, 8), heads), slice(None))]
                for s in range(steps)
            ],
            axis=0,
        )

    def collect(ref, i, value, lead=()):
        for s in range(steps):
            ref[(*lead, pl.ds(pl.multiple_of(per_step * s + heads * i, 8), heads), slice(None))] = (
                value[heads * s : heads * s + heads]
            )

    copy_payload.wait()
    tails[...] = payload[:, 256:264, :].astype(F32).reshape(tails.shape)

    def unpack(i, carry):
        dest, rank = split(placing[i])
        cell = payload[dest, pl.ds(pl.multiple_of(rank * 64, 64), 64), :].astype(F32)
        collect(q_nope, i, cell[:32])
        rope = jnp.concatenate([cell[32:48, :64], cell[32:48, 64:]], axis=0)
        collect(q_rope, i, jnp.concatenate([rope, jnp.zeros_like(rope)], axis=1))
        for b in range(chunks):
            fresh[b, pl.ds(steps * i, steps), :] = cell[48 + 4 * b : 52 + 4 * b]
        last = tails[pl.ds(dest * 8 + rank * 2, 2), :]
        last = jnp.concatenate([last[:, :64], last[:, 64:]], axis=0)
        fresh[chunks, pl.ds(steps * i, steps), :] = jnp.concatenate(
            [last, jnp.zeros_like(last)], axis=1
        )
        return carry

    lax.fori_loop(0, slots, unpack, 0, unroll=4)
    copy_uk.wait()
    for h in range(heads):
        rows = pl.ds(h, many, stride=heads)
        a = lax.dot_general(
            q_nope[rows, :].astype(BF16), w_uk[h], NT, preferred_element_type=F32
        )
        a = a.astype(BF16).astype(F32)
        for c in range(chunks):
            acc[c, rows, :] = a[:, 128 * c : 128 * c + 128]
    keys = jnp.concatenate([fresh[b] for b in range(chunks + 1)], axis=1).astype(BF16)

    def score(k, carry):
        rows = pl.ds(pl.multiple_of(k * 128, 128), 128)
        q = jnp.concatenate(
            [acc[c, rows, :] for c in range(chunks)] + [q_rope[rows, :]], axis=1
        ).astype(BF16)
        fresh_score[rows, :] = scale * lax.dot_general(q, keys, NT, preferred_element_type=F32)
        return carry

    lax.fori_loop(0, per_step * steps // 128, score, 0)

    def one(i):
        q = jnp.concatenate(
            [spread(acc, i, (c,)) for c in range(chunks)] + [spread(q_rope, i)[:, :ROPE]], axis=1
        ).astype(BF16)
        s_prompt = scale * jnp.dot(q, prompt[i], preferred_element_type=F32)
        s_fresh = spread(fresh_score, i)
        column = lax.broadcasted_iota(jnp.int32, s_prompt.shape, 1)
        s_prompt = jnp.where(column < lengths[first + i], s_prompt, FLOOR)
        step_of = lax.broadcasted_iota(jnp.int32, s_fresh.shape, 0) // heads
        column = lax.broadcasted_iota(jnp.int32, s_fresh.shape, 1) - steps * i
        s_fresh = jnp.where((column >= 0) & (column <= step_of), s_fresh, FLOOR)
        peak = jnp.maximum(
            jnp.max(s_prompt, axis=1, keepdims=True), jnp.max(s_fresh, axis=1, keepdims=True)
        )
        w_prompt = jnp.exp(s_prompt - peak)
        w_fresh = jnp.exp(s_fresh - peak)
        sums = jnp.sum(w_prompt, axis=1, keepdims=True) + jnp.sum(w_fresh, axis=1, keepdims=True)
        mixed = lax.dot_general(
            w_prompt.astype(BF16), prompt[i, :latent], NT, preferred_element_type=F32
        )
        for c in range(chunks):
            collect(acc, i, mixed[:, 128 * c : 128 * c + 128], (c,))
        collect(fresh_score, i, w_fresh)
        collect(total, i, jnp.broadcast_to(sums, s_fresh.shape))

    def attend(k, carry):
        copy_prompt(k).wait()
        for n in range(GROUP):
            one(k * GROUP + n)
        return carry

    lax.fori_loop(0, slots // GROUP, attend, 0)

    values = jnp.concatenate([fresh[b] for b in range(chunks)], axis=1).astype(BF16)
    copy_uv.wait()
    for h in range(heads):
        rows = pl.ds(h, many, stride=heads)
        mixed = jnp.dot(fresh_score[rows, :].astype(BF16), values, preferred_element_type=F32)
        mixed = mixed + jnp.concatenate([acc[c, rows, :] for c in range(chunks)], axis=1)
        part = total[rows, :]
        mixed = (mixed / jnp.concatenate([part] * chunks, axis=1)).astype(BF16)
        head_out[:, h * 128 : h * 128 + 128] = jnp.dot(
            mixed, w_uv[h], preferred_element_type=F32
        ).astype(BF16)
    copy_out.wait()
    half = many // 2
    core = where[0] % 2
    mine = head_out[pl.ds(pl.multiple_of(core * half, half), half), :]
    theirs = head_out[pl.ds(pl.multiple_of((1 - core) * half, half), half), :]
    for b in range(w_out.shape[1] // 512):
        at_b = slice(b * 512, b * 512 + 512)
        given_ref[:, at_b] = jnp.dot(theirs, w_out[:, at_b], preferred_element_type=F32).astype(
            BF16
        )
        kept_ref[:, at_b] = jnp.dot(mine, w_out[:, at_b], preferred_element_type=F32)


def attention(placing, lengths, where, payload, prompt_latent, w_uk, w_uv, w_out, steps):
    slots, feature, span = prompt_latent.shape
    heads, latent, nope = w_uk.shape
    width = w_out.shape[1]
    rows = steps * slots * heads
    half = steps * slots // 2
    chunks = latent // 128
    return pl.pallas_call(
        attention_kernel,
        out_shape=(
            jax.ShapeDtypeStruct((half, width), BF16),
            jax.ShapeDtypeStruct((half, width), F32),
        ),
        in_specs=[SMEM_SPEC] * 3 + [ANY_SPEC] * 5,
        out_specs=(VMEM_SPEC, VMEM_SPEC),
        scratch_shapes=[
            pltpu.VMEM(payload.shape, BF16),
            pltpu.VMEM(prompt_latent.shape, BF16),
            pltpu.VMEM(w_uk.shape, BF16),
            pltpu.VMEM(w_uv.shape, BF16),
            pltpu.VMEM(w_out.shape, BF16),
            pltpu.VMEM((rows, 128), F32),
            pltpu.VMEM((rows, 128), F32),
            pltpu.VMEM((chunks, rows, 128), F32),
            pltpu.VMEM((chunks + 1, steps * slots, 128), F32),
            pltpu.VMEM((payload.shape[0] * 8, 128), F32),
            pltpu.VMEM((rows, 128), F32),
            pltpu.VMEM((rows, 128), F32),
            pltpu.VMEM((steps * slots, heads * 128), BF16),
            pltpu.SemaphoreType.DMA((4 + slots // GROUP,)),
        ],
        compiler_params=params(60),
        cost_estimate=cost(),
        name="attention",
    )(placing, lengths, where, payload, prompt_latent, w_uk, w_uv, w_out)


def share_kernel(where, kept, swapped, mine, *parts):
    block = mine.shape[1]
    z = where[0] >> 1
    for d, part in enumerate((mine,) + parts):
        at = pl.ds(pl.multiple_of((z ^ d) * block, 128), block)
        part[...] = (kept[:, at] + swapped[:, at].astype(F32)).astype(part.dtype)


def share(where, kept, swapped, z_count):
    rows, width = kept.shape
    block = width // z_count
    return pl.pallas_call(
        share_kernel,
        out_shape=(jax.ShapeDtypeStruct((rows, block), F32),)
        + (jax.ShapeDtypeStruct((rows, block), BF16),) * (z_count - 1),
        in_specs=[SMEM_SPEC] + [VMEM_SPEC] * 2,
        out_specs=(VMEM_SPEC,) * z_count,
        compiler_params=params(),
        cost_estimate=cost(),
        name="share",
    )(where, kept, swapped)


def pack_back_kernel(placing, second, mine, *rest):
    parts, (out_ref, total, rows) = rest[:-3], rest[-3:]
    slots = placing.shape[0]
    blocks = mine.shape[1] // 128
    steps = mine.shape[0] // slots
    context_rows = second.shape[1]
    whole = mine[...]
    for part in parts:
        whole = whole + part[...].astype(F32)
    for b in range(blocks):
        total[b] = whole[:, 128 * b : 128 * b + 128]
    out_ref[:, :context_rows, :] = second[...]
    rows[...] = jnp.zeros(rows.shape, F32)

    def one(i, carry):
        dest, rank = split(placing[i])
        for s in range(steps):
            for b in range(blocks):
                at = dest * (8 * blocks) + 8 * b + steps * rank + s
                rows[pl.ds(at, 1), :] = total[b, pl.ds(slots * s + i, 1), :]
        return carry

    lax.fori_loop(0, slots, one, 0, unroll=4)
    out_ref[:, context_rows:, :] = (
        rows[...].reshape(out_ref.shape[0], 8 * blocks, 128).astype(BF16)
    )


def pack_back(placing, second, mine, parts):
    pool_count, context_rows, _ = second.shape
    blocks = mine.shape[1] // 128
    return pl.pallas_call(
        pack_back_kernel,
        out_shape=jax.ShapeDtypeStruct((pool_count, context_rows + 8 * blocks, 128), BF16),
        in_specs=[SMEM_SPEC] + [VMEM_SPEC] * (2 + len(parts)),
        out_specs=VMEM_SPEC,
        scratch_shapes=[
            pltpu.VMEM((blocks, mine.shape[0], 128), F32),
            pltpu.VMEM((pool_count * 8 * blocks, 128), F32),
        ],
        compiler_params=params(),
        cost_estimate=cost(),
        name="pack_back",
    )(placing, second, mine, *parts)


def unpack_back_kernel(steps, arrival, packed, out_ref, rows, total):
    slots = out_ref.shape[0] // steps
    blocks = out_ref.shape[1] // 128
    first = packed.shape[1] - 8 * blocks
    rows[...] = packed[:, first:, :].astype(F32).reshape(rows.shape)

    def one(j, carry):
        owner, rank = split(arrival[j])
        for b in range(blocks):
            at = owner * (8 * blocks) + 8 * b + steps * rank
            total[b, pl.ds(steps * j, steps), :] = rows[pl.ds(at, steps), :]
        return carry

    lax.fori_loop(0, slots, one, 0, unroll=4)
    for b in range(blocks):
        out_ref[:, 128 * b : 128 * b + 128] = total[b].astype(BF16)


def unpack_back(arrival, packed, steps, slots, block):
    return pl.pallas_call(
        functools.partial(unpack_back_kernel, steps),
        out_shape=jax.ShapeDtypeStruct((steps * slots, block), BF16),
        in_specs=[SMEM_SPEC, VMEM_SPEC],
        out_specs=VMEM_SPEC,
        scratch_shapes=[
            pltpu.VMEM((packed.shape[0] * 8 * (block // 128), 128), F32),
            pltpu.VMEM((block // 128, steps * slots, 128), F32),
        ],
        compiler_params=params(),
        cost_estimate=cost(),
        name="unpack_back",
    )(arrival, packed)


def assemble_kernel(where, *rest):
    parts, (out_ref, part, whole) = rest[:-3], rest[-3:]
    slots, steps, width = out_ref.shape
    z_count = len(parts) // 2
    block = width // z_count
    core, z = where[0] & 1, where[0] >> 1
    for n, ref in enumerate(parts):
        side = core if n < z_count else 1 - core
        start = (z ^ (n % z_count)) * (block // 128)
        for b in range(block // 128):
            part[...] = ref[:, 128 * b : 128 * b + 128].astype(F32)
            for s in range(steps // 2):
                whole[start + b, pl.ds((steps // 2) * side + s, slots, stride=steps), :] = part[
                    pl.ds(s, slots, stride=steps // 2), :
                ]
    for j in range(slots):
        for b in range(width // 128):
            out_ref[j, :, 128 * b : 128 * b + 128] = whole[
                b, steps * j : steps * j + steps, :
            ].astype(BF16)


def assemble(where, parts, slots, steps, width):
    return pl.pallas_call(
        assemble_kernel,
        out_shape=jax.ShapeDtypeStruct((slots, steps, width), BF16),
        in_specs=[SMEM_SPEC] + [VMEM_SPEC] * len(parts),
        out_specs=VMEM_SPEC,
        scratch_shapes=[
            pltpu.VMEM((parts[0].shape[0], 128), F32),
            pltpu.VMEM((width // 128, slots * steps, 128), F32),
        ],
        compiler_params=params(),
        cost_estimate=cost(),
        name="assemble",
    )(where, *parts)


def exchange(x):
    return lax.all_to_all(x, "pool", split_axis=0, concat_axis=0, tiled=True)


def body(prompt_latent, prompt_lengths, decode_slot, new_latent, queries, w_uk, w_uv, w_out):
    pool_count = lax.axis_size("pool")
    tp_count = lax.axis_size("tp")
    tp_index = lax.axis_index("tp")
    latent_t = prompt_latent.transpose(0, 2, 1)
    steps, slots, heads, width = queries.shape
    span, feature = prompt_latent.shape[1:]
    piece = span // tp_count
    out_width = w_out.shape[1]
    z_count = tp_count // 2
    where = jnp.stack([tp_index, lax.axis_index("pool")]).astype(jnp.int32)
    swap = [(i, i ^ 1) for i in range(tp_count)]
    hops = [[(i, i ^ (2 * d)) for i in range(tp_count)] for d in range(1, z_count)]

    payload, arrival, lengths = pack_queries(
        decode_slot, prompt_lengths, where, queries, new_latent, pool_count
    )
    payload = exchange(payload)
    first, second, placing = pack_context(decode_slot, where, latent_t, piece, pool_count)
    payload, first = lax.optimization_barrier((payload, first))
    first = exchange(first)

    given, kept = attention(
        placing, prompt_lengths, where, payload, latent_t, w_uk, w_uv, w_out, steps
    )

    swapped = lax.ppermute(given, "tp", swap)
    mine, *parts = share(where, kept, swapped, z_count)
    parts = [lax.ppermute(part, "tp", hop) for part, hop in zip(parts, hops)]

    back = pack_back(placing, second, mine, parts)
    back, first = lax.optimization_barrier((back, first))
    back = exchange(back)
    context = place(0, FIRST_RANKS, arrival, lengths, where, first, piece, feature)
    back, context = lax.optimization_barrier((back, context))

    own = unpack_back(arrival, back, steps // 2, slots, out_width // z_count)
    parts = [own] + [lax.ppermute(own, "tp", hop) for hop in hops]
    parts = parts + [lax.ppermute(part, "tp", swap) for part in parts]
    context = place(FIRST_RANKS, CAP, arrival, lengths, where, back, piece, feature, context)
    decoded = assemble(where, parts, slots, steps, out_width)
    return decoded, context


def solution(mesh):
    in_specs = (
        P("pool", None, None),
        P(),
        P(),
        P(None, "pool", None),
        P(None, "pool", "tp", None),
        P("tp", None, None),
        P("tp", None, None),
        P("tp", None),
    )
    out_specs = (P("pool", None, None), P("pool", "tp", None))
    return jax.shard_map(body, mesh=mesh, in_specs=in_specs, out_specs=out_specs, check_vma=False)
```

```python
import functools
import math

import jax
import jax.numpy as jnp
from jax import lax
from jax.experimental import pallas as pl
from jax.experimental.pallas import tpu as pltpu
from jax.sharding import PartitionSpec as P

ROPE = 64
NOPE = 128
CAP = 4
GROUP = 4
FLOOR = -1e30
BF16 = jnp.bfloat16
F32 = jnp.float32

MIB = 1024 * 1024
SMEM_SPEC = pl.BlockSpec(memory_space=pltpu.SMEM)
VMEM_SPEC = pl.BlockSpec(memory_space=pltpu.VMEM)
ANY_SPEC = pl.BlockSpec(memory_space=pl.ANY)
NT = (((1,), (1,)), ((), ()))


def params(mib=16):
    return pltpu.CompilerParams(vmem_limit_bytes=mib * MIB)


def cost(flops=1000, bytes_accessed=1000):
    return pl.CostEstimate(flops=flops, bytes_accessed=bytes_accessed, transcendentals=0)


def split(cell):
    return cell // CAP, cell % CAP


def pack_queries_kernel(
    decode_slot, prompt_lengths, where, q_hbm, n_hbm,
    out_ref, arrival, lengths,
    q_ref, n_ref, new_rows, tails, sems,
):
    steps, slots, heads, width = q_ref.shape
    rows = steps * heads
    blocks = n_ref.shape[2] // 128
    copy_n = pltpu.make_async_copy(n_hbm, n_ref, sems.at[0])
    copy_q = pltpu.make_async_copy(q_hbm, q_ref, sems.at[1])
    copy_n.start()
    copy_q.start()
    first = where[1] * slots

    def locate(p, carry):
        rank = jnp.int32(0)
        for k in range(slots):
            inner = decode_slot[p * slots + k] - first
            hit = (inner >= 0) & (inner < slots)
            at = jnp.where(hit, inner, slots)
            arrival[at] = p * CAP + rank
            lengths[at] = prompt_lengths[p * slots + k]
            rank = rank + hit.astype(jnp.int32)
        return carry

    lax.fori_loop(0, out_ref.shape[0], locate, 0)
    tails[...] = jnp.zeros(tails.shape, F32)
    copy_n.wait()
    new_rows[...] = n_ref[...].astype(F32)
    copy_q.wait()

    def one(j, carry):
        dest, rank = split(arrival[j])
        x = q_ref[:, j].astype(F32)
        nope = x[:, :, :NOPE].reshape(rows, NOPE)
        rope = x[:, :, NOPE:].reshape(rows, ROPE)
        rope = jnp.concatenate([rope[: rows // 2], rope[rows // 2 :]], axis=1)
        fresh = jnp.concatenate([new_rows[s, pl.ds(j, 1), :] for s in range(steps)], axis=0)
        body = [fresh[:, 128 * b : 128 * b + 128] for b in range(blocks)]
        last = fresh[:, 128 * blocks :]
        cell = jnp.concatenate([nope, rope] + body, axis=0)
        out_ref[dest, pl.ds(pl.multiple_of(rank * 64, 64), 64), :] = cell.astype(BF16)
        tails[pl.ds(dest * 8 + rank * 2, 2), :] = jnp.concatenate(
            [last[: steps // 2], last[steps // 2 :]], axis=1
        )
        return carry

    lax.fori_loop(0, slots, one, 0, unroll=4)
    out_ref[:, 256:264, :] = tails[...].reshape(out_ref.shape[0], 8, 128).astype(BF16)


def pack_queries(decode_slot, prompt_lengths, where, queries, new_latent, pool_count):
    slots = queries.shape[1]
    return pl.pallas_call(
        pack_queries_kernel,
        out_shape=(
            jax.ShapeDtypeStruct((pool_count, 264, 128), BF16),
            jax.ShapeDtypeStruct((slots + 8,), jnp.int32),
            jax.ShapeDtypeStruct((slots + 8,), jnp.int32),
        ),
        in_specs=[SMEM_SPEC] * 3 + [ANY_SPEC] * 2,
        out_specs=(VMEM_SPEC, SMEM_SPEC, SMEM_SPEC),
        scratch_shapes=[
            pltpu.VMEM(queries.shape, BF16),
            pltpu.VMEM(new_latent.shape, BF16),
            pltpu.VMEM(new_latent.shape, F32),
            pltpu.VMEM((pool_count * 8, 128), F32),
            pltpu.SemaphoreType.DMA((2,)),
        ],
        compiler_params=params(60),
        cost_estimate=cost(),
        name="pack_queries",
    )(decode_slot, prompt_lengths, where, queries, new_latent)


def pack_context_kernel(
    decode_slot, where, p_ref, out_ref, placing, counts, buf, sems
):
    slots, feature, window = buf.shape
    blocks = feature // 128
    piece = out_ref.shape[2] * 128 // feature
    chunk = slots // sems.shape[0]
    row = where[0] * piece
    start = pl.multiple_of(jnp.where(row + piece > window, p_ref.shape[2] - window, 0), 128)
    copies = [
        pltpu.make_async_copy(
            p_ref.at[pl.ds(k * chunk, chunk), :, pl.ds(start, window)],
            buf.at[pl.ds(k * chunk, chunk)],
            sems.at[k],
        )
        for k in range(sems.shape[0])
    ]
    for copy in copies:
        copy.start()
    bits = slots.bit_length() - 1
    for p in range(counts.shape[0]):
        counts[p] = 0
    for g in range(slots):
        owner = decode_slot[where[1] * slots + g] >> bits
        rank = counts[owner]
        counts[owner] = rank + 1
        placing[g] = owner * CAP + rank
    pick = lax.broadcasted_iota(jnp.int32, (piece, window), 1) - (
        row - start + lax.broadcasted_iota(jnp.int32, (piece, window), 0)
    )
    pick = jnp.where(pick == 0, 1.0, 0.0).astype(BF16)

    for k, copy in enumerate(copies):
        copy.wait()

        def one(n, carry):
            g = k * chunk + n
            dest, rank = split(placing[g])
            turned = lax.dot_general(pick, buf[g], NT, preferred_element_type=F32)
            last = turned[:, 128 * blocks :]
            last = jnp.concatenate([last[: piece // 2], last[piece // 2 :]], axis=1)
            out_ref[dest, rank] = jnp.concatenate(
                [turned[:, 128 * b : 128 * b + 128] for b in range(blocks)] + [last], axis=0
            ).astype(BF16)
            return carry

        lax.fori_loop(0, chunk, one, 0, unroll=2)


def pack_context(decode_slot, where, prompt_latent, piece, pool_count):
    slots, feature, _ = prompt_latent.shape
    rows = piece * feature // 128
    return pl.pallas_call(
        pack_context_kernel,
        out_shape=(
            jax.ShapeDtypeStruct((pool_count, CAP, rows, 128), BF16),
            jax.ShapeDtypeStruct((slots,), jnp.int32),
        ),
        in_specs=[SMEM_SPEC, SMEM_SPEC, ANY_SPEC],
        out_specs=(VMEM_SPEC, SMEM_SPEC),
        scratch_shapes=[
            pltpu.SMEM((pool_count,), jnp.int32),
            pltpu.VMEM((slots, feature, 256), BF16),
            pltpu.SemaphoreType.DMA((4,)),
        ],
        compiler_params=params(60),
        cost_estimate=cost(),
        name="pack_context",
    )(decode_slot, where, prompt_latent)


def unpack_piece(packed, row, first_row, length, piece, feature):
    blocks = feature // 128
    parts = [packed[(*row, pl.ds(b * piece, piece), slice(None))] for b in range(blocks)]
    last = packed[(*row, pl.ds(blocks * piece, piece // 2), slice(None))].astype(F32)
    last = jnp.concatenate([last[:, :64], last[:, 64:]], axis=0).astype(BF16)
    whole = jnp.concatenate(parts + [last], axis=1)
    position = first_row + lax.broadcasted_iota(jnp.int32, whole.shape, 0)
    return jnp.where(position < length, whole.astype(F32), 0.0).astype(BF16)


def place_kernel(arrival, lengths, where, packed, out_ref, inbox, outbox, in_sems, out_sems):
    slots, piece, feature = out_ref.shape
    first_row = where[0] * piece

    def copy_in(j):
        owner, rank = split(arrival[j])
        return pltpu.make_async_copy(packed.at[owner, rank], inbox.at[j], in_sems.at[j])

    def copy_out(j):
        return pltpu.make_async_copy(outbox.at[j], out_ref.at[j], out_sems.at[j])

    def each(action):
        def step(j, carry):
            action(j)
            return carry

        lax.fori_loop(0, slots, step, 0)

    def work(j):
        copy_in(j).wait()
        outbox[j] = unpack_piece(inbox, (j,), first_row, lengths[j], piece, feature)
        copy_out(j).start()

    each(lambda j: copy_in(j).start())
    each(work)
    each(lambda j: copy_out(j).wait())


def place(arrival, lengths, where, packed, piece, feature):
    slots = arrival.shape[0] - 8
    rows = packed.shape[-2]
    return pl.pallas_call(
        place_kernel,
        out_shape=jax.ShapeDtypeStruct((slots, piece, feature), BF16),
        in_specs=[SMEM_SPEC] * 3 + [ANY_SPEC],
        out_specs=ANY_SPEC,
        scratch_shapes=[
            pltpu.VMEM((slots, rows, 128), BF16),
            pltpu.VMEM((slots, piece, feature), BF16),
            pltpu.SemaphoreType.DMA((slots,)),
            pltpu.SemaphoreType.DMA((slots,)),
        ],
        compiler_params=params(),
        cost_estimate=cost(bytes_accessed=12_000_000),
        name="place_context",
    )(arrival, lengths, where, packed)


def attention_kernel(
    placing, lengths, where, payload_hbm, p_hbm, w_uk_hbm, w_uv_hbm, w_out_hbm,
    given_ref, kept_ref,
    payload, prompt, w_uk, w_uv, w_out,
    q_nope, q_rope, acc, fresh, tails, fresh_score, total, head_out, sems,
):
    steps = 4
    heads, latent, nope = w_uk.shape
    slots, feature, span = prompt.shape
    chunks = latent // 128
    per_step = slots * heads
    many = slots * steps
    scale = 1.0 / math.sqrt(nope + ROPE)
    first = where[1] * slots
    copy_payload = pltpu.make_async_copy(payload_hbm, payload, sems.at[0])
    copy_uk = pltpu.make_async_copy(w_uk_hbm, w_uk, sems.at[1])
    copy_uv = pltpu.make_async_copy(w_uv_hbm, w_uv, sems.at[2])
    copy_out = pltpu.make_async_copy(w_out_hbm, w_out, sems.at[3])

    def copy_prompt(k):
        part = pl.ds(k * GROUP, GROUP)
        return pltpu.make_async_copy(p_hbm.at[part], prompt.at[part], sems.at[4 + k])

    copy_payload.start()
    copy_uk.start()
    for k in range(slots // GROUP):
        copy_prompt(k).start()
    copy_uv.start()
    copy_out.start()

    def spread(ref, i, lead=()):
        return jnp.concatenate(
            [
                ref[(*lead, pl.ds(pl.multiple_of(per_step * s + heads * i, 8), heads), slice(None))]
                for s in range(steps)
            ],
            axis=0,
        )

    def collect(ref, i, value, lead=()):
        for s in range(steps):
            ref[(*lead, pl.ds(pl.multiple_of(per_step * s + heads * i, 8), heads), slice(None))] = (
                value[heads * s : heads * s + heads]
            )

    copy_payload.wait()
    tails[...] = payload[:, 256:264, :].astype(F32).reshape(tails.shape)

    def unpack(i, carry):
        dest, rank = split(placing[i])
        cell = payload[dest, pl.ds(pl.multiple_of(rank * 64, 64), 64), :].astype(F32)
        collect(q_nope, i, cell[:32])
        rope = jnp.concatenate([cell[32:48, :64], cell[32:48, 64:]], axis=0)
        collect(q_rope, i, jnp.concatenate([rope, jnp.zeros_like(rope)], axis=1))
        for b in range(chunks):
            fresh[b, pl.ds(steps * i, steps), :] = cell[48 + 4 * b : 52 + 4 * b]
        last = tails[pl.ds(dest * 8 + rank * 2, 2), :]
        last = jnp.concatenate([last[:, :64], last[:, 64:]], axis=0)
        fresh[chunks, pl.ds(steps * i, steps), :] = jnp.concatenate(
            [last, jnp.zeros_like(last)], axis=1
        )
        return carry

    lax.fori_loop(0, slots, unpack, 0, unroll=4)
    copy_uk.wait()
    for h in range(heads):
        rows = pl.ds(h, many, stride=heads)
        a = lax.dot_general(
            q_nope[rows, :].astype(BF16), w_uk[h], NT, preferred_element_type=F32
        )
        a = a.astype(BF16).astype(F32)
        for c in range(chunks):
            acc[c, rows, :] = a[:, 128 * c : 128 * c + 128]
    keys = jnp.concatenate([fresh[b] for b in range(chunks + 1)], axis=1).astype(BF16)

    def score(k, carry):
        rows = pl.ds(pl.multiple_of(k * 128, 128), 128)
        q = jnp.concatenate(
            [acc[c, rows, :] for c in range(chunks)] + [q_rope[rows, :]], axis=1
        ).astype(BF16)
        fresh_score[rows, :] = scale * lax.dot_general(q, keys, NT, preferred_element_type=F32)
        return carry

    lax.fori_loop(0, per_step * steps // 128, score, 0)

    def one(i):
        q = jnp.concatenate(
            [spread(acc, i, (c,)) for c in range(chunks)] + [spread(q_rope, i)[:, :ROPE]], axis=1
        ).astype(BF16)
        s_prompt = scale * jnp.dot(q, prompt[i], preferred_element_type=F32)
        s_fresh = spread(fresh_score, i)
        column = lax.broadcasted_iota(jnp.int32, s_prompt.shape, 1)
        s_prompt = jnp.where(column < lengths[first + i], s_prompt, FLOOR)
        step_of = lax.broadcasted_iota(jnp.int32, s_fresh.shape, 0) // heads
        column = lax.broadcasted_iota(jnp.int32, s_fresh.shape, 1) - steps * i
        s_fresh = jnp.where((column >= 0) & (column <= step_of), s_fresh, FLOOR)
        peak = jnp.maximum(
            jnp.max(s_prompt, axis=1, keepdims=True), jnp.max(s_fresh, axis=1, keepdims=True)
        )
        w_prompt = jnp.exp(s_prompt - peak)
        w_fresh = jnp.exp(s_fresh - peak)
        sums = jnp.sum(w_prompt, axis=1, keepdims=True) + jnp.sum(w_fresh, axis=1, keepdims=True)
        mixed = lax.dot_general(
            w_prompt.astype(BF16), prompt[i, :latent], NT, preferred_element_type=F32
        )
        for c in range(chunks):
            collect(acc, i, mixed[:, 128 * c : 128 * c + 128], (c,))
        collect(fresh_score, i, w_fresh)
        collect(total, i, jnp.broadcast_to(sums, s_fresh.shape))

    def attend(k, carry):
        copy_prompt(k).wait()
        for n in range(GROUP):
            one(k * GROUP + n)
        return carry

    lax.fori_loop(0, slots // GROUP, attend, 0)

    values = jnp.concatenate([fresh[b] for b in range(chunks)], axis=1).astype(BF16)
    copy_uv.wait()
    for h in range(heads):
        rows = pl.ds(h, many, stride=heads)
        mixed = jnp.dot(fresh_score[rows, :].astype(BF16), values, preferred_element_type=F32)
        mixed = mixed + jnp.concatenate([acc[c, rows, :] for c in range(chunks)], axis=1)
        part = total[rows, :]
        mixed = (mixed / jnp.concatenate([part] * chunks, axis=1)).astype(BF16)
        head_out[:, h * 128 : h * 128 + 128] = jnp.dot(
            mixed, w_uv[h], preferred_element_type=F32
        ).astype(BF16)
    copy_out.wait()
    half = many // 2
    core = where[0] % 2
    mine = head_out[pl.ds(pl.multiple_of(core * half, half), half), :]
    theirs = head_out[pl.ds(pl.multiple_of((1 - core) * half, half), half), :]
    for b in range(w_out.shape[1] // 512):
        at_b = slice(b * 512, b * 512 + 512)
        given_ref[:, at_b] = jnp.dot(theirs, w_out[:, at_b], preferred_element_type=F32).astype(
            BF16
        )
        kept_ref[:, at_b] = jnp.dot(mine, w_out[:, at_b], preferred_element_type=F32)


def attention(placing, lengths, where, payload, prompt_latent, w_uk, w_uv, w_out, steps):
    slots, feature, span = prompt_latent.shape
    heads, latent, nope = w_uk.shape
    width = w_out.shape[1]
    rows = steps * slots * heads
    half = steps * slots // 2
    chunks = latent // 128
    return pl.pallas_call(
        attention_kernel,
        out_shape=(
            jax.ShapeDtypeStruct((half, width), BF16),
            jax.ShapeDtypeStruct((half, width), F32),
        ),
        in_specs=[SMEM_SPEC] * 3 + [ANY_SPEC] * 5,
        out_specs=(VMEM_SPEC, VMEM_SPEC),
        scratch_shapes=[
            pltpu.VMEM(payload.shape, BF16),
            pltpu.VMEM(prompt_latent.shape, BF16),
            pltpu.VMEM(w_uk.shape, BF16),
            pltpu.VMEM(w_uv.shape, BF16),
            pltpu.VMEM(w_out.shape, BF16),
            pltpu.VMEM((rows, 128), F32),
            pltpu.VMEM((rows, 128), F32),
            pltpu.VMEM((chunks, rows, 128), F32),
            pltpu.VMEM((chunks + 1, steps * slots, 128), F32),
            pltpu.VMEM((payload.shape[0] * 8, 128), F32),
            pltpu.VMEM((rows, 128), F32),
            pltpu.VMEM((rows, 128), F32),
            pltpu.VMEM((steps * slots, heads * 128), BF16),
            pltpu.SemaphoreType.DMA((4 + slots // GROUP,)),
        ],
        compiler_params=params(60),
        cost_estimate=cost(),
        name="attention",
    )(placing, lengths, where, payload, prompt_latent, w_uk, w_uv, w_out)


def share_kernel(where, kept, swapped, mine, *parts):
    block = mine.shape[1]
    z = where[0] >> 1
    for d, part in enumerate((mine,) + parts):
        at = pl.ds(pl.multiple_of((z ^ d) * block, 128), block)
        part[...] = (kept[:, at] + swapped[:, at].astype(F32)).astype(part.dtype)


def share(where, kept, swapped, z_count):
    rows, width = kept.shape
    block = width // z_count
    return pl.pallas_call(
        share_kernel,
        out_shape=(jax.ShapeDtypeStruct((rows, block), F32),)
        + (jax.ShapeDtypeStruct((rows, block), BF16),) * (z_count - 1),
        in_specs=[SMEM_SPEC] + [VMEM_SPEC] * 2,
        out_specs=(VMEM_SPEC,) * z_count,
        compiler_params=params(),
        cost_estimate=cost(),
        name="share",
    )(where, kept, swapped)


def pack_back_kernel(placing, mine, *rest):
    parts, (out_ref, total, rows) = rest[:-3], rest[-3:]
    slots = placing.shape[0]
    blocks = mine.shape[1] // 128
    steps = mine.shape[0] // slots
    whole = mine[...]
    for part in parts:
        whole = whole + part[...].astype(F32)
    for b in range(blocks):
        total[b] = whole[:, 128 * b : 128 * b + 128]
    rows[...] = jnp.zeros(rows.shape, F32)

    def one(i, carry):
        dest, rank = split(placing[i])
        for s in range(steps):
            for b in range(blocks):
                at = dest * (8 * blocks) + 8 * b + steps * rank + s
                rows[pl.ds(at, 1), :] = total[b, pl.ds(slots * s + i, 1), :]
        return carry

    lax.fori_loop(0, slots, one, 0, unroll=4)
    out_ref[...] = rows[...].reshape(out_ref.shape).astype(BF16)


def pack_back(placing, mine, parts, pool_count):
    blocks = mine.shape[1] // 128
    return pl.pallas_call(
        pack_back_kernel,
        out_shape=jax.ShapeDtypeStruct((pool_count, 8 * blocks, 128), BF16),
        in_specs=[SMEM_SPEC] + [VMEM_SPEC] * (1 + len(parts)),
        out_specs=VMEM_SPEC,
        scratch_shapes=[
            pltpu.VMEM((blocks, mine.shape[0], 128), F32),
            pltpu.VMEM((pool_count * 8 * blocks, 128), F32),
        ],
        compiler_params=params(),
        cost_estimate=cost(),
        name="pack_back",
    )(placing, mine, *parts)


def unpack_back_kernel(steps, arrival, packed, out_ref, rows, total):
    slots = out_ref.shape[0] // steps
    blocks = out_ref.shape[1] // 128
    rows[...] = packed[...].astype(F32).reshape(rows.shape)

    def one(j, carry):
        owner, rank = split(arrival[j])
        for b in range(blocks):
            at = owner * (8 * blocks) + 8 * b + steps * rank
            total[b, pl.ds(steps * j, steps), :] = rows[pl.ds(at, steps), :]
        return carry

    lax.fori_loop(0, slots, one, 0, unroll=4)
    for b in range(blocks):
        out_ref[:, 128 * b : 128 * b + 128] = total[b].astype(BF16)


def unpack_back(arrival, packed, steps, slots, block):
    return pl.pallas_call(
        functools.partial(unpack_back_kernel, steps),
        out_shape=jax.ShapeDtypeStruct((steps * slots, block), BF16),
        in_specs=[SMEM_SPEC, VMEM_SPEC],
        out_specs=VMEM_SPEC,
        scratch_shapes=[
            pltpu.VMEM((packed.shape[0] * 8 * (block // 128), 128), F32),
            pltpu.VMEM((block // 128, steps * slots, 128), F32),
        ],
        compiler_params=params(),
        cost_estimate=cost(),
        name="unpack_back",
    )(arrival, packed)


def assemble_kernel(where, *rest):
    parts, (out_ref, part, whole) = rest[:-3], rest[-3:]
    slots, steps, width = out_ref.shape
    z_count = len(parts) // 2
    block = width // z_count
    core, z = where[0] & 1, where[0] >> 1
    for n, ref in enumerate(parts):
        side = core if n < z_count else 1 - core
        start = (z ^ (n % z_count)) * (block // 128)
        for b in range(block // 128):
            part[...] = ref[:, 128 * b : 128 * b + 128].astype(F32)
            for s in range(steps // 2):
                whole[start + b, pl.ds((steps // 2) * side + s, slots, stride=steps), :] = part[
                    pl.ds(s, slots, stride=steps // 2), :
                ]
    for j in range(slots):
        for b in range(width // 128):
            out_ref[j, :, 128 * b : 128 * b + 128] = whole[
                b, steps * j : steps * j + steps, :
            ].astype(BF16)


def assemble(where, parts, slots, steps, width):
    return pl.pallas_call(
        assemble_kernel,
        out_shape=jax.ShapeDtypeStruct((slots, steps, width), BF16),
        in_specs=[SMEM_SPEC] + [VMEM_SPEC] * len(parts),
        out_specs=VMEM_SPEC,
        scratch_shapes=[
            pltpu.VMEM((parts[0].shape[0], 128), F32),
            pltpu.VMEM((width // 128, slots * steps, 128), F32),
        ],
        compiler_params=params(),
        cost_estimate=cost(),
        name="assemble",
    )(where, *parts)


def exchange(x):
    return lax.all_to_all(x, "pool", split_axis=0, concat_axis=0, tiled=True)


def body(prompt_latent, prompt_lengths, decode_slot, new_latent, queries, w_uk, w_uv, w_out):
    pool_count = lax.axis_size("pool")
    tp_count = lax.axis_size("tp")
    tp_index = lax.axis_index("tp")
    latent_t = prompt_latent.transpose(0, 2, 1)
    steps, slots, heads, width = queries.shape
    span, feature = prompt_latent.shape[1:]
    piece = span // tp_count
    out_width = w_out.shape[1]
    z_count = tp_count // 2
    where = jnp.stack([tp_index, lax.axis_index("pool")]).astype(jnp.int32)
    swap = [(i, i ^ 1) for i in range(tp_count)]
    hops = [[(i, i ^ (2 * d)) for i in range(tp_count)] for d in range(1, z_count)]

    payload, arrival, lengths = pack_queries(
        decode_slot, prompt_lengths, where, queries, new_latent, pool_count
    )
    payload = exchange(payload)
    first, placing = pack_context(decode_slot, where, latent_t, piece, pool_count)
    payload, first = lax.optimization_barrier((payload, first))
    first = exchange(first)

    given, kept = attention(
        placing, prompt_lengths, where, payload, latent_t, w_uk, w_uv, w_out, steps
    )

    swapped = lax.ppermute(given, "tp", swap)
    mine, *parts = share(where, kept, swapped, z_count)
    parts = [lax.ppermute(part, "tp", hop) for part, hop in zip(parts, hops)]

    back = pack_back(placing, mine, parts, pool_count)
    back, first = lax.optimization_barrier((back, first))
    back = exchange(back)
    context = place(arrival, lengths, where, first, piece, feature)
    back, context = lax.optimization_barrier((back, context))

    own = unpack_back(arrival, back, steps // 2, slots, out_width // z_count)
    parts = [own] + [lax.ppermute(own, "tp", hop) for hop in hops]
    parts = parts + [lax.ppermute(part, "tp", swap) for part in parts]
    decoded = assemble(where, parts, slots, steps, out_width)
    return decoded, context


def solution(mesh):
    in_specs = (
        P("pool", None, None),
        P(),
        P(),
        P(None, "pool", None),
        P(None, "pool", "tp", None),
        P("tp", None, None),
        P("tp", None, None),
        P("tp", None),
    )
    out_specs = (P("pool", None, None), P("pool", "tp", None))
    return jax.shard_map(body, mesh=mesh, in_specs=in_specs, out_specs=out_specs, check_vma=False)
```

```python
import functools
import math

import jax
import jax.numpy as jnp
from jax import lax
from jax.experimental import pallas as pl
from jax.experimental.pallas import tpu as pltpu
from jax.sharding import PartitionSpec as P

ROPE = 64
NOPE = 128
CAP = 4
DIRECT = 2
SPILL = 2
STRIP = 16
GROUP = 4
FLOOR = -1e30
BF16 = jnp.bfloat16
F32 = jnp.float32

MIB = 1024 * 1024
SMEM_SPEC = pl.BlockSpec(memory_space=pltpu.SMEM)
VMEM_SPEC = pl.BlockSpec(memory_space=pltpu.VMEM)
ANY_SPEC = pl.BlockSpec(memory_space=pl.ANY)
NT = (((1,), (1,)), ((), ()))


def params(mib=16):
    return pltpu.CompilerParams(vmem_limit_bytes=mib * MIB)


def cost(flops=1000, bytes_accessed=1000):
    return pl.CostEstimate(flops=flops, bytes_accessed=bytes_accessed, transcendentals=0)


def split(cell):
    return cell // CAP, cell % CAP


def pack_queries_kernel(
    decode_slot, prompt_lengths, where, q_hbm, n_hbm,
    out_ref, arrival, lengths,
    q_ref, n_ref, new_rows, tails, sems,
):
    steps, slots, heads, width = q_ref.shape
    rows = steps * heads
    blocks = n_ref.shape[2] // 128
    copy_n = pltpu.make_async_copy(n_hbm, n_ref, sems.at[0])
    copy_q = pltpu.make_async_copy(q_hbm, q_ref, sems.at[1])
    copy_n.start()
    copy_q.start()
    first = where[1] * slots

    def locate(p, carry):
        rank = jnp.int32(0)
        for k in range(slots):
            inner = decode_slot[p * slots + k] - first
            hit = (inner >= 0) & (inner < slots)
            at = jnp.where(hit, inner, slots)
            arrival[at] = p * CAP + rank
            lengths[at] = prompt_lengths[p * slots + k]
            rank = rank + hit.astype(jnp.int32)
        return carry

    lax.fori_loop(0, out_ref.shape[0], locate, 0)
    tails[...] = jnp.zeros(tails.shape, F32)
    copy_n.wait()
    new_rows[...] = n_ref[...].astype(F32)
    copy_q.wait()

    def one(j, carry):
        dest, rank = split(arrival[j])
        x = q_ref[:, j].astype(F32)
        nope = x[:, :, :NOPE].reshape(rows, NOPE)
        rope = x[:, :, NOPE:].reshape(rows, ROPE)
        rope = jnp.concatenate([rope[: rows // 2], rope[rows // 2 :]], axis=1)
        fresh = jnp.concatenate([new_rows[s, pl.ds(j, 1), :] for s in range(steps)], axis=0)
        body = [fresh[:, 128 * b : 128 * b + 128] for b in range(blocks)]
        last = fresh[:, 128 * blocks :]
        cell = jnp.concatenate([nope, rope] + body, axis=0)
        out_ref[dest, pl.ds(pl.multiple_of(rank * 64, 64), 64), :] = cell.astype(BF16)
        tails[pl.ds(dest * 8 + rank * 2, 2), :] = jnp.concatenate(
            [last[: steps // 2], last[steps // 2 :]], axis=1
        )
        return carry

    lax.fori_loop(0, slots, one, 0, unroll=4)
    out_ref[:, 256:264, :] = tails[...].reshape(out_ref.shape[0], 8, 128).astype(BF16)


def pack_queries(decode_slot, prompt_lengths, where, queries, new_latent, pool_count):
    slots = queries.shape[1]
    return pl.pallas_call(
        pack_queries_kernel,
        out_shape=(
            jax.ShapeDtypeStruct((pool_count, 264, 128), BF16),
            jax.ShapeDtypeStruct((slots + 8,), jnp.int32),
            jax.ShapeDtypeStruct((slots + 8,), jnp.int32),
        ),
        in_specs=[SMEM_SPEC] * 3 + [ANY_SPEC] * 2,
        out_specs=(VMEM_SPEC, SMEM_SPEC, SMEM_SPEC),
        scratch_shapes=[
            pltpu.VMEM(queries.shape, BF16),
            pltpu.VMEM(new_latent.shape, BF16),
            pltpu.VMEM(new_latent.shape, F32),
            pltpu.VMEM((pool_count * 8, 128), F32),
            pltpu.SemaphoreType.DMA((2,)),
        ],
        compiler_params=params(60),
        cost_estimate=cost(),
        name="pack_queries",
    )(decode_slot, prompt_lengths, where, queries, new_latent)


def padded_rows(piece, feature):
    return -(-(piece * feature // 128) // STRIP) * STRIP


def window_start(row, piece, window, span):
    return pl.multiple_of(jnp.where(row + piece > window, span - window, 0), 128)


def picker(row, start, piece, window):
    pick = lax.broadcasted_iota(jnp.int32, (piece, window), 1) - (
        row - start + lax.broadcasted_iota(jnp.int32, (piece, window), 0)
    )
    return jnp.where(pick == 0, 1.0, 0.0).astype(BF16)


def packed_piece(pick, latents):
    piece = pick.shape[0]
    blocks = latents.shape[0] // 128
    turned = lax.dot_general(pick, latents, NT, preferred_element_type=F32)
    last = turned[:, 128 * blocks :]
    last = jnp.concatenate([last[: piece // 2], last[piece // 2 :]], axis=1)
    return jnp.concatenate(
        [turned[:, 128 * b : 128 * b + 128] for b in range(blocks)] + [last], axis=0
    ).astype(BF16)


def pack_context_kernel(
    decode_slot, where, p_ref,
    out_ref, placing, leaving, coming, relay, rounds,
    counts, entered, buf, sems,
):
    slots, feature, window = buf.shape
    owners = counts.shape[0]
    padded = (out_ref.shape[1] - SPILL * STRIP) // DIRECT
    piece = padded * 128 // feature // 16 * 16
    rows = piece * feature // 128
    strips = padded // STRIP
    chunk = slots // sems.shape[0]
    row = where[0] * piece
    start = window_start(row, piece, window, p_ref.shape[2])
    copies = [
        pltpu.make_async_copy(
            p_ref.at[pl.ds(k * chunk, chunk), :, pl.ds(start, window)],
            buf.at[pl.ds(k * chunk, chunk)],
            sems.at[k],
        )
        for k in range(sems.shape[0])
    ]
    for copy in copies:
        copy.start()
    bits = slots.bit_length() - 1

    for p in range(owners):
        counts[p] = 0
    spilled = jnp.int32(0)
    for g in range(slots):
        owner = decode_slot[where[1] * slots + g] >> bits
        rank = counts[owner]
        counts[owner] = rank + 1
        placing[g] = owner * CAP + rank
        over = rank >= DIRECT
        leaving[g] = jnp.where(over, spilled, -1)
        spilled = spilled + over.astype(jnp.int32)
    pick = picker(row, start, piece, window)

    for k, copy in enumerate(copies):
        copy.wait()

        def one(n, carry):
            g = k * chunk + n
            dest, rank = split(placing[g])
            cell = packed_piece(pick, buf[g])

            @pl.when(rank < DIRECT)
            def _():
                out_ref[dest, pl.ds(pl.multiple_of(rank * padded, STRIP), rows), :] = cell

            @pl.when((rank >= DIRECT) & (leaving[g] < SPILL))
            def _():
                at = DIRECT * padded + leaving[g] * STRIP
                for m in range(strips):
                    high = min(STRIP, rows - m * STRIP)
                    out_ref[m, pl.ds(pl.multiple_of(at, STRIP), high), :] = cell[
                        m * STRIP : m * STRIP + high
                    ]

            return carry

        lax.fori_loop(0, chunk, one, 0, unroll=2)

    for q in range(owners):
        entered[q] = 0
        for e in range(SPILL):
            relay[q * SPILL + e] = 0

    def locate(p, longest):
        for q in range(owners):
            counts[q] = 0

        def look(k, state):
            spilled, left = state
            slot = decode_slot[p * slots + k]
            owner = slot >> bits
            rank = counts[owner]
            counts[owner] = rank + 1
            over = rank >= DIRECT
            hops = over & (spilled < SPILL) & (entered[owner] < SPILL)
            entry = entered[owner]

            @pl.when(hops)
            def _():
                entered[owner] = entry + 1
                relay[owner * SPILL + entry] = p * SPILL + spilled

            code = jnp.where(hops, entry, SPILL + left)
            code = jnp.where(over, code, -1)

            @pl.when(owner == where[1])
            def _():
                coming[slot & (slots - 1)] = code

            @pl.when(p == where[1])
            def _():
                leaving[k] = code

            rest = over & jnp.logical_not(hops)
            return spilled + over.astype(jnp.int32), left + rest.astype(jnp.int32)

        _, left = lax.fori_loop(0, slots, look, (jnp.int32(0), jnp.int32(0)), unroll=4)
        return jnp.maximum(longest, left)

    longest = lax.fori_loop(0, owners, locate, jnp.int32(0))
    rounds[0] = (longest + SPILL - 1) // SPILL


def pack_context(decode_slot, where, prompt_latent, piece, pool_count):
    slots, feature, _ = prompt_latent.shape
    rows = padded_rows(piece, feature)
    return pl.pallas_call(
        pack_context_kernel,
        out_shape=(
            jax.ShapeDtypeStruct((pool_count, DIRECT * rows + SPILL * STRIP, 128), BF16),
            jax.ShapeDtypeStruct((slots,), jnp.int32),
            jax.ShapeDtypeStruct((slots,), jnp.int32),
            jax.ShapeDtypeStruct((slots,), jnp.int32),
            jax.ShapeDtypeStruct((pool_count * SPILL,), jnp.int32),
            jax.ShapeDtypeStruct((1,), jnp.int32),
        ),
        in_specs=[SMEM_SPEC, SMEM_SPEC, ANY_SPEC],
        out_specs=(VMEM_SPEC,) + (SMEM_SPEC,) * 5,
        scratch_shapes=[
            pltpu.SMEM((pool_count,), jnp.int32),
            pltpu.SMEM((pool_count,), jnp.int32),
            pltpu.VMEM((slots, feature, 256), BF16),
            pltpu.SemaphoreType.DMA((4,)),
        ],
        compiler_params=params(60),
        cost_estimate=cost(),
        name="pack_context",
    )(decode_slot, where, prompt_latent)


def pack_spill_kernel(turn, leaving, where, p_ref, spill_ref, buf, sem):
    feature, window = buf.shape
    piece = spill_ref.shape[1] * 128 // feature // 16 * 16
    row = where[0] * piece
    start = window_start(row, piece, window, p_ref.shape[2])
    pick = picker(row, start, piece, window)

    def one(g, carry):
        at = leaving[g] - SPILL - turn[0] * SPILL

        @pl.when((at >= 0) & (at < SPILL))
        def _():
            copy = pltpu.make_async_copy(p_ref.at[g, :, pl.ds(start, window)], buf, sem)
            copy.start()
            copy.wait()
            cell = packed_piece(pick, buf[...])
            spill_ref[at, : cell.shape[0], :] = cell

        return carry

    lax.fori_loop(0, p_ref.shape[0], one, 0)


def pack_spill(turn, leaving, where, prompt_latent, piece):
    slots, feature, _ = prompt_latent.shape
    return pl.pallas_call(
        pack_spill_kernel,
        out_shape=jax.ShapeDtypeStruct((SPILL, padded_rows(piece, feature), 128), BF16),
        in_specs=[SMEM_SPEC] * 3 + [ANY_SPEC],
        out_specs=VMEM_SPEC,
        scratch_shapes=[pltpu.VMEM((feature, 256), BF16), pltpu.SemaphoreType.DMA],
        compiler_params=params(),
        cost_estimate=cost(),
        name="pack_spill",
    )(turn, leaving, where, prompt_latent)


def unpack_piece(packed, row, first_row, length, piece, feature):
    blocks = feature // 128
    parts = [packed[(*row, pl.ds(b * piece, piece), slice(None))] for b in range(blocks)]
    last = packed[(*row, pl.ds(blocks * piece, piece // 2), slice(None))].astype(F32)
    last = jnp.concatenate([last[:, :64], last[:, 64:]], axis=0).astype(BF16)
    whole = jnp.concatenate(parts + [last], axis=1)
    position = first_row + lax.broadcasted_iota(jnp.int32, whole.shape, 0)
    return jnp.where(position < length, whole.astype(F32), 0.0).astype(BF16)


def place_kernel(
    arrival, coming, lengths, where, direct, out_ref, inbox, outbox, in_sems, out_sems
):
    slots, piece, feature = out_ref.shape
    rows = inbox.shape[1]

    def copy_in(j):
        owner, rank = split(arrival[j])
        rank = jnp.minimum(rank, DIRECT - 1)
        source = direct.at[owner, pl.ds(pl.multiple_of(rank * rows, STRIP), rows), :]
        return pltpu.make_async_copy(source, inbox.at[j], in_sems.at[j])

    def copy_out(j):
        return pltpu.make_async_copy(outbox.at[j], out_ref.at[j], out_sems.at[j])

    def each(action):
        def step(j, carry):
            @pl.when(coming[j] < 0)
            def _():
                action(j)

            return carry

        lax.fori_loop(0, slots, step, 0)

    def work(j):
        copy_in(j).wait()
        outbox[j] = unpack_piece(inbox, (j,), where[0] * piece, lengths[j], piece, feature)
        copy_out(j).start()

    each(lambda j: copy_in(j).start())
    each(work)
    each(lambda j: copy_out(j).wait())


def place(arrival, coming, lengths, where, direct, piece, feature):
    slots = coming.shape[0]
    rows = padded_rows(piece, feature)
    return pl.pallas_call(
        place_kernel,
        out_shape=jax.ShapeDtypeStruct((slots, piece, feature), BF16),
        in_specs=[SMEM_SPEC] * 4 + [ANY_SPEC],
        out_specs=ANY_SPEC,
        scratch_shapes=[
            pltpu.VMEM((slots, rows, 128), BF16),
            pltpu.VMEM((slots, piece, feature), BF16),
            pltpu.SemaphoreType.DMA((slots,)),
            pltpu.SemaphoreType.DMA((slots,)),
        ],
        compiler_params=params(),
        cost_estimate=cost(bytes_accessed=12_000_000),
        name="place_context",
    )(arrival, coming, lengths, where, direct)


def place_strips_kernel(
    coming, lengths, where, back, context, out_ref, inbox, whole, outbox, in_sems, out_sems
):
    slots, piece, feature = out_ref.shape
    strips = inbox.shape[1]

    def copy_in(e):
        source = back.at[pl.ds(0, strips), pl.ds(e * STRIP, STRIP), :]
        return pltpu.make_async_copy(source, inbox.at[e], in_sems.at[e])

    def copy_out(j, e):
        return pltpu.make_async_copy(outbox.at[e], out_ref.at[j], out_sems.at[e])

    for e in range(SPILL):
        copy_in(e).start()
    for e in range(SPILL):
        copy_in(e).wait()
        for m in range(strips):
            whole[e, m * STRIP : m * STRIP + STRIP, :] = inbox[e, m]

    def each(action):
        def step(j, carry):
            for e in range(SPILL):

                @pl.when(coming[j] == e)
                def _():
                    action(j, e)

            return carry

        lax.fori_loop(0, slots, step, 0)

    def work(j, e):
        outbox[e] = unpack_piece(whole, (e,), where[0] * piece, lengths[j], piece, feature)
        copy_out(j, e).start()

    each(work)
    each(lambda j, e: copy_out(j, e).wait())


def place_strips(coming, lengths, where, back, context):
    slots, piece, feature = context.shape
    strips = padded_rows(piece, feature) // STRIP
    return pl.pallas_call(
        place_strips_kernel,
        out_shape=jax.ShapeDtypeStruct(context.shape, BF16),
        in_specs=[SMEM_SPEC] * 3 + [ANY_SPEC] * 2,
        out_specs=ANY_SPEC,
        scratch_shapes=[
            pltpu.VMEM((SPILL, strips, STRIP, 128), BF16),
            pltpu.VMEM((SPILL, strips * STRIP, 128), BF16),
            pltpu.VMEM((SPILL, piece, feature), BF16),
            pltpu.SemaphoreType.DMA((SPILL,)),
            pltpu.SemaphoreType.DMA((SPILL,)),
        ],
        input_output_aliases={4: 0},
        compiler_params=params(),
        cost_estimate=cost(bytes_accessed=6_000_000),
        name="place_strips",
    )(coming, lengths, where, back, context)


def place_spill_kernel(
    turn, arrival, coming, lengths, where, spill, context, out_ref, inbox, outbox, sem
):
    slots, piece, feature = out_ref.shape

    def one(j, carry):
        at = coming[j] - SPILL - turn[0] * SPILL

        @pl.when((at >= 0) & (at < SPILL))
        def _():
            owner = split(arrival[j])[0]
            copy = pltpu.make_async_copy(
                spill.at[owner, jnp.clip(at, 0, SPILL - 1)], inbox.at[0], sem
            )
            copy.start()
            copy.wait()
            outbox[...] = unpack_piece(
                inbox, (0,), where[0] * piece, lengths[j], piece, feature
            )
            copy = pltpu.make_async_copy(outbox, out_ref.at[j], sem)
            copy.start()
            copy.wait()

        return carry

    lax.fori_loop(0, slots, one, 0)


def place_spill(turn, arrival, coming, lengths, where, spill, context):
    return pl.pallas_call(
        place_spill_kernel,
        out_shape=jax.ShapeDtypeStruct(context.shape, BF16),
        in_specs=[SMEM_SPEC] * 5 + [ANY_SPEC] * 2,
        out_specs=ANY_SPEC,
        scratch_shapes=[
            pltpu.VMEM((1,) + spill.shape[-2:], BF16),
            pltpu.VMEM(context.shape[1:], BF16),
            pltpu.SemaphoreType.DMA,
        ],
        input_output_aliases={6: 0},
        compiler_params=params(),
        cost_estimate=cost(),
        name="place_spill",
    )(turn, arrival, coming, lengths, where, spill, context)


def attention_kernel(
    placing, lengths, where, payload_hbm, p_hbm, w_uk_hbm, w_uv_hbm, w_out_hbm,
    given_ref, kept_ref,
    payload, prompt, w_uk, w_uv, w_out,
    q_nope, q_rope, acc, fresh, tails, fresh_score, total, head_out, sems,
):
    steps = 4
    heads, latent, nope = w_uk.shape
    slots, feature, span = prompt.shape
    chunks = latent // 128
    per_step = slots * heads
    many = slots * steps
    scale = 1.0 / math.sqrt(nope + ROPE)
    first = where[1] * slots
    copy_payload = pltpu.make_async_copy(payload_hbm, payload, sems.at[0])
    copy_uk = pltpu.make_async_copy(w_uk_hbm, w_uk, sems.at[1])
    copy_uv = pltpu.make_async_copy(w_uv_hbm, w_uv, sems.at[2])
    copy_out = pltpu.make_async_copy(w_out_hbm, w_out, sems.at[3])

    def copy_prompt(k):
        part = pl.ds(k * GROUP, GROUP)
        return pltpu.make_async_copy(p_hbm.at[part], prompt.at[part], sems.at[4 + k])

    copy_payload.start()
    copy_uk.start()
    for k in range(slots // GROUP):
        copy_prompt(k).start()
    copy_uv.start()
    copy_out.start()

    def spread(ref, i, lead=()):
        return jnp.concatenate(
            [
                ref[(*lead, pl.ds(pl.multiple_of(per_step * s + heads * i, 8), heads), slice(None))]
                for s in range(steps)
            ],
            axis=0,
        )

    def collect(ref, i, value, lead=()):
        for s in range(steps):
            ref[(*lead, pl.ds(pl.multiple_of(per_step * s + heads * i, 8), heads), slice(None))] = (
                value[heads * s : heads * s + heads]
            )

    copy_payload.wait()
    tails[...] = payload[:, 256:264, :].astype(F32).reshape(tails.shape)

    def unpack(i, carry):
        dest, rank = split(placing[i])
        cell = payload[dest, pl.ds(pl.multiple_of(rank * 64, 64), 64), :].astype(F32)
        collect(q_nope, i, cell[:32])
        rope = jnp.concatenate([cell[32:48, :64], cell[32:48, 64:]], axis=0)
        collect(q_rope, i, jnp.concatenate([rope, jnp.zeros_like(rope)], axis=1))
        for b in range(chunks):
            fresh[b, pl.ds(steps * i, steps), :] = cell[48 + 4 * b : 52 + 4 * b]
        last = tails[pl.ds(dest * 8 + rank * 2, 2), :]
        last = jnp.concatenate([last[:, :64], last[:, 64:]], axis=0)
        fresh[chunks, pl.ds(steps * i, steps), :] = jnp.concatenate(
            [last, jnp.zeros_like(last)], axis=1
        )
        return carry

    lax.fori_loop(0, slots, unpack, 0, unroll=4)
    copy_uk.wait()
    for h in range(heads):
        rows = pl.ds(h, many, stride=heads)
        a = lax.dot_general(
            q_nope[rows, :].astype(BF16), w_uk[h], NT, preferred_element_type=F32
        )
        a = a.astype(BF16).astype(F32)
        for c in range(chunks):
            acc[c, rows, :] = a[:, 128 * c : 128 * c + 128]
    keys = jnp.concatenate([fresh[b] for b in range(chunks + 1)], axis=1).astype(BF16)

    def score(k, carry):
        rows = pl.ds(pl.multiple_of(k * 128, 128), 128)
        q = jnp.concatenate(
            [acc[c, rows, :] for c in range(chunks)] + [q_rope[rows, :]], axis=1
        ).astype(BF16)
        fresh_score[rows, :] = scale * lax.dot_general(q, keys, NT, preferred_element_type=F32)
        return carry

    lax.fori_loop(0, per_step * steps // 128, score, 0)

    def one(i):
        q = jnp.concatenate(
            [spread(acc, i, (c,)) for c in range(chunks)] + [spread(q_rope, i)[:, :ROPE]], axis=1
        ).astype(BF16)
        s_prompt = scale * jnp.dot(q, prompt[i], preferred_element_type=F32)
        s_fresh = spread(fresh_score, i)
        column = lax.broadcasted_iota(jnp.int32, s_prompt.shape, 1)
        s_prompt = jnp.where(column < lengths[first + i], s_prompt, FLOOR)
        step_of = lax.broadcasted_iota(jnp.int32, s_fresh.shape, 0) // heads
        column = lax.broadcasted_iota(jnp.int32, s_fresh.shape, 1) - steps * i
        s_fresh = jnp.where((column >= 0) & (column <= step_of), s_fresh, FLOOR)
        peak = jnp.maximum(
            jnp.max(s_prompt, axis=1, keepdims=True), jnp.max(s_fresh, axis=1, keepdims=True)
        )
        w_prompt = jnp.exp(s_prompt - peak)
        w_fresh = jnp.exp(s_fresh - peak)
        sums = jnp.sum(w_prompt, axis=1, keepdims=True) + jnp.sum(w_fresh, axis=1, keepdims=True)
        mixed = lax.dot_general(
            w_prompt.astype(BF16), prompt[i, :latent], NT, preferred_element_type=F32
        )
        for c in range(chunks):
            collect(acc, i, mixed[:, 128 * c : 128 * c + 128], (c,))
        collect(fresh_score, i, w_fresh)
        collect(total, i, jnp.broadcast_to(sums, s_fresh.shape))

    def attend(k, carry):
        copy_prompt(k).wait()
        for n in range(GROUP):
            one(k * GROUP + n)
        return carry

    lax.fori_loop(0, slots // GROUP, attend, 0)

    values = jnp.concatenate([fresh[b] for b in range(chunks)], axis=1).astype(BF16)
    copy_uv.wait()
    for h in range(heads):
        rows = pl.ds(h, many, stride=heads)
        mixed = jnp.dot(fresh_score[rows, :].astype(BF16), values, preferred_element_type=F32)
        mixed = mixed + jnp.concatenate([acc[c, rows, :] for c in range(chunks)], axis=1)
        part = total[rows, :]
        mixed = (mixed / jnp.concatenate([part] * chunks, axis=1)).astype(BF16)
        head_out[:, h * 128 : h * 128 + 128] = jnp.dot(
            mixed, w_uv[h], preferred_element_type=F32
        ).astype(BF16)
    copy_out.wait()
    half = many // 2
    core = where[0] % 2
    mine = head_out[pl.ds(pl.multiple_of(core * half, half), half), :]
    theirs = head_out[pl.ds(pl.multiple_of((1 - core) * half, half), half), :]
    for b in range(w_out.shape[1] // 512):
        at_b = slice(b * 512, b * 512 + 512)
        given_ref[:, at_b] = jnp.dot(theirs, w_out[:, at_b], preferred_element_type=F32).astype(
            BF16
        )
        kept_ref[:, at_b] = jnp.dot(mine, w_out[:, at_b], preferred_element_type=F32)


def attention(placing, lengths, where, payload, prompt_latent, w_uk, w_uv, w_out, steps):
    slots, feature, span = prompt_latent.shape
    heads, latent, nope = w_uk.shape
    width = w_out.shape[1]
    rows = steps * slots * heads
    half = steps * slots // 2
    chunks = latent // 128
    return pl.pallas_call(
        attention_kernel,
        out_shape=(
            jax.ShapeDtypeStruct((half, width), BF16),
            jax.ShapeDtypeStruct((half, width), F32),
        ),
        in_specs=[SMEM_SPEC] * 3 + [ANY_SPEC] * 5,
        out_specs=(VMEM_SPEC, VMEM_SPEC),
        scratch_shapes=[
            pltpu.VMEM(payload.shape, BF16),
            pltpu.VMEM(prompt_latent.shape, BF16),
            pltpu.VMEM(w_uk.shape, BF16),
            pltpu.VMEM(w_uv.shape, BF16),
            pltpu.VMEM(w_out.shape, BF16),
            pltpu.VMEM((rows, 128), F32),
            pltpu.VMEM((rows, 128), F32),
            pltpu.VMEM((chunks, rows, 128), F32),
            pltpu.VMEM((chunks + 1, steps * slots, 128), F32),
            pltpu.VMEM((payload.shape[0] * 8, 128), F32),
            pltpu.VMEM((rows, 128), F32),
            pltpu.VMEM((rows, 128), F32),
            pltpu.VMEM((steps * slots, heads * 128), BF16),
            pltpu.SemaphoreType.DMA((4 + slots // GROUP,)),
        ],
        compiler_params=params(60),
        cost_estimate=cost(),
        name="attention",
    )(placing, lengths, where, payload, prompt_latent, w_uk, w_uv, w_out)


def share_kernel(where, kept, swapped, mine, *parts):
    block = mine.shape[1]
    z = where[0] >> 1
    for d, part in enumerate((mine,) + parts):
        at = pl.ds(pl.multiple_of((z ^ d) * block, 128), block)
        part[...] = (kept[:, at] + swapped[:, at].astype(F32)).astype(part.dtype)


def share(where, kept, swapped, z_count):
    rows, width = kept.shape
    block = width // z_count
    return pl.pallas_call(
        share_kernel,
        out_shape=(jax.ShapeDtypeStruct((rows, block), F32),)
        + (jax.ShapeDtypeStruct((rows, block), BF16),) * (z_count - 1),
        in_specs=[SMEM_SPEC] + [VMEM_SPEC] * 2,
        out_specs=(VMEM_SPEC,) * z_count,
        compiler_params=params(),
        cost_estimate=cost(),
        name="share",
    )(where, kept, swapped)


def pack_back_kernel(placing, relay, direct, mine, *rest):
    parts, (out_ref, strips, total, rows, sem) = rest[:-5], rest[-5:]
    slots = placing.shape[0]
    blocks = mine.shape[1] // 128
    steps = mine.shape[0] // slots
    hop = SPILL * STRIP
    fetch = pltpu.make_async_copy(
        direct.at[:, pl.ds(direct.shape[1] - hop, hop), :], strips, sem
    )
    fetch.start()
    whole = mine[...]
    for part in parts:
        whole = whole + part[...].astype(F32)
    for b in range(blocks):
        total[b] = whole[:, 128 * b : 128 * b + 128]
    rows[...] = jnp.zeros(rows.shape, F32)

    def one(i, carry):
        dest, rank = split(placing[i])
        for s in range(steps):
            for b in range(blocks):
                at = dest * (8 * blocks) + 8 * b + steps * rank + s
                rows[pl.ds(at, 1), :] = total[b, pl.ds(slots * s + i, 1), :]
        return carry

    lax.fori_loop(0, slots, one, 0, unroll=4)
    out_ref[:, hop:, :] = rows[...].reshape(out_ref.shape[0], 8 * blocks, 128).astype(BF16)
    fetch.wait()
    for q in range(out_ref.shape[0]):
        for e in range(SPILL):
            came = relay[q * SPILL + e]
            at = pl.multiple_of((came % SPILL) * STRIP, STRIP)
            out_ref[q, e * STRIP : e * STRIP + STRIP, :] = strips[
                came // SPILL, pl.ds(at, STRIP), :
            ]


def pack_back(placing, relay, direct, mine, parts):
    pool_count = direct.shape[0]
    blocks = mine.shape[1] // 128
    hop = SPILL * STRIP
    return pl.pallas_call(
        pack_back_kernel,
        out_shape=jax.ShapeDtypeStruct((pool_count, hop + 8 * blocks, 128), BF16),
        in_specs=[SMEM_SPEC] * 2 + [ANY_SPEC] + [VMEM_SPEC] * (1 + len(parts)),
        out_specs=VMEM_SPEC,
        scratch_shapes=[
            pltpu.VMEM((pool_count, hop, 128), BF16),
            pltpu.VMEM((blocks, mine.shape[0], 128), F32),
            pltpu.VMEM((pool_count * 8 * blocks, 128), F32),
            pltpu.SemaphoreType.DMA,
        ],
        compiler_params=params(),
        cost_estimate=cost(),
        name="pack_back",
    )(placing, relay, direct, mine, *parts)


def unpack_back_kernel(steps, arrival, packed, out_ref, rows, total):
    slots = out_ref.shape[0] // steps
    blocks = out_ref.shape[1] // 128
    first = packed.shape[1] - 8 * blocks
    rows[...] = packed[:, first:, :].astype(F32).reshape(rows.shape)

    def one(j, carry):
        owner, rank = split(arrival[j])
        for b in range(blocks):
            at = owner * (8 * blocks) + 8 * b + steps * rank
            total[b, pl.ds(steps * j, steps), :] = rows[pl.ds(at, steps), :]
        return carry

    lax.fori_loop(0, slots, one, 0, unroll=4)
    for b in range(blocks):
        out_ref[:, 128 * b : 128 * b + 128] = total[b].astype(BF16)


def unpack_back(arrival, packed, steps, slots, block):
    return pl.pallas_call(
        functools.partial(unpack_back_kernel, steps),
        out_shape=jax.ShapeDtypeStruct((steps * slots, block), BF16),
        in_specs=[SMEM_SPEC, VMEM_SPEC],
        out_specs=VMEM_SPEC,
        scratch_shapes=[
            pltpu.VMEM((packed.shape[0] * 8 * (block // 128), 128), F32),
            pltpu.VMEM((block // 128, steps * slots, 128), F32),
        ],
        compiler_params=params(),
        cost_estimate=cost(),
        name="unpack_back",
    )(arrival, packed)


def assemble_kernel(where, *rest):
    parts, (out_ref, part, whole) = rest[:-3], rest[-3:]
    slots, steps, width = out_ref.shape
    z_count = len(parts) // 2
    block = width // z_count
    core, z = where[0] & 1, where[0] >> 1
    for n, ref in enumerate(parts):
        side = core if n < z_count else 1 - core
        start = (z ^ (n % z_count)) * (block // 128)
        for b in range(block // 128):
            part[...] = ref[:, 128 * b : 128 * b + 128].astype(F32)
            for s in range(steps // 2):
                whole[start + b, pl.ds((steps // 2) * side + s, slots, stride=steps), :] = part[
                    pl.ds(s, slots, stride=steps // 2), :
                ]
    for j in range(slots):
        for b in range(width // 128):
            out_ref[j, :, 128 * b : 128 * b + 128] = whole[
                b, steps * j : steps * j + steps, :
            ].astype(BF16)


def assemble(where, parts, slots, steps, width):
    return pl.pallas_call(
        assemble_kernel,
        out_shape=jax.ShapeDtypeStruct((slots, steps, width), BF16),
        in_specs=[SMEM_SPEC] + [VMEM_SPEC] * len(parts),
        out_specs=VMEM_SPEC,
        scratch_shapes=[
            pltpu.VMEM((parts[0].shape[0], 128), F32),
            pltpu.VMEM((width // 128, slots * steps, 128), F32),
        ],
        compiler_params=params(),
        cost_estimate=cost(),
        name="assemble",
    )(where, *parts)


def exchange(x):
    return lax.all_to_all(x, "pool", split_axis=0, concat_axis=0, tiled=True)


def body(prompt_latent, prompt_lengths, decode_slot, new_latent, queries, w_uk, w_uv, w_out):
    pool_count = lax.axis_size("pool")
    tp_count = lax.axis_size("tp")
    tp_index = lax.axis_index("tp")
    latent_t = prompt_latent.transpose(0, 2, 1)
    steps, slots, heads, width = queries.shape
    span, feature = prompt_latent.shape[1:]
    piece = span // tp_count
    out_width = w_out.shape[1]
    z_count = tp_count // 2
    where = jnp.stack([tp_index, lax.axis_index("pool")]).astype(jnp.int32)
    swap = [(i, i ^ 1) for i in range(tp_count)]
    hops = [[(i, i ^ (2 * d)) for i in range(tp_count)] for d in range(1, z_count)]

    payload, arrival, lengths = pack_queries(
        decode_slot, prompt_lengths, where, queries, new_latent, pool_count
    )
    payload = exchange(payload)
    direct, placing, leaving, coming, relay, rounds = pack_context(
        decode_slot, where, latent_t, piece, pool_count
    )
    payload, direct = lax.optimization_barrier((payload, direct))
    direct = exchange(direct)

    given, kept = attention(
        placing, prompt_lengths, where, payload, latent_t, w_uk, w_uv, w_out, steps
    )

    swapped = lax.ppermute(given, "tp", swap)
    mine, *parts = share(where, kept, swapped, z_count)
    parts = [lax.ppermute(part, "tp", hop) for part, hop in zip(parts, hops)]

    back = exchange(pack_back(placing, relay, direct, mine, parts))
    context = place(arrival, coming, lengths, where, direct, piece, feature)
    back, context = lax.optimization_barrier((back, context))
    own = unpack_back(arrival, back, steps // 2, slots, out_width // z_count)
    parts = [own] + [lax.ppermute(own, "tp", hop) for hop in hops]
    parts = parts + [lax.ppermute(part, "tp", swap) for part in parts]
    context = place_strips(coming, lengths, where, back, context)
    decoded = assemble(where, parts, slots, steps, out_width)

    def more(state):
        turn, context = state
        spill = pack_spill(turn, leaving, where, latent_t, piece)
        spill = exchange(jnp.broadcast_to(spill[None], (pool_count,) + spill.shape))
        context = place_spill(turn, arrival, coming, lengths, where, spill, context)
        return turn + 1, context

    context = lax.while_loop(
        lambda state: state[0][0] < rounds[0], more, (jnp.zeros((1,), jnp.int32), context)
    )[1]
    return decoded, context


def solution(mesh):
    in_specs = (
        P("pool", None, None),
        P(),
        P(),
        P(None, "pool", None),
        P(None, "pool", "tp", None),
        P("tp", None, None),
        P("tp", None, None),
        P("tp", None),
    )
    out_specs = (P("pool", None, None), P("pool", "tp", None))
    return jax.shard_map(body, mesh=mesh, in_specs=in_specs, out_specs=out_specs, check_vma=False)
```

```python
import functools
import math

import jax
import jax.numpy as jnp
from jax import lax
from jax.experimental import pallas as pl
from jax.experimental.pallas import tpu as pltpu
from jax.sharding import PartitionSpec as P

ROPE = 64
NOPE = 128
CAP = 4
DIRECT = 2
SPILL = 2
STRIP = 16
GROUP = 8
FLOOR = -1e30
BF16 = jnp.bfloat16
F32 = jnp.float32

MIB = 1024 * 1024
SMEM_SPEC = pl.BlockSpec(memory_space=pltpu.SMEM)
VMEM_SPEC = pl.BlockSpec(memory_space=pltpu.VMEM)
ANY_SPEC = pl.BlockSpec(memory_space=pl.ANY)
NT = (((1,), (1,)), ((), ()))


def params(mib=16):
    return pltpu.CompilerParams(vmem_limit_bytes=mib * MIB)


def cost(flops=1000, bytes_accessed=1000):
    return pl.CostEstimate(flops=flops, bytes_accessed=bytes_accessed, transcendentals=0)


def split(cell):
    return cell // CAP, cell % CAP


def pack_queries_kernel(
    decode_slot, prompt_lengths, where, q_hbm, n_hbm,
    out_ref, arrival, lengths,
    q_ref, n_ref, new_rows, tails, sems,
):
    steps, slots, heads, width = q_ref.shape
    rows = steps * heads
    blocks = n_ref.shape[2] // 128
    copy_n = pltpu.make_async_copy(n_hbm, n_ref, sems.at[0])
    copy_q = pltpu.make_async_copy(q_hbm, q_ref, sems.at[1])
    copy_n.start()
    copy_q.start()
    first = where[1] * slots

    def locate(p, carry):
        rank = jnp.int32(0)
        for k in range(slots):
            inner = decode_slot[p * slots + k] - first
            hit = (inner >= 0) & (inner < slots)
            at = jnp.where(hit, inner, slots)
            arrival[at] = p * CAP + rank
            lengths[at] = prompt_lengths[p * slots + k]
            rank = rank + hit.astype(jnp.int32)
        return carry

    lax.fori_loop(0, out_ref.shape[0], locate, 0)
    tails[...] = jnp.zeros(tails.shape, F32)
    copy_n.wait()
    new_rows[...] = n_ref[...].astype(F32)
    copy_q.wait()

    def one(j, carry):
        dest, rank = split(arrival[j])
        x = q_ref[:, j].astype(F32)
        nope = x[:, :, :NOPE].reshape(rows, NOPE)
        rope = x[:, :, NOPE:].reshape(rows, ROPE)
        rope = jnp.concatenate([rope[: rows // 2], rope[rows // 2 :]], axis=1)
        fresh = jnp.concatenate([new_rows[s, pl.ds(j, 1), :] for s in range(steps)], axis=0)
        body = [fresh[:, 128 * b : 128 * b + 128] for b in range(blocks)]
        last = fresh[:, 128 * blocks :]
        cell = jnp.concatenate([nope, rope] + body, axis=0)
        out_ref[dest, pl.ds(pl.multiple_of(rank * 64, 64), 64), :] = cell.astype(BF16)
        tails[pl.ds(dest * 8 + rank * 2, 2), :] = jnp.concatenate(
            [last[: steps // 2], last[steps // 2 :]], axis=1
        )
        return carry

    lax.fori_loop(0, slots, one, 0, unroll=4)
    out_ref[:, 256:264, :] = tails[...].reshape(out_ref.shape[0], 8, 128).astype(BF16)


def pack_queries(decode_slot, prompt_lengths, where, queries, new_latent, pool_count):
    slots = queries.shape[1]
    return pl.pallas_call(
        pack_queries_kernel,
        out_shape=(
            jax.ShapeDtypeStruct((pool_count, 264, 128), BF16),
            jax.ShapeDtypeStruct((slots + 8,), jnp.int32),
            jax.ShapeDtypeStruct((slots + 8,), jnp.int32),
        ),
        in_specs=[SMEM_SPEC] * 3 + [ANY_SPEC] * 2,
        out_specs=(VMEM_SPEC, SMEM_SPEC, SMEM_SPEC),
        scratch_shapes=[
            pltpu.VMEM(queries.shape, BF16),
            pltpu.VMEM(new_latent.shape, BF16),
            pltpu.VMEM(new_latent.shape, F32),
            pltpu.VMEM((pool_count * 8, 128), F32),
            pltpu.SemaphoreType.DMA((2,)),
        ],
        compiler_params=params(60),
        cost_estimate=cost(),
        name="pack_queries",
    )(decode_slot, prompt_lengths, where, queries, new_latent)


def padded_rows(piece, feature):
    return -(-(piece * feature // 128) // STRIP) * STRIP


def window_start(row, piece, window, span):
    return pl.multiple_of(jnp.where(row + piece > window, span - window, 0), 128)


def picker(row, start, piece, window):
    pick = lax.broadcasted_iota(jnp.int32, (piece, window), 1) - (
        row - start + lax.broadcasted_iota(jnp.int32, (piece, window), 0)
    )
    return jnp.where(pick == 0, 1.0, 0.0).astype(BF16)


def packed_piece(pick, latents):
    piece = pick.shape[0]
    blocks = latents.shape[0] // 128
    turned = lax.dot_general(pick, latents, NT, preferred_element_type=F32)
    last = turned[:, 128 * blocks :]
    last = jnp.concatenate([last[: piece // 2], last[piece // 2 :]], axis=1)
    return jnp.concatenate(
        [turned[:, 128 * b : 128 * b + 128] for b in range(blocks)] + [last], axis=0
    ).astype(BF16)


def pack_context_kernel(
    decode_slot, where, p_ref,
    out_ref, placing, later, coming, relay, rounds,
    leaving, counts, ahead, code, source, buf, sems,
):
    slots, feature, window = buf.shape
    owners = out_ref.shape[0]
    padded = (out_ref.shape[1] - SPILL * STRIP) // DIRECT
    piece = padded * 128 // feature // 16 * 16
    rows = piece * feature // 128
    strips = padded // STRIP
    chunk = slots // sems.shape[0]
    row = where[0] * piece
    start = window_start(row, piece, window, p_ref.shape[2])
    copies = [
        pltpu.make_async_copy(
            p_ref.at[pl.ds(k * chunk, chunk), :, pl.ds(start, window)],
            buf.at[pl.ds(k * chunk, chunk)],
            sems.at[k],
        )
        for k in range(sems.shape[0])
    ]
    for copy in copies:
        copy.start()
    bits = slots.bit_length() - 1

    for p in range(owners):
        counts[p] = 0
    spilled = jnp.int32(0)
    for g in range(slots):
        owner = decode_slot[where[1] * slots + g] >> bits
        rank = counts[owner]
        counts[owner] = rank + 1
        placing[g] = owner * CAP + rank
        over = rank >= DIRECT
        leaving[g] = jnp.where(over, spilled, -1)
        spilled = spilled + over.astype(jnp.int32)
    pick = picker(row, start, piece, window)

    def clear(n, carry):
        counts[n] = 0
        return carry

    lax.fori_loop(0, owners * owners, clear, 0, unroll=16)
    first = where[1] * slots

    def look(k, spilled):
        after = []
        for p in range(owners):
            slot = decode_slot[p * slots + k]
            owner = slot >> bits
            rank = counts[p * owners + owner]
            counts[p * owners + owner] = rank + 1
            over = rank >= DIRECT
            ahead[p * (SPILL + 1) + jnp.where(over, jnp.minimum(spilled[p], SPILL), SPILL)] = owner
            inner = slot - first
            at = jnp.where((inner >= 0) & (inner < slots), inner, slots)
            coming[at] = jnp.where(over, spilled[p], -1)
            source[at] = p
            after.append(spilled[p] + over.astype(jnp.int32))
        return tuple(after)

    spilled = lax.fori_loop(0, slots, look, (jnp.int32(0),) * owners)
    for q in range(owners):
        counts[q] = 0
    for n in range(owners * SPILL):
        relay[n] = 0
    longest = jnp.int32(0)
    for p in range(owners):
        hopped = jnp.int32(0)
        for n in range(SPILL):
            owner = jnp.where(n < spilled[p], ahead[p * (SPILL + 1) + n], 0)
            entry = counts[owner]
            hops = (n < spilled[p]) & (entry < SPILL)
            counts[owner] = entry + hops.astype(jnp.int32)
            relay[jnp.where(hops, owner * SPILL + entry, owners * SPILL)] = p * SPILL + n
            code[p * (SPILL + 1) + n] = jnp.where(hops, entry, SPILL + n - hopped)
            hopped = hopped + hops.astype(jnp.int32)
        code[p * (SPILL + 1) + SPILL] = SPILL - hopped
        longest = jnp.maximum(longest, spilled[p] - hopped)
    rounds[0] = (longest + SPILL - 1) // SPILL

    def coded(p, n):
        found = code[p * (SPILL + 1) + jnp.clip(n, 0, SPILL)]
        return jnp.where(n < 0, -1, jnp.where(n < SPILL, found, found + n))

    def finish(n, carry):
        coming[n] = coded(source[n], coming[n])
        later[n] = coded(where[1], leaving[n])
        return carry

    lax.fori_loop(0, slots, finish, 0, unroll=4)

    for k, copy in enumerate(copies):
        copy.wait()

        def one(n, carry):
            g = k * chunk + n
            dest, rank = split(placing[g])
            cell = packed_piece(pick, buf[g])

            @pl.when(rank < DIRECT)
            def _():
                out_ref[dest, pl.ds(pl.multiple_of(rank * padded, STRIP), rows), :] = cell

            @pl.when((rank >= DIRECT) & (leaving[g] < SPILL))
            def _():
                at = DIRECT * padded + leaving[g] * STRIP
                for m in range(strips):
                    high = min(STRIP, rows - m * STRIP)
                    out_ref[m, pl.ds(pl.multiple_of(at, STRIP), high), :] = cell[
                        m * STRIP : m * STRIP + high
                    ]

            return carry

        lax.fori_loop(0, chunk, one, 0, unroll=4)


def pack_context(decode_slot, where, prompt_latent, piece, pool_count):
    slots, feature, _ = prompt_latent.shape
    rows = padded_rows(piece, feature)
    return pl.pallas_call(
        pack_context_kernel,
        out_shape=(
            jax.ShapeDtypeStruct((pool_count, DIRECT * rows + SPILL * STRIP, 128), BF16),
            jax.ShapeDtypeStruct((slots,), jnp.int32),
            jax.ShapeDtypeStruct((slots,), jnp.int32),
            jax.ShapeDtypeStruct((slots + 8,), jnp.int32),
            jax.ShapeDtypeStruct((pool_count * SPILL + 8,), jnp.int32),
            jax.ShapeDtypeStruct((1,), jnp.int32),
        ),
        in_specs=[SMEM_SPEC, SMEM_SPEC, ANY_SPEC],
        out_specs=(VMEM_SPEC,) + (SMEM_SPEC,) * 5,
        scratch_shapes=[
            pltpu.SMEM((slots,), jnp.int32),
            pltpu.SMEM((pool_count * pool_count,), jnp.int32),
            pltpu.SMEM((pool_count * (SPILL + 1),), jnp.int32),
            pltpu.SMEM((pool_count * (SPILL + 1),), jnp.int32),
            pltpu.SMEM((slots + 8,), jnp.int32),
            pltpu.VMEM((slots, feature, 256), BF16),
            pltpu.SemaphoreType.DMA((4,)),
        ],
        compiler_params=params(60),
        cost_estimate=cost(),
        name="pack_context",
    )(decode_slot, where, prompt_latent)


def pack_spill_kernel(turn, leaving, where, p_ref, spill_ref, buf, sem):
    feature, window = buf.shape
    piece = spill_ref.shape[1] * 128 // feature // 16 * 16
    row = where[0] * piece
    start = window_start(row, piece, window, p_ref.shape[2])
    pick = picker(row, start, piece, window)

    def one(g, carry):
        at = leaving[g] - SPILL - turn[0] * SPILL

        @pl.when((at >= 0) & (at < SPILL))
        def _():
            copy = pltpu.make_async_copy(p_ref.at[g, :, pl.ds(start, window)], buf, sem)
            copy.start()
            copy.wait()
            cell = packed_piece(pick, buf[...])
            spill_ref[at, : cell.shape[0], :] = cell

        return carry

    lax.fori_loop(0, p_ref.shape[0], one, 0)


def pack_spill(turn, leaving, where, prompt_latent, piece):
    slots, feature, _ = prompt_latent.shape
    return pl.pallas_call(
        pack_spill_kernel,
        out_shape=jax.ShapeDtypeStruct((SPILL, padded_rows(piece, feature), 128), BF16),
        in_specs=[SMEM_SPEC] * 3 + [ANY_SPEC],
        out_specs=VMEM_SPEC,
        scratch_shapes=[pltpu.VMEM((feature, 256), BF16), pltpu.SemaphoreType.DMA],
        compiler_params=params(),
        cost_estimate=cost(),
        name="pack_spill",
    )(turn, leaving, where, prompt_latent)


def unpack_piece(out_ref, row, packed, at, start, first_row, length):
    piece, feature = out_ref.shape[1:]
    blocks = feature // 128
    for b in range(blocks):
        out_ref[row, :, 128 * b : 128 * b + 128] = packed[at, pl.ds(start + b * piece, piece), :]
    last = packed[at, pl.ds(start + blocks * piece, piece // 2), :].astype(F32)
    last = jnp.concatenate([last[:, :64], last[:, 64:]], axis=0)
    out_ref[row, :, 128 * blocks :] = last.astype(BF16)

    @pl.when(length < first_row + piece)
    def _():
        whole = out_ref[row].astype(F32)
        position = first_row + lax.broadcasted_iota(jnp.int32, whole.shape, 0)
        out_ref[row] = jnp.where(position < length, whole, 0.0).astype(BF16)


def place_kernel(arrival, lengths, where, direct, out_ref, outbox, sems):
    slots, piece, feature = out_ref.shape
    padded = (direct.shape[1] - SPILL * STRIP) // DIRECT
    chunk = slots // sems.shape[0]

    def copy_out(k):
        part = pl.ds(k * chunk, chunk)
        return pltpu.make_async_copy(outbox.at[part], out_ref.at[part], sems.at[k])

    def one(j, carry):
        owner, rank = split(arrival[j])
        at = pl.multiple_of(jnp.minimum(rank, DIRECT - 1) * padded, STRIP)
        unpack_piece(outbox, j, direct, owner, at, where[0] * piece, lengths[j])
        return carry

    for k in range(sems.shape[0]):
        lax.fori_loop(k * chunk, k * chunk + chunk, one, 0, unroll=2)
        copy_out(k).start()
    for k in range(sems.shape[0]):
        copy_out(k).wait()


def place(arrival, lengths, where, direct, piece, feature):
    slots = arrival.shape[0] - 8
    return pl.pallas_call(
        place_kernel,
        out_shape=jax.ShapeDtypeStruct((slots, piece, feature), BF16),
        in_specs=[SMEM_SPEC] * 3 + [VMEM_SPEC],
        out_specs=ANY_SPEC,
        scratch_shapes=[
            pltpu.VMEM((slots, piece, feature), BF16),
            pltpu.SemaphoreType.DMA((4,)),
        ],
        compiler_params=params(),
        cost_estimate=cost(bytes_accessed=12_000_000),
        name="place_context",
    )(arrival, lengths, where, direct)


def place_strips_kernel(
    coming, lengths, where, back, context, out_ref, inbox, whole, outbox, in_sems, out_sems
):
    slots, piece, feature = out_ref.shape
    strips = inbox.shape[1]

    def copy_in(e):
        source = back.at[pl.ds(0, strips), pl.ds(e * STRIP, STRIP), :]
        return pltpu.make_async_copy(source, inbox.at[e], in_sems.at[e])

    def copy_out(j, e):
        return pltpu.make_async_copy(outbox.at[e], out_ref.at[j], out_sems.at[e])

    for e in range(SPILL):
        copy_in(e).start()
    for e in range(SPILL):
        copy_in(e).wait()
        for m in range(strips):
            whole[e, m * STRIP : m * STRIP + STRIP, :] = inbox[e, m]

    def each(action):
        def step(j, carry):
            for e in range(SPILL):

                @pl.when(coming[j] == e)
                def _():
                    action(j, e)

            return carry

        lax.fori_loop(0, slots, step, 0)

    def work(j, e):
        unpack_piece(outbox, e, whole, e, 0, where[0] * piece, lengths[j])
        copy_out(j, e).start()

    each(work)
    each(lambda j, e: copy_out(j, e).wait())


def place_strips(coming, lengths, where, back, context):
    slots, piece, feature = context.shape
    strips = padded_rows(piece, feature) // STRIP
    return pl.pallas_call(
        place_strips_kernel,
        out_shape=jax.ShapeDtypeStruct(context.shape, BF16),
        in_specs=[SMEM_SPEC] * 3 + [ANY_SPEC] * 2,
        out_specs=ANY_SPEC,
        scratch_shapes=[
            pltpu.VMEM((SPILL, strips, STRIP, 128), BF16),
            pltpu.VMEM((SPILL, strips * STRIP, 128), BF16),
            pltpu.VMEM((SPILL, piece, feature), BF16),
            pltpu.SemaphoreType.DMA((SPILL,)),
            pltpu.SemaphoreType.DMA((SPILL,)),
        ],
        input_output_aliases={4: 0},
        compiler_params=params(),
        cost_estimate=cost(bytes_accessed=6_000_000),
        name="place_strips",
    )(coming, lengths, where, back, context)


def place_spill_kernel(
    turn, arrival, coming, lengths, where, spill, context, out_ref, inbox, outbox, sem
):
    slots, piece, feature = out_ref.shape

    def one(j, carry):
        at = coming[j] - SPILL - turn[0] * SPILL

        @pl.when((at >= 0) & (at < SPILL))
        def _():
            owner = split(arrival[j])[0]
            copy = pltpu.make_async_copy(
                spill.at[owner, jnp.clip(at, 0, SPILL - 1)], inbox.at[0], sem
            )
            copy.start()
            copy.wait()
            unpack_piece(outbox, 0, inbox, 0, 0, where[0] * piece, lengths[j])
            copy = pltpu.make_async_copy(outbox.at[0], out_ref.at[j], sem)
            copy.start()
            copy.wait()

        return carry

    lax.fori_loop(0, slots, one, 0)


def place_spill(turn, arrival, coming, lengths, where, spill, context):
    return pl.pallas_call(
        place_spill_kernel,
        out_shape=jax.ShapeDtypeStruct(context.shape, BF16),
        in_specs=[SMEM_SPEC] * 5 + [ANY_SPEC] * 2,
        out_specs=ANY_SPEC,
        scratch_shapes=[
            pltpu.VMEM((1,) + spill.shape[-2:], BF16),
            pltpu.VMEM((1,) + context.shape[1:], BF16),
            pltpu.SemaphoreType.DMA,
        ],
        input_output_aliases={6: 0},
        compiler_params=params(),
        cost_estimate=cost(),
        name="place_spill",
    )(turn, arrival, coming, lengths, where, spill, context)


def attention_kernel(
    placing, lengths, where, payload_hbm, p_hbm, w_uk_hbm, w_uv_hbm, w_out_hbm,
    given_ref, kept_ref,
    payload, prompt, w_uk, w_uv, w_out,
    q_nope, q_rope, acc, fresh, tails, fresh_score, total, head_out, sems,
):
    steps = 4
    heads, latent, nope = w_uk.shape
    slots, feature, span = prompt.shape
    chunks = latent // 128
    per_step = slots * heads
    many = slots * steps
    scale = 1.0 / math.sqrt(nope + ROPE)
    first = where[1] * slots
    copy_payload = pltpu.make_async_copy(payload_hbm, payload, sems.at[0])
    copy_uk = pltpu.make_async_copy(w_uk_hbm, w_uk, sems.at[1])
    copy_uv = pltpu.make_async_copy(w_uv_hbm, w_uv, sems.at[2])
    copy_out = pltpu.make_async_copy(w_out_hbm, w_out, sems.at[3])

    def copy_prompt(k):
        part = pl.ds(k * GROUP, GROUP)
        return pltpu.make_async_copy(p_hbm.at[part], prompt.at[part], sems.at[4 + k])

    copy_payload.start()
    copy_uk.start()
    for k in range(slots // GROUP):
        copy_prompt(k).start()
    copy_uv.start()
    copy_out.start()

    def spread(ref, i, lead=()):
        return jnp.concatenate(
            [
                ref[(*lead, pl.ds(pl.multiple_of(per_step * s + heads * i, 8), heads), slice(None))]
                for s in range(steps)
            ],
            axis=0,
        )

    def collect(ref, i, value, lead=()):
        for s in range(steps):
            ref[(*lead, pl.ds(pl.multiple_of(per_step * s + heads * i, 8), heads), slice(None))] = (
                value[heads * s : heads * s + heads]
            )

    copy_payload.wait()
    tails[...] = payload[:, 256:264, :].astype(F32).reshape(tails.shape)

    def unpack(i, carry):
        dest, rank = split(placing[i])
        cell = payload[dest, pl.ds(pl.multiple_of(rank * 64, 64), 64), :].astype(F32)
        collect(q_nope, i, cell[:32])
        rope = jnp.concatenate([cell[32:48, :64], cell[32:48, 64:]], axis=0)
        collect(q_rope, i, jnp.concatenate([rope, jnp.zeros_like(rope)], axis=1))
        for b in range(chunks):
            fresh[b, pl.ds(steps * i, steps), :] = cell[48 + 4 * b : 52 + 4 * b]
        last = tails[pl.ds(dest * 8 + rank * 2, 2), :]
        last = jnp.concatenate([last[:, :64], last[:, 64:]], axis=0)
        fresh[chunks, pl.ds(steps * i, steps), :] = jnp.concatenate(
            [last, jnp.zeros_like(last)], axis=1
        )
        return carry

    lax.fori_loop(0, slots, unpack, 0, unroll=4)
    copy_uk.wait()
    for h in range(heads):
        rows = pl.ds(h, many, stride=heads)
        a = lax.dot_general(
            q_nope[rows, :].astype(BF16), w_uk[h], NT, preferred_element_type=F32
        )
        a = a.astype(BF16).astype(F32)
        for c in range(chunks):
            acc[c, rows, :] = a[:, 128 * c : 128 * c + 128]
    keys = jnp.concatenate([fresh[b] for b in range(chunks + 1)], axis=1).astype(BF16)

    def score(k, carry):
        rows = pl.ds(pl.multiple_of(k * 128, 128), 128)
        q = jnp.concatenate(
            [acc[c, rows, :] for c in range(chunks)] + [q_rope[rows, :]], axis=1
        ).astype(BF16)
        fresh_score[rows, :] = scale * lax.dot_general(q, keys, NT, preferred_element_type=F32)
        return carry

    lax.fori_loop(0, per_step * steps // 128, score, 0)

    def one(i):
        q = jnp.concatenate(
            [spread(acc, i, (c,)) for c in range(chunks)] + [spread(q_rope, i)[:, :ROPE]], axis=1
        ).astype(BF16)
        s_prompt = scale * jnp.dot(q, prompt[i], preferred_element_type=F32)
        s_fresh = spread(fresh_score, i)
        column = lax.broadcasted_iota(jnp.int32, s_prompt.shape, 1)
        s_prompt = jnp.where(column < lengths[first + i], s_prompt, FLOOR)
        step_of = lax.broadcasted_iota(jnp.int32, s_fresh.shape, 0) // heads
        column = lax.broadcasted_iota(jnp.int32, s_fresh.shape, 1) - steps * i
        s_fresh = jnp.where((column >= 0) & (column <= step_of), s_fresh, FLOOR)
        peak = jnp.maximum(
            jnp.max(s_prompt, axis=1, keepdims=True), jnp.max(s_fresh, axis=1, keepdims=True)
        )
        w_prompt = jnp.exp(s_prompt - peak)
        w_fresh = jnp.exp(s_fresh - peak)
        sums = jnp.sum(w_prompt, axis=1, keepdims=True) + jnp.sum(w_fresh, axis=1, keepdims=True)
        mixed = lax.dot_general(
            w_prompt.astype(BF16), prompt[i, :latent], NT, preferred_element_type=F32
        )
        for c in range(chunks):
            collect(acc, i, mixed[:, 128 * c : 128 * c + 128], (c,))
        collect(fresh_score, i, w_fresh)
        collect(total, i, jnp.broadcast_to(sums, s_fresh.shape))

    def attend(k, carry):
        copy_prompt(k).wait()
        for n in range(GROUP):
            one(k * GROUP + n)
        return carry

    lax.fori_loop(0, slots // GROUP, attend, 0)

    values = jnp.concatenate([fresh[b] for b in range(chunks)], axis=1).astype(BF16)
    copy_uv.wait()
    for h in range(heads):
        rows = pl.ds(h, many, stride=heads)
        mixed = jnp.dot(fresh_score[rows, :].astype(BF16), values, preferred_element_type=F32)
        mixed = mixed + jnp.concatenate([acc[c, rows, :] for c in range(chunks)], axis=1)
        part = 1.0 / total[rows, :]
        mixed = (mixed * jnp.concatenate([part] * chunks, axis=1)).astype(BF16)
        head_out[:, h * 128 : h * 128 + 128] = jnp.dot(
            mixed, w_uv[h], preferred_element_type=F32
        ).astype(BF16)
    copy_out.wait()
    half = many // 2
    core = where[0] % 2
    mine = head_out[pl.ds(pl.multiple_of(core * half, half), half), :]
    theirs = head_out[pl.ds(pl.multiple_of((1 - core) * half, half), half), :]
    both = jnp.concatenate([theirs, mine], axis=0)
    for b in range(w_out.shape[1] // 512):
        at_b = slice(b * 512, b * 512 + 512)
        summed = jnp.dot(both, w_out[:, at_b], preferred_element_type=F32)
        given_ref[:, at_b] = summed[:half].astype(BF16)
        kept_ref[:, at_b] = summed[half:]


def attention(placing, lengths, where, payload, prompt_latent, w_uk, w_uv, w_out, steps):
    slots, feature, span = prompt_latent.shape
    heads, latent, nope = w_uk.shape
    width = w_out.shape[1]
    rows = steps * slots * heads
    half = steps * slots // 2
    chunks = latent // 128
    return pl.pallas_call(
        attention_kernel,
        out_shape=(
            jax.ShapeDtypeStruct((half, width), BF16),
            jax.ShapeDtypeStruct((half, width), F32),
        ),
        in_specs=[SMEM_SPEC] * 3 + [ANY_SPEC] * 5,
        out_specs=(VMEM_SPEC, VMEM_SPEC),
        scratch_shapes=[
            pltpu.VMEM(payload.shape, BF16),
            pltpu.VMEM(prompt_latent.shape, BF16),
            pltpu.VMEM(w_uk.shape, BF16),
            pltpu.VMEM(w_uv.shape, BF16),
            pltpu.VMEM(w_out.shape, BF16),
            pltpu.VMEM((rows, 128), F32),
            pltpu.VMEM((rows, 128), F32),
            pltpu.VMEM((chunks, rows, 128), F32),
            pltpu.VMEM((chunks + 1, steps * slots, 128), F32),
            pltpu.VMEM((payload.shape[0] * 8, 128), F32),
            pltpu.VMEM((rows, 128), F32),
            pltpu.VMEM((rows, 128), F32),
            pltpu.VMEM((steps * slots, heads * 128), BF16),
            pltpu.SemaphoreType.DMA((4 + slots // GROUP,)),
        ],
        compiler_params=params(60),
        cost_estimate=cost(),
        name="attention",
    )(placing, lengths, where, payload, prompt_latent, w_uk, w_uv, w_out)


def share_kernel(where, kept, swapped, mine, *parts):
    block = mine.shape[1]
    z = where[0] >> 1
    for d, part in enumerate((mine,) + parts):
        at = pl.ds(pl.multiple_of((z ^ d) * block, 128), block)
        part[...] = (kept[:, at] + swapped[:, at].astype(F32)).astype(part.dtype)


def share(where, kept, swapped, z_count):
    rows, width = kept.shape
    block = width // z_count
    return pl.pallas_call(
        share_kernel,
        out_shape=(jax.ShapeDtypeStruct((rows, block), F32),)
        + (jax.ShapeDtypeStruct((rows, block), BF16),) * (z_count - 1),
        in_specs=[SMEM_SPEC] + [VMEM_SPEC] * 2,
        out_specs=(VMEM_SPEC,) * z_count,
        compiler_params=params(),
        cost_estimate=cost(),
        name="share",
    )(where, kept, swapped)


def pack_back_kernel(placing, relay, direct, mine, *rest):
    parts, (out_ref, strips, total, rows, sem) = rest[:-5], rest[-5:]
    slots = placing.shape[0]
    blocks = mine.shape[1] // 128
    steps = mine.shape[0] // slots
    hop = SPILL * STRIP
    fetch = pltpu.make_async_copy(
        direct.at[:, pl.ds(direct.shape[1] - hop, hop), :], strips, sem
    )
    fetch.start()
    whole = mine[...]
    for part in parts:
        whole = whole + part[...].astype(F32)
    for b in range(blocks):
        total[b] = whole[:, 128 * b : 128 * b + 128]
    rows[...] = jnp.zeros(rows.shape, F32)

    def one(i, carry):
        dest, rank = split(placing[i])
        for s in range(steps):
            for b in range(blocks):
                at = dest * (8 * blocks) + 8 * b + steps * rank + s
                rows[pl.ds(at, 1), :] = total[b, pl.ds(slots * s + i, 1), :]
        return carry

    lax.fori_loop(0, slots, one, 0, unroll=4)
    out_ref[:, hop:, :] = rows[...].reshape(out_ref.shape[0], 8 * blocks, 128).astype(BF16)
    fetch.wait()
    for q in range(out_ref.shape[0]):
        for e in range(SPILL):
            came = relay[q * SPILL + e]
            at = pl.multiple_of((came % SPILL) * STRIP, STRIP)
            out_ref[q, e * STRIP : e * STRIP + STRIP, :] = strips[
                came // SPILL, pl.ds(at, STRIP), :
            ]


def pack_back(placing, relay, direct, mine, parts):
    pool_count = direct.shape[0]
    blocks = mine.shape[1] // 128
    hop = SPILL * STRIP
    return pl.pallas_call(
        pack_back_kernel,
        out_shape=jax.ShapeDtypeStruct((pool_count, hop + 8 * blocks, 128), BF16),
        in_specs=[SMEM_SPEC] * 2 + [ANY_SPEC] + [VMEM_SPEC] * (1 + len(parts)),
        out_specs=VMEM_SPEC,
        scratch_shapes=[
            pltpu.VMEM((pool_count, hop, 128), BF16),
            pltpu.VMEM((blocks, mine.shape[0], 128), F32),
            pltpu.VMEM((pool_count * 8 * blocks, 128), F32),
            pltpu.SemaphoreType.DMA,
        ],
        compiler_params=params(),
        cost_estimate=cost(),
        name="pack_back",
    )(placing, relay, direct, mine, *parts)


def unpack_back_kernel(steps, arrival, packed, out_ref, rows, total):
    slots = out_ref.shape[0] // steps
    blocks = out_ref.shape[1] // 128
    first = packed.shape[1] - 8 * blocks
    rows[...] = packed[:, first:, :].astype(F32).reshape(rows.shape)

    def one(j, carry):
        owner, rank = split(arrival[j])
        for b in range(blocks):
            at = owner * (8 * blocks) + 8 * b + steps * rank
            total[b, pl.ds(steps * j, steps), :] = rows[pl.ds(at, steps), :]
        return carry

    lax.fori_loop(0, slots, one, 0, unroll=4)
    for b in range(blocks):
        out_ref[:, 128 * b : 128 * b + 128] = total[b].astype(BF16)


def unpack_back(arrival, packed, steps, slots, block):
    return pl.pallas_call(
        functools.partial(unpack_back_kernel, steps),
        out_shape=jax.ShapeDtypeStruct((steps * slots, block), BF16),
        in_specs=[SMEM_SPEC, VMEM_SPEC],
        out_specs=VMEM_SPEC,
        scratch_shapes=[
            pltpu.VMEM((packed.shape[0] * 8 * (block // 128), 128), F32),
            pltpu.VMEM((block // 128, steps * slots, 128), F32),
        ],
        compiler_params=params(),
        cost_estimate=cost(),
        name="unpack_back",
    )(arrival, packed)


def assemble_kernel(where, *rest):
    parts, (out_ref, part, whole) = rest[:-3], rest[-3:]
    slots, steps, width = out_ref.shape
    z_count = len(parts) // 2
    block = width // z_count
    core, z = where[0] & 1, where[0] >> 1
    for n, ref in enumerate(parts):
        side = core if n < z_count else 1 - core
        start = (z ^ (n % z_count)) * (block // 128)
        for b in range(block // 128):
            part[...] = ref[:, 128 * b : 128 * b + 128].astype(F32)
            for s in range(steps // 2):
                whole[start + b, pl.ds((steps // 2) * side + s, slots, stride=steps), :] = part[
                    pl.ds(s, slots, stride=steps // 2), :
                ]
    for j in range(slots):
        for b in range(width // 128):
            out_ref[j, :, 128 * b : 128 * b + 128] = whole[
                b, steps * j : steps * j + steps, :
            ].astype(BF16)


def assemble(where, parts, slots, steps, width):
    return pl.pallas_call(
        assemble_kernel,
        out_shape=jax.ShapeDtypeStruct((slots, steps, width), BF16),
        in_specs=[SMEM_SPEC] + [VMEM_SPEC] * len(parts),
        out_specs=VMEM_SPEC,
        scratch_shapes=[
            pltpu.VMEM((parts[0].shape[0], 128), F32),
            pltpu.VMEM((width // 128, slots * steps, 128), F32),
        ],
        compiler_params=params(),
        cost_estimate=cost(),
        name="assemble",
    )(where, *parts)


def exchange(x):
    return lax.all_to_all(x, "pool", split_axis=0, concat_axis=0, tiled=True)


def body(prompt_latent, prompt_lengths, decode_slot, new_latent, queries, w_uk, w_uv, w_out):
    pool_count = lax.axis_size("pool")
    tp_count = lax.axis_size("tp")
    tp_index = lax.axis_index("tp")
    latent_t = prompt_latent.transpose(0, 2, 1)
    steps, slots, heads, width = queries.shape
    span, feature = prompt_latent.shape[1:]
    piece = span // tp_count
    out_width = w_out.shape[1]
    z_count = tp_count // 2
    where = jnp.stack([tp_index, lax.axis_index("pool")]).astype(jnp.int32)
    swap = [(i, i ^ 1) for i in range(tp_count)]
    hops = [[(i, i ^ (2 * d)) for i in range(tp_count)] for d in range(1, z_count)]

    payload, arrival, lengths = pack_queries(
        decode_slot, prompt_lengths, where, queries, new_latent, pool_count
    )
    payload = exchange(payload)
    direct, placing, leaving, coming, relay, rounds = pack_context(
        decode_slot, where, latent_t, piece, pool_count
    )
    payload, direct = lax.optimization_barrier((payload, direct))
    direct = exchange(direct)

    given, kept = attention(
        placing, prompt_lengths, where, payload, latent_t, w_uk, w_uv, w_out, steps
    )

    swapped = lax.ppermute(given, "tp", swap)
    mine, *parts = share(where, kept, swapped, z_count)
    parts = [lax.ppermute(part, "tp", hop) for part, hop in zip(parts, hops)]

    back = exchange(pack_back(placing, relay, direct, mine, parts))
    context = place(arrival, lengths, where, direct, piece, feature)
    back, context = lax.optimization_barrier((back, context))
    own = unpack_back(arrival, back, steps // 2, slots, out_width // z_count)
    parts = [own] + [lax.ppermute(own, "tp", hop) for hop in hops]
    swapped = [lax.ppermute(own, "tp", swap)]
    context = place_strips(coming, lengths, where, back, context)

    def more(state):
        turn, context = state
        spill = pack_spill(turn, leaving, where, latent_t, piece)
        spill = exchange(jnp.broadcast_to(spill[None], (pool_count,) + spill.shape))
        context = place_spill(turn, arrival, coming, lengths, where, spill, context)
        return turn + 1, context

    context = lax.while_loop(
        lambda state: state[0][0] < rounds[0], more, (jnp.zeros((1,), jnp.int32), context)
    )[1]
    context, *parts = lax.optimization_barrier((context, *parts))
    parts = parts + swapped + [lax.ppermute(part, "tp", swap) for part in parts[1:]]
    decoded = assemble(where, parts, slots, steps, out_width)
    return decoded, context


def solution(mesh):
    in_specs = (
        P("pool", None, None),
        P(),
        P(),
        P(None, "pool", None),
        P(None, "pool", "tp", None),
        P("tp", None, None),
        P("tp", None, None),
        P("tp", None),
    )
    out_specs = (P("pool", None, None), P("pool", "tp", None))
    return jax.shard_map(body, mesh=mesh, in_specs=in_specs, out_specs=out_specs, check_vma=False)
```

```python
import functools
import math

import jax
import jax.numpy as jnp
from jax import lax
from jax.experimental import pallas as pl
from jax.experimental.pallas import tpu as pltpu
from jax.sharding import PartitionSpec as P

ROPE = 64
NOPE = 128
CAP = 4
DIRECT = 2
SPILL = 2
STRIP = 16
GROUP = 8
FLOOR = -1e30
BF16 = jnp.bfloat16
F32 = jnp.float32

MIB = 1024 * 1024
SMEM_SPEC = pl.BlockSpec(memory_space=pltpu.SMEM)
VMEM_SPEC = pl.BlockSpec(memory_space=pltpu.VMEM)
ANY_SPEC = pl.BlockSpec(memory_space=pl.ANY)
NT = (((1,), (1,)), ((), ()))


def params(mib=16):
    return pltpu.CompilerParams(vmem_limit_bytes=mib * MIB)


def cost(flops=1000, bytes_accessed=1000):
    return pl.CostEstimate(flops=flops, bytes_accessed=bytes_accessed, transcendentals=0)


def split(cell):
    return cell // CAP, cell % CAP


def pack_queries_kernel(
    decode_slot, prompt_lengths, where, q_hbm, n_hbm,
    out_ref, arrival, lengths,
    q_ref, n_ref, new_rows, tails, sems,
):
    steps, slots, heads, width = q_ref.shape
    rows = steps * heads
    blocks = n_ref.shape[2] // 128
    copy_n = pltpu.make_async_copy(n_hbm, n_ref, sems.at[0])
    copy_q = pltpu.make_async_copy(q_hbm, q_ref, sems.at[1])
    copy_n.start()
    copy_q.start()
    first = where[1] * slots

    def locate(p, carry):
        rank = jnp.int32(0)
        for k in range(slots):
            inner = decode_slot[p * slots + k] - first
            hit = (inner >= 0) & (inner < slots)
            at = jnp.where(hit, inner, slots)
            arrival[at] = p * CAP + rank
            lengths[at] = prompt_lengths[p * slots + k]
            rank = rank + hit.astype(jnp.int32)
        return carry

    lax.fori_loop(0, out_ref.shape[0], locate, 0)
    tails[...] = jnp.zeros(tails.shape, F32)
    copy_n.wait()
    new_rows[...] = n_ref[...].astype(F32)
    copy_q.wait()

    def one(j, carry):
        dest, rank = split(arrival[j])
        x = q_ref[:, j].astype(F32)
        nope = x[:, :, :NOPE].reshape(rows, NOPE)
        rope = x[:, :, NOPE:].reshape(rows, ROPE)
        rope = jnp.concatenate([rope[: rows // 2], rope[rows // 2 :]], axis=1)
        fresh = jnp.concatenate([new_rows[s, pl.ds(j, 1), :] for s in range(steps)], axis=0)
        body = [fresh[:, 128 * b : 128 * b + 128] for b in range(blocks)]
        last = fresh[:, 128 * blocks :]
        cell = jnp.concatenate([nope, rope] + body, axis=0)
        out_ref[dest, pl.ds(pl.multiple_of(rank * 64, 64), 64), :] = cell.astype(BF16)
        tails[pl.ds(dest * 8 + rank * 2, 2), :] = jnp.concatenate(
            [last[: steps // 2], last[steps // 2 :]], axis=1
        )
        return carry

    lax.fori_loop(0, slots, one, 0, unroll=4)
    out_ref[:, 256:264, :] = tails[...].reshape(out_ref.shape[0], 8, 128).astype(BF16)


def pack_queries(decode_slot, prompt_lengths, where, queries, new_latent, pool_count):
    slots = queries.shape[1]
    return pl.pallas_call(
        pack_queries_kernel,
        out_shape=(
            jax.ShapeDtypeStruct((pool_count, 264, 128), BF16),
            jax.ShapeDtypeStruct((slots + 8,), jnp.int32),
            jax.ShapeDtypeStruct((slots + 8,), jnp.int32),
        ),
        in_specs=[SMEM_SPEC] * 3 + [ANY_SPEC] * 2,
        out_specs=(VMEM_SPEC, SMEM_SPEC, SMEM_SPEC),
        scratch_shapes=[
            pltpu.VMEM(queries.shape, BF16),
            pltpu.VMEM(new_latent.shape, BF16),
            pltpu.VMEM(new_latent.shape, F32),
            pltpu.VMEM((pool_count * 8, 128), F32),
            pltpu.SemaphoreType.DMA((2,)),
        ],
        compiler_params=params(60),
        cost_estimate=cost(),
        name="pack_queries",
    )(decode_slot, prompt_lengths, where, queries, new_latent)


def padded_rows(piece, feature):
    return -(-(piece * feature // 128) // STRIP) * STRIP


def window_start(row, piece, window, span):
    return pl.multiple_of(jnp.where(row + piece > window, span - window, 0), 128)


def picker(row, start, piece, window):
    pick = lax.broadcasted_iota(jnp.int32, (piece, window), 1) - (
        row - start + lax.broadcasted_iota(jnp.int32, (piece, window), 0)
    )
    return jnp.where(pick == 0, 1.0, 0.0).astype(BF16)


def packed_piece(pick, latents):
    piece = pick.shape[0]
    blocks = latents.shape[0] // 128
    turned = lax.dot_general(pick, latents, NT, preferred_element_type=F32)
    last = turned[:, 128 * blocks :]
    last = jnp.concatenate([last[: piece // 2], last[piece // 2 :]], axis=1)
    return jnp.concatenate(
        [turned[:, 128 * b : 128 * b + 128] for b in range(blocks)] + [last], axis=0
    ).astype(BF16)


def pack_context_kernel(
    decode_slot, where, p_ref,
    out_ref, placing, later, coming, relay, rounds,
    leaving, counts, ahead, code, source, buf, sems,
):
    slots, feature, window = buf.shape
    owners = out_ref.shape[0]
    padded = (out_ref.shape[1] - SPILL * STRIP) // DIRECT
    piece = padded * 128 // feature // 16 * 16
    rows = piece * feature // 128
    strips = padded // STRIP
    chunk = slots // sems.shape[0]
    row = where[0] * piece
    start = window_start(row, piece, window, p_ref.shape[2])
    copies = [
        pltpu.make_async_copy(
            p_ref.at[pl.ds(k * chunk, chunk), :, pl.ds(start, window)],
            buf.at[pl.ds(k * chunk, chunk)],
            sems.at[k],
        )
        for k in range(sems.shape[0])
    ]
    for copy in copies:
        copy.start()
    bits = slots.bit_length() - 1

    for p in range(owners):
        counts[p] = 0
    spilled = jnp.int32(0)
    for g in range(slots):
        owner = decode_slot[where[1] * slots + g] >> bits
        rank = counts[owner]
        counts[owner] = rank + 1
        placing[g] = owner * CAP + rank
        over = rank >= DIRECT
        leaving[g] = jnp.where(over, spilled, -1)
        spilled = spilled + over.astype(jnp.int32)
    pick = picker(row, start, piece, window)

    def clear(n, carry):
        counts[n] = 0
        return carry

    lax.fori_loop(0, owners * owners, clear, 0, unroll=16)
    first = where[1] * slots

    def look(k, spilled):
        after = []
        for p in range(owners):
            slot = decode_slot[p * slots + k]
            owner = slot >> bits
            rank = counts[p * owners + owner]
            counts[p * owners + owner] = rank + 1
            over = rank >= DIRECT
            ahead[p * (SPILL + 1) + jnp.where(over, jnp.minimum(spilled[p], SPILL), SPILL)] = owner
            inner = slot - first
            at = jnp.where((inner >= 0) & (inner < slots), inner, slots)
            coming[at] = jnp.where(over, spilled[p], -1)
            source[at] = p
            after.append(spilled[p] + over.astype(jnp.int32))
        return tuple(after)

    spilled = lax.fori_loop(0, slots, look, (jnp.int32(0),) * owners)
    for q in range(owners):
        counts[q] = 0
    for n in range(owners * SPILL):
        relay[n] = 0
    longest = jnp.int32(0)
    for p in range(owners):
        hopped = jnp.int32(0)
        for n in range(SPILL):
            owner = jnp.where(n < spilled[p], ahead[p * (SPILL + 1) + n], 0)
            entry = counts[owner]
            hops = (n < spilled[p]) & (entry < SPILL)
            counts[owner] = entry + hops.astype(jnp.int32)
            relay[jnp.where(hops, owner * SPILL + entry, owners * SPILL)] = p * SPILL + n
            code[p * (SPILL + 1) + n] = jnp.where(hops, entry, SPILL + n - hopped)
            hopped = hopped + hops.astype(jnp.int32)
        code[p * (SPILL + 1) + SPILL] = SPILL - hopped
        longest = jnp.maximum(longest, spilled[p] - hopped)
    rounds[0] = (longest + SPILL - 1) // SPILL

    def coded(p, n):
        found = code[p * (SPILL + 1) + jnp.clip(n, 0, SPILL)]
        return jnp.where(n < 0, -1, jnp.where(n < SPILL, found, found + n))

    def finish(n, carry):
        coming[n] = coded(source[n], coming[n])
        later[n] = coded(where[1], leaving[n])
        return carry

    lax.fori_loop(0, slots, finish, 0, unroll=4)

    for k, copy in enumerate(copies):
        copy.wait()

        def one(n, carry):
            g = k * chunk + n
            dest, rank = split(placing[g])
            cell = packed_piece(pick, buf[g])

            @pl.when(rank < DIRECT)
            def _():
                out_ref[dest, pl.ds(pl.multiple_of(rank * padded, STRIP), rows), :] = cell

            @pl.when((rank >= DIRECT) & (leaving[g] < SPILL))
            def _():
                at = DIRECT * padded + leaving[g] * STRIP
                for m in range(strips):
                    high = min(STRIP, rows - m * STRIP)
                    out_ref[m, pl.ds(pl.multiple_of(at, STRIP), high), :] = cell[
                        m * STRIP : m * STRIP + high
                    ]

            return carry

        lax.fori_loop(0, chunk, one, 0, unroll=4)


def pack_context(decode_slot, where, prompt_latent, piece, pool_count):
    slots, feature, _ = prompt_latent.shape
    rows = padded_rows(piece, feature)
    return pl.pallas_call(
        pack_context_kernel,
        out_shape=(
            jax.ShapeDtypeStruct((pool_count, DIRECT * rows + SPILL * STRIP, 128), BF16),
            jax.ShapeDtypeStruct((slots,), jnp.int32),
            jax.ShapeDtypeStruct((slots,), jnp.int32),
            jax.ShapeDtypeStruct((slots + 8,), jnp.int32),
            jax.ShapeDtypeStruct((pool_count * SPILL + 8,), jnp.int32),
            jax.ShapeDtypeStruct((1,), jnp.int32),
        ),
        in_specs=[SMEM_SPEC, SMEM_SPEC, ANY_SPEC],
        out_specs=(VMEM_SPEC,) + (SMEM_SPEC,) * 5,
        scratch_shapes=[
            pltpu.SMEM((slots,), jnp.int32),
            pltpu.SMEM((pool_count * pool_count,), jnp.int32),
            pltpu.SMEM((pool_count * (SPILL + 1),), jnp.int32),
            pltpu.SMEM((pool_count * (SPILL + 1),), jnp.int32),
            pltpu.SMEM((slots + 8,), jnp.int32),
            pltpu.VMEM((slots, feature, 256), BF16),
            pltpu.SemaphoreType.DMA((4,)),
        ],
        compiler_params=params(63),
        cost_estimate=cost(),
        name="pack_context",
    )(decode_slot, where, prompt_latent)


def pack_spill_kernel(turn, leaving, where, p_ref, spill_ref, buf, sem):
    feature, window = buf.shape
    piece = spill_ref.shape[1] * 128 // feature // 16 * 16
    row = where[0] * piece
    start = window_start(row, piece, window, p_ref.shape[2])
    pick = picker(row, start, piece, window)

    def one(g, carry):
        at = leaving[g] - SPILL - turn[0] * SPILL

        @pl.when((at >= 0) & (at < SPILL))
        def _():
            copy = pltpu.make_async_copy(p_ref.at[g, :, pl.ds(start, window)], buf, sem)
            copy.start()
            copy.wait()
            cell = packed_piece(pick, buf[...])
            spill_ref[at, : cell.shape[0], :] = cell

        return carry

    lax.fori_loop(0, p_ref.shape[0], one, 0)


def pack_spill(turn, leaving, where, prompt_latent, piece):
    slots, feature, _ = prompt_latent.shape
    return pl.pallas_call(
        pack_spill_kernel,
        out_shape=jax.ShapeDtypeStruct((SPILL, padded_rows(piece, feature), 128), BF16),
        in_specs=[SMEM_SPEC] * 3 + [ANY_SPEC],
        out_specs=VMEM_SPEC,
        scratch_shapes=[pltpu.VMEM((feature, 256), BF16), pltpu.SemaphoreType.DMA],
        compiler_params=params(),
        cost_estimate=cost(),
        name="pack_spill",
    )(turn, leaving, where, prompt_latent)


def unpack_piece(out_ref, row, packed, at, start, first_row, length):
    piece, feature = out_ref.shape[1:]
    blocks = feature // 128
    for b in range(blocks):
        out_ref[row, :, 128 * b : 128 * b + 128] = packed[at, pl.ds(start + b * piece, piece), :]
    last = packed[at, pl.ds(start + blocks * piece, piece // 2), :].astype(F32)
    last = jnp.concatenate([last[:, :64], last[:, 64:]], axis=0)
    out_ref[row, :, 128 * blocks :] = last.astype(BF16)

    @pl.when(length < first_row + piece)
    def _():
        whole = out_ref[row].astype(F32)
        position = first_row + lax.broadcasted_iota(jnp.int32, whole.shape, 0)
        out_ref[row] = jnp.where(position < length, whole, 0.0).astype(BF16)


def place_kernel(arrival, lengths, where, direct, out_ref, outbox, sems):
    slots, piece, feature = out_ref.shape
    padded = (direct.shape[1] - SPILL * STRIP) // DIRECT
    chunk = slots // sems.shape[0]

    def copy_out(k):
        part = pl.ds(k * chunk, chunk)
        return pltpu.make_async_copy(outbox.at[part], out_ref.at[part], sems.at[k])

    def one(j, carry):
        owner, rank = split(arrival[j])
        at = pl.multiple_of(jnp.minimum(rank, DIRECT - 1) * padded, STRIP)
        unpack_piece(outbox, j, direct, owner, at, where[0] * piece, lengths[j])
        return carry

    for k in range(sems.shape[0]):
        lax.fori_loop(k * chunk, k * chunk + chunk, one, 0, unroll=2)
        copy_out(k).start()
    for k in range(sems.shape[0]):
        copy_out(k).wait()


def place(arrival, lengths, where, direct, piece, feature):
    slots = arrival.shape[0] - 8
    return pl.pallas_call(
        place_kernel,
        out_shape=jax.ShapeDtypeStruct((slots, piece, feature), BF16),
        in_specs=[SMEM_SPEC] * 3 + [VMEM_SPEC],
        out_specs=ANY_SPEC,
        scratch_shapes=[
            pltpu.VMEM((slots, piece, feature), BF16),
            pltpu.SemaphoreType.DMA((4,)),
        ],
        compiler_params=params(),
        cost_estimate=cost(bytes_accessed=12_000_000),
        name="place_context",
    )(arrival, lengths, where, direct)


def place_strips_kernel(
    coming, lengths, where, back, context, out_ref, inbox, whole, outbox, in_sems, out_sems
):
    slots, piece, feature = out_ref.shape
    strips = inbox.shape[1]

    def copy_in(e):
        source = back.at[pl.ds(0, strips), pl.ds(e * STRIP, STRIP), :]
        return pltpu.make_async_copy(source, inbox.at[e], in_sems.at[e])

    def copy_out(j, e):
        return pltpu.make_async_copy(outbox.at[e], out_ref.at[j], out_sems.at[e])

    for e in range(SPILL):
        copy_in(e).start()
    for e in range(SPILL):
        copy_in(e).wait()
        for m in range(strips):
            whole[e, m * STRIP : m * STRIP + STRIP, :] = inbox[e, m]

    def each(action):
        def step(j, carry):
            for e in range(SPILL):

                @pl.when(coming[j] == e)
                def _():
                    action(j, e)

            return carry

        lax.fori_loop(0, slots, step, 0)

    def work(j, e):
        unpack_piece(outbox, e, whole, e, 0, where[0] * piece, lengths[j])
        copy_out(j, e).start()

    each(work)
    each(lambda j, e: copy_out(j, e).wait())


def place_strips(coming, lengths, where, back, context):
    slots, piece, feature = context.shape
    strips = padded_rows(piece, feature) // STRIP
    return pl.pallas_call(
        place_strips_kernel,
        out_shape=jax.ShapeDtypeStruct(context.shape, BF16),
        in_specs=[SMEM_SPEC] * 3 + [ANY_SPEC] * 2,
        out_specs=ANY_SPEC,
        scratch_shapes=[
            pltpu.VMEM((SPILL, strips, STRIP, 128), BF16),
            pltpu.VMEM((SPILL, strips * STRIP, 128), BF16),
            pltpu.VMEM((SPILL, piece, feature), BF16),
            pltpu.SemaphoreType.DMA((SPILL,)),
            pltpu.SemaphoreType.DMA((SPILL,)),
        ],
        input_output_aliases={4: 0},
        compiler_params=params(),
        cost_estimate=cost(bytes_accessed=6_000_000),
        name="place_strips",
    )(coming, lengths, where, back, context)


def place_spill_kernel(
    turn, arrival, coming, lengths, where, spill, context, out_ref, inbox, outbox, sem
):
    slots, piece, feature = out_ref.shape

    def one(j, carry):
        at = coming[j] - SPILL - turn[0] * SPILL

        @pl.when((at >= 0) & (at < SPILL))
        def _():
            owner = split(arrival[j])[0]
            copy = pltpu.make_async_copy(
                spill.at[owner, jnp.clip(at, 0, SPILL - 1)], inbox.at[0], sem
            )
            copy.start()
            copy.wait()
            unpack_piece(outbox, 0, inbox, 0, 0, where[0] * piece, lengths[j])
            copy = pltpu.make_async_copy(outbox.at[0], out_ref.at[j], sem)
            copy.start()
            copy.wait()

        return carry

    lax.fori_loop(0, slots, one, 0)


def place_spill(turn, arrival, coming, lengths, where, spill, context):
    return pl.pallas_call(
        place_spill_kernel,
        out_shape=jax.ShapeDtypeStruct(context.shape, BF16),
        in_specs=[SMEM_SPEC] * 5 + [ANY_SPEC] * 2,
        out_specs=ANY_SPEC,
        scratch_shapes=[
            pltpu.VMEM((1,) + spill.shape[-2:], BF16),
            pltpu.VMEM((1,) + context.shape[1:], BF16),
            pltpu.SemaphoreType.DMA,
        ],
        input_output_aliases={6: 0},
        compiler_params=params(),
        cost_estimate=cost(),
        name="place_spill",
    )(turn, arrival, coming, lengths, where, spill, context)


def attention_kernel(
    placing, lengths, where, payload_hbm, p_hbm, w_uk_hbm, w_uv_hbm, w_out_hbm,
    given_ref, kept_ref,
    payload, prompt, w_uk, w_uv, w_out,
    q_nope, q_rope, acc, fresh, tails, fresh_score, total, head_out, sems,
):
    steps = 4
    heads, latent, nope = w_uk.shape
    slots, feature, span = prompt.shape
    chunks = latent // 128
    per_step = slots * heads
    many = slots * steps
    scale = 1.0 / math.sqrt(nope + ROPE)
    first = where[1] * slots
    copy_payload = pltpu.make_async_copy(payload_hbm, payload, sems.at[0])
    copy_uk = pltpu.make_async_copy(w_uk_hbm, w_uk, sems.at[1])
    copy_uv = pltpu.make_async_copy(w_uv_hbm, w_uv, sems.at[2])
    copy_out = pltpu.make_async_copy(w_out_hbm, w_out, sems.at[3])

    def copy_prompt(k):
        part = pl.ds(k * GROUP, GROUP)
        return pltpu.make_async_copy(p_hbm.at[part], prompt.at[part], sems.at[4 + k])

    copy_payload.start()
    copy_uk.start()
    for k in range(slots // GROUP):
        copy_prompt(k).start()
    copy_uv.start()
    copy_out.start()

    def spread(ref, i, lead=()):
        return jnp.concatenate(
            [
                ref[(*lead, pl.ds(pl.multiple_of(per_step * s + heads * i, 8), heads), slice(None))]
                for s in range(steps)
            ],
            axis=0,
        )

    def collect(ref, i, value, lead=()):
        for s in range(steps):
            ref[(*lead, pl.ds(pl.multiple_of(per_step * s + heads * i, 8), heads), slice(None))] = (
                value[heads * s : heads * s + heads]
            )

    copy_payload.wait()
    tails[...] = payload[:, 256:264, :].astype(F32).reshape(tails.shape)

    def unpack(i, carry):
        dest, rank = split(placing[i])
        cell = payload[dest, pl.ds(pl.multiple_of(rank * 64, 64), 64), :].astype(F32)
        collect(q_nope, i, cell[:32])
        rope = jnp.concatenate([cell[32:48, :64], cell[32:48, 64:]], axis=0)
        collect(q_rope, i, jnp.concatenate([rope, jnp.zeros_like(rope)], axis=1))
        for b in range(chunks):
            fresh[b, pl.ds(steps * i, steps), :] = cell[48 + 4 * b : 52 + 4 * b]
        last = tails[pl.ds(dest * 8 + rank * 2, 2), :]
        last = jnp.concatenate([last[:, :64], last[:, 64:]], axis=0)
        fresh[chunks, pl.ds(steps * i, steps), :] = jnp.concatenate(
            [last, jnp.zeros_like(last)], axis=1
        )
        return carry

    lax.fori_loop(0, slots, unpack, 0, unroll=8)
    copy_uk.wait()
    for h in range(heads):
        rows = pl.ds(h, many, stride=heads)
        a = lax.dot_general(
            q_nope[rows, :].astype(BF16), w_uk[h], NT, preferred_element_type=F32
        )
        a = a.astype(BF16).astype(F32)
        for c in range(chunks):
            acc[c, rows, :] = a[:, 128 * c : 128 * c + 128]
    keys = jnp.concatenate([fresh[b] for b in range(chunks + 1)], axis=1).astype(BF16)

    def score(k, carry):
        rows = pl.ds(pl.multiple_of(k * 128, 128), 128)
        q = jnp.concatenate(
            [acc[c, rows, :] for c in range(chunks)] + [q_rope[rows, :]], axis=1
        ).astype(BF16)
        fresh_score[rows, :] = scale * lax.dot_general(q, keys, NT, preferred_element_type=F32)
        return carry

    lax.fori_loop(0, per_step * steps // 128, score, 0, unroll=2)

    def one(i):
        q = jnp.concatenate(
            [spread(acc, i, (c,)) for c in range(chunks)] + [spread(q_rope, i)[:, :ROPE]], axis=1
        ).astype(BF16)
        s_prompt = scale * jnp.dot(q, prompt[i], preferred_element_type=F32)
        s_fresh = spread(fresh_score, i)
        column = lax.broadcasted_iota(jnp.int32, s_prompt.shape, 1)
        s_prompt = jnp.where(column < lengths[first + i], s_prompt, FLOOR)
        step_of = lax.broadcasted_iota(jnp.int32, s_fresh.shape, 0) // heads
        column = lax.broadcasted_iota(jnp.int32, s_fresh.shape, 1) - steps * i
        s_fresh = jnp.where((column >= 0) & (column <= step_of), s_fresh, FLOOR)
        peak = jnp.maximum(
            jnp.max(s_prompt, axis=1, keepdims=True), jnp.max(s_fresh, axis=1, keepdims=True)
        )
        w_prompt = jnp.exp(s_prompt - peak)
        w_fresh = jnp.exp(s_fresh - peak)
        sums = jnp.sum(w_prompt, axis=1, keepdims=True) + jnp.sum(w_fresh, axis=1, keepdims=True)
        mixed = lax.dot_general(
            w_prompt.astype(BF16), prompt[i, :latent], NT, preferred_element_type=F32
        )
        for c in range(chunks):
            collect(acc, i, mixed[:, 128 * c : 128 * c + 128], (c,))
        collect(fresh_score, i, w_fresh)
        collect(total, i, jnp.broadcast_to(sums, s_fresh.shape))

    def attend(k, carry):
        copy_prompt(k).wait()
        for n in range(GROUP):
            one(k * GROUP + n)
        return carry

    lax.fori_loop(0, slots // GROUP, attend, 0)

    values = jnp.concatenate([fresh[b] for b in range(chunks)], axis=1).astype(BF16)
    copy_uv.wait()
    for h in range(heads):
        rows = pl.ds(h, many, stride=heads)
        mixed = jnp.dot(fresh_score[rows, :].astype(BF16), values, preferred_element_type=F32)
        mixed = mixed + jnp.concatenate([acc[c, rows, :] for c in range(chunks)], axis=1)
        part = 1.0 / total[rows, :]
        mixed = (mixed * jnp.concatenate([part] * chunks, axis=1)).astype(BF16)
        head_out[:, h * 128 : h * 128 + 128] = jnp.dot(
            mixed, w_uv[h], preferred_element_type=F32
        ).astype(BF16)
    copy_out.wait()
    half = many // 2
    core = where[0] % 2
    mine = head_out[pl.ds(pl.multiple_of(core * half, half), half), :]
    theirs = head_out[pl.ds(pl.multiple_of((1 - core) * half, half), half), :]
    both = jnp.concatenate([theirs, mine], axis=0)
    for b in range(w_out.shape[1] // 512):
        at_b = slice(b * 512, b * 512 + 512)
        summed = jnp.dot(both, w_out[:, at_b], preferred_element_type=F32)
        given_ref[:, at_b] = summed[:half].astype(BF16)
        kept_ref[:, at_b] = summed[half:].astype(BF16)


def attention(placing, lengths, where, payload, prompt_latent, w_uk, w_uv, w_out, steps):
    slots, feature, span = prompt_latent.shape
    heads, latent, nope = w_uk.shape
    width = w_out.shape[1]
    rows = steps * slots * heads
    half = steps * slots // 2
    chunks = latent // 128
    return pl.pallas_call(
        attention_kernel,
        out_shape=(
            jax.ShapeDtypeStruct((half, width), BF16),
            jax.ShapeDtypeStruct((half, width), BF16),
        ),
        in_specs=[SMEM_SPEC] * 3 + [ANY_SPEC] * 5,
        out_specs=(VMEM_SPEC, VMEM_SPEC),
        scratch_shapes=[
            pltpu.VMEM(payload.shape, BF16),
            pltpu.VMEM(prompt_latent.shape, BF16),
            pltpu.VMEM(w_uk.shape, BF16),
            pltpu.VMEM(w_uv.shape, BF16),
            pltpu.VMEM(w_out.shape, BF16),
            pltpu.VMEM((rows, 128), F32),
            pltpu.VMEM((rows, 128), F32),
            pltpu.VMEM((chunks, rows, 128), F32),
            pltpu.VMEM((chunks + 1, steps * slots, 128), F32),
            pltpu.VMEM((payload.shape[0] * 8, 128), F32),
            pltpu.VMEM((rows, 128), F32),
            pltpu.VMEM((rows, 128), F32),
            pltpu.VMEM((steps * slots, heads * 128), BF16),
            pltpu.SemaphoreType.DMA((4 + slots // GROUP,)),
        ],
        compiler_params=params(60),
        cost_estimate=cost(),
        name="attention",
    )(placing, lengths, where, payload, prompt_latent, w_uk, w_uv, w_out)


def share_kernel(where, kept, swapped, mine, *parts):
    block = mine.shape[1]
    z = where[0] >> 1
    for d, part in enumerate((mine,) + parts):
        at = pl.ds(pl.multiple_of((z ^ d) * block, 128), block)
        part[...] = (kept[:, at].astype(F32) + swapped[:, at].astype(F32)).astype(part.dtype)


def share(where, kept, swapped, z_count):
    rows, width = kept.shape
    block = width // z_count
    return pl.pallas_call(
        share_kernel,
        out_shape=(jax.ShapeDtypeStruct((rows, block), F32),)
        + (jax.ShapeDtypeStruct((rows, block), BF16),) * (z_count - 1),
        in_specs=[SMEM_SPEC] + [VMEM_SPEC] * 2,
        out_specs=(VMEM_SPEC,) * z_count,
        compiler_params=params(),
        cost_estimate=cost(),
        name="share",
    )(where, kept, swapped)


def pack_back_kernel(placing, relay, direct, mine, *rest):
    parts, (out_ref, strips, total, rows, sem) = rest[:-5], rest[-5:]
    slots = placing.shape[0]
    blocks = mine.shape[1] // 128
    steps = mine.shape[0] // slots
    hop = SPILL * STRIP
    fetch = pltpu.make_async_copy(
        direct.at[:, pl.ds(direct.shape[1] - hop, hop), :], strips, sem
    )
    fetch.start()
    whole = mine[...]
    for part in parts:
        whole = whole + part[...].astype(F32)
    for b in range(blocks):
        total[b] = whole[:, 128 * b : 128 * b + 128]
    def one(i, carry):
        dest, rank = split(placing[i])
        for s in range(steps):
            for b in range(blocks):
                at = dest * (8 * blocks) + 8 * b + steps * rank + s
                rows[pl.ds(at, 1), :] = total[b, pl.ds(slots * s + i, 1), :]
        return carry

    lax.fori_loop(0, slots, one, 0, unroll=4)
    out_ref[:, hop:, :] = rows[...].reshape(out_ref.shape[0], 8 * blocks, 128).astype(BF16)
    fetch.wait()
    for q in range(out_ref.shape[0]):
        for e in range(SPILL):
            came = relay[q * SPILL + e]
            at = pl.multiple_of((came % SPILL) * STRIP, STRIP)
            out_ref[q, e * STRIP : e * STRIP + STRIP, :] = strips[
                came // SPILL, pl.ds(at, STRIP), :
            ]


def pack_back(placing, relay, direct, mine, parts):
    pool_count = direct.shape[0]
    blocks = mine.shape[1] // 128
    hop = SPILL * STRIP
    return pl.pallas_call(
        pack_back_kernel,
        out_shape=jax.ShapeDtypeStruct((pool_count, hop + 8 * blocks, 128), BF16),
        in_specs=[SMEM_SPEC] * 2 + [ANY_SPEC] + [VMEM_SPEC] * (1 + len(parts)),
        out_specs=VMEM_SPEC,
        scratch_shapes=[
            pltpu.VMEM((pool_count, hop, 128), BF16),
            pltpu.VMEM((blocks, mine.shape[0], 128), F32),
            pltpu.VMEM((pool_count * 8 * blocks, 128), F32),
            pltpu.SemaphoreType.DMA,
        ],
        compiler_params=params(),
        cost_estimate=cost(),
        name="pack_back",
    )(placing, relay, direct, mine, *parts)


def unpack_back_kernel(steps, arrival, packed, out_ref, rows, total):
    slots = out_ref.shape[0] // steps
    blocks = out_ref.shape[1] // 128
    first = packed.shape[1] - 8 * blocks
    rows[...] = packed[:, first:, :].astype(F32).reshape(rows.shape)

    def one(j, carry):
        owner, rank = split(arrival[j])
        for b in range(blocks):
            at = owner * (8 * blocks) + 8 * b + steps * rank
            total[b, pl.ds(steps * j, steps), :] = rows[pl.ds(at, steps), :]
        return carry

    lax.fori_loop(0, slots, one, 0, unroll=4)
    for b in range(blocks):
        out_ref[:, 128 * b : 128 * b + 128] = total[b].astype(BF16)


def unpack_back(arrival, packed, steps, slots, block):
    return pl.pallas_call(
        functools.partial(unpack_back_kernel, steps),
        out_shape=jax.ShapeDtypeStruct((steps * slots, block), BF16),
        in_specs=[SMEM_SPEC, VMEM_SPEC],
        out_specs=VMEM_SPEC,
        scratch_shapes=[
            pltpu.VMEM((packed.shape[0] * 8 * (block // 128), 128), F32),
            pltpu.VMEM((block // 128, steps * slots, 128), F32),
        ],
        compiler_params=params(),
        cost_estimate=cost(),
        name="unpack_back",
    )(arrival, packed)


def assemble_kernel(where, *rest):
    parts, (out_ref, part, whole) = rest[:-3], rest[-3:]
    slots, steps, width = out_ref.shape
    z_count = len(parts) // 2
    block = width // z_count
    core, z = where[0] & 1, where[0] >> 1
    for n, ref in enumerate(parts):
        side = core if n < z_count else 1 - core
        start = (z ^ (n % z_count)) * (block // 128)
        for b in range(block // 128):
            part[...] = ref[:, 128 * b : 128 * b + 128].astype(F32)
            for s in range(steps // 2):
                whole[start + b, pl.ds((steps // 2) * side + s, slots, stride=steps), :] = part[
                    pl.ds(s, slots, stride=steps // 2), :
                ]
    for b in range(width // 128):
        out_ref[:, :, 128 * b : 128 * b + 128] = (
            whole[b].reshape(slots, steps, 128).astype(BF16)
        )


def assemble(where, parts, slots, steps, width):
    return pl.pallas_call(
        assemble_kernel,
        out_shape=jax.ShapeDtypeStruct((slots, steps, width), BF16),
        in_specs=[SMEM_SPEC] + [VMEM_SPEC] * len(parts),
        out_specs=VMEM_SPEC,
        scratch_shapes=[
            pltpu.VMEM((parts[0].shape[0], 128), F32),
            pltpu.VMEM((width // 128, slots * steps, 128), F32),
        ],
        compiler_params=params(),
        cost_estimate=cost(),
        name="assemble",
    )(where, *parts)


def exchange(x):
    return lax.all_to_all(x, "pool", split_axis=0, concat_axis=0, tiled=True)


def body(prompt_latent, prompt_lengths, decode_slot, new_latent, queries, w_uk, w_uv, w_out):
    pool_count = lax.axis_size("pool")
    tp_count = lax.axis_size("tp")
    tp_index = lax.axis_index("tp")
    latent_t = prompt_latent.transpose(0, 2, 1)
    steps, slots, heads, width = queries.shape
    span, feature = prompt_latent.shape[1:]
    piece = span // tp_count
    out_width = w_out.shape[1]
    z_count = tp_count // 2
    where = jnp.stack([tp_index, lax.axis_index("pool")]).astype(jnp.int32)
    swap = [(i, i ^ 1) for i in range(tp_count)]
    hops = [[(i, i ^ (2 * d)) for i in range(tp_count)] for d in range(1, z_count)]

    payload, arrival, lengths = pack_queries(
        decode_slot, prompt_lengths, where, queries, new_latent, pool_count
    )
    payload = exchange(payload)
    direct, placing, leaving, coming, relay, rounds = pack_context(
        decode_slot, where, latent_t, piece, pool_count
    )
    payload, direct = lax.optimization_barrier((payload, direct))
    direct = exchange(direct)

    given, kept = attention(
        placing, prompt_lengths, where, payload, latent_t, w_uk, w_uv, w_out, steps
    )

    swapped = lax.ppermute(given, "tp", swap)
    mine, *parts = share(where, kept, swapped, z_count)
    parts = [lax.ppermute(part, "tp", hop) for part, hop in zip(parts, hops)]

    back = exchange(pack_back(placing, relay, direct, mine, parts))
    context = place(arrival, lengths, where, direct, piece, feature)
    back, context = lax.optimization_barrier((back, context))
    own = unpack_back(arrival, back, steps // 2, slots, out_width // z_count)
    parts = [own] + [lax.ppermute(own, "tp", hop) for hop in hops]
    swapped = [lax.ppermute(own, "tp", swap)]
    context = place_strips(coming, lengths, where, back, context)

    def more(state):
        turn, context = state
        spill = pack_spill(turn, leaving, where, latent_t, piece)
        spill = exchange(jnp.broadcast_to(spill[None], (pool_count,) + spill.shape))
        context = place_spill(turn, arrival, coming, lengths, where, spill, context)
        return turn + 1, context

    context = lax.while_loop(
        lambda state: state[0][0] < rounds[0], more, (jnp.zeros((1,), jnp.int32), context)
    )[1]
    context, *parts = lax.optimization_barrier((context, *parts))
    parts = parts + swapped + [lax.ppermute(part, "tp", swap) for part in parts[1:]]
    decoded = assemble(where, parts, slots, steps, out_width)
    return decoded, context


def solution(mesh):
    in_specs = (
        P("pool", None, None),
        P(),
        P(),
        P(None, "pool", None),
        P(None, "pool", "tp", None),
        P("tp", None, None),
        P("tp", None, None),
        P("tp", None),
    )
    out_specs = (P("pool", None, None), P("pool", "tp", None))
    return jax.shard_map(body, mesh=mesh, in_specs=in_specs, out_specs=out_specs, check_vma=False)
```

```python
import functools
import math

import jax
import jax.numpy as jnp
from jax import lax
from jax.experimental import pallas as pl
from jax.experimental.pallas import tpu as pltpu
from jax.sharding import PartitionSpec as P

ROPE = 64
NOPE = 128
CAP = 4
DIRECT = 2
SPILL = 2
STRIP = 16
GROUP = 16
FLOOR = -1e30
BF16 = jnp.bfloat16
F32 = jnp.float32

MIB = 1024 * 1024
SMEM_SPEC = pl.BlockSpec(memory_space=pltpu.SMEM)
VMEM_SPEC = pl.BlockSpec(memory_space=pltpu.VMEM)
ANY_SPEC = pl.BlockSpec(memory_space=pl.ANY)
NT = (((1,), (1,)), ((), ()))


def params(mib=16):
    return pltpu.CompilerParams(vmem_limit_bytes=mib * MIB)


def cost(flops=1000, bytes_accessed=1000):
    return pl.CostEstimate(flops=flops, bytes_accessed=bytes_accessed, transcendentals=0)


def split(cell):
    return cell // CAP, cell % CAP


def pack_queries_kernel(
    decode_slot, where, q_hbm, n_hbm,
    out_ref, arrival,
    q_ref, n_ref, new_rows, tails, sems,
):
    steps, slots, heads, width = q_ref.shape
    rows = steps * heads
    blocks = n_ref.shape[2] // 128
    copy_n = pltpu.make_async_copy(n_hbm, n_ref, sems.at[0])
    copy_q = pltpu.make_async_copy(q_hbm, q_ref, sems.at[1])
    copy_n.start()
    copy_q.start()
    first = where[1] * slots

    def locate(p, carry):
        rank = jnp.int32(0)
        for k in range(slots):
            inner = decode_slot[p * slots + k] - first
            hit = (inner >= 0) & (inner < slots)
            at = jnp.where(hit, inner, slots)
            arrival[at] = p * CAP + rank
            rank = rank + hit.astype(jnp.int32)
        return carry

    lax.fori_loop(0, out_ref.shape[0], locate, 0)
    tails[...] = jnp.zeros(tails.shape, F32)
    copy_n.wait()
    new_rows[...] = n_ref[...].astype(F32)
    copy_q.wait()

    def one(j, carry):
        dest, rank = split(arrival[j])
        x = q_ref[:, j].astype(F32)
        nope = x[:, :, :NOPE].reshape(rows, NOPE)
        rope = x[:, :, NOPE:].reshape(rows, ROPE)
        rope = jnp.concatenate([rope[: rows // 2], rope[rows // 2 :]], axis=1)
        fresh = jnp.concatenate([new_rows[s, pl.ds(j, 1), :] for s in range(steps)], axis=0)
        body = [fresh[:, 128 * b : 128 * b + 128] for b in range(blocks)]
        last = fresh[:, 128 * blocks :]
        cell = jnp.concatenate([nope, rope] + body, axis=0)
        out_ref[dest, pl.ds(pl.multiple_of(rank * 64, 64), 64), :] = cell.astype(BF16)
        tails[pl.ds(dest * 8 + rank * 2, 2), :] = jnp.concatenate(
            [last[: steps // 2], last[steps // 2 :]], axis=1
        )
        return carry

    lax.fori_loop(0, slots, one, 0, unroll=4)
    out_ref[:, 256:264, :] = tails[...].reshape(out_ref.shape[0], 8, 128).astype(BF16)


def pack_queries(decode_slot, where, queries, new_latent, pool_count):
    slots = queries.shape[1]
    return pl.pallas_call(
        pack_queries_kernel,
        out_shape=(
            jax.ShapeDtypeStruct((pool_count, 264, 128), BF16),
            jax.ShapeDtypeStruct((slots + 8,), jnp.int32),
        ),
        in_specs=[SMEM_SPEC] * 2 + [ANY_SPEC] * 2,
        out_specs=(VMEM_SPEC, SMEM_SPEC),
        scratch_shapes=[
            pltpu.VMEM(queries.shape, BF16),
            pltpu.VMEM(new_latent.shape, BF16),
            pltpu.VMEM(new_latent.shape, F32),
            pltpu.VMEM((pool_count * 8, 128), F32),
            pltpu.SemaphoreType.DMA((2,)),
        ],
        compiler_params=params(60),
        cost_estimate=cost(),
        name="pack_queries",
    )(decode_slot, where, queries, new_latent)


def padded_rows(piece, feature):
    return -(-(piece * feature // 128) // STRIP) * STRIP


def window_start(row, piece, window, span):
    return pl.multiple_of(jnp.where(row + piece > window, span - window, 0), 128)


def picker(row, start, piece, window):
    pick = lax.broadcasted_iota(jnp.int32, (piece, window), 1) - (
        row - start + lax.broadcasted_iota(jnp.int32, (piece, window), 0)
    )
    return jnp.where(pick == 0, 1.0, 0.0).astype(BF16)


def packed_piece(pick, latents):
    piece = pick.shape[0]
    blocks = latents.shape[0] // 128
    turned = lax.dot_general(pick, latents, NT, preferred_element_type=F32)
    last = turned[:, 128 * blocks :]
    last = jnp.concatenate([last[: piece // 2], last[piece // 2 :]], axis=1)
    return jnp.concatenate(
        [turned[:, 128 * b : 128 * b + 128] for b in range(blocks)] + [last], axis=0
    ).astype(BF16)


def pack_context_kernel(
    decode_slot, where, p_ref,
    out_ref, placing, later, coming, relay, rounds,
    leaving, counts, ahead, code, source, buf, sems,
):
    slots, feature, window = buf.shape
    owners = out_ref.shape[0]
    padded = (out_ref.shape[1] - SPILL * STRIP) // DIRECT
    piece = padded * 128 // feature // 16 * 16
    rows = piece * feature // 128
    strips = padded // STRIP
    chunk = slots // sems.shape[0]
    row = where[0] * piece
    start = window_start(row, piece, window, p_ref.shape[2])
    copies = [
        pltpu.make_async_copy(
            p_ref.at[pl.ds(k * chunk, chunk), :, pl.ds(start, window)],
            buf.at[pl.ds(k * chunk, chunk)],
            sems.at[k],
        )
        for k in range(sems.shape[0])
    ]
    for copy in copies:
        copy.start()
    bits = slots.bit_length() - 1

    for p in range(owners):
        counts[p] = 0
    spilled = jnp.int32(0)
    for g in range(slots):
        owner = decode_slot[where[1] * slots + g] >> bits
        rank = counts[owner]
        counts[owner] = rank + 1
        placing[g] = owner * CAP + rank
        over = rank >= DIRECT
        leaving[g] = jnp.where(over, spilled, -1)
        spilled = spilled + over.astype(jnp.int32)
    pick = picker(row, start, piece, window)

    def clear(n, carry):
        counts[n] = 0
        return carry

    lax.fori_loop(0, owners * owners, clear, 0, unroll=16)
    first = where[1] * slots

    def look(k, spilled):
        after = []
        for p in range(owners):
            slot = decode_slot[p * slots + k]
            owner = slot >> bits
            rank = counts[p * owners + owner]
            counts[p * owners + owner] = rank + 1
            over = rank >= DIRECT
            ahead[p * (SPILL + 1) + jnp.where(over, jnp.minimum(spilled[p], SPILL), SPILL)] = owner
            inner = slot - first
            at = jnp.where((inner >= 0) & (inner < slots), inner, slots)
            coming[at] = jnp.where(over, spilled[p], -1)
            source[at] = p
            after.append(spilled[p] + over.astype(jnp.int32))
        return tuple(after)

    spilled = lax.fori_loop(0, slots, look, (jnp.int32(0),) * owners)
    for q in range(owners):
        counts[q] = 0
    for n in range(owners * SPILL):
        relay[n] = 0
    longest = jnp.int32(0)
    for p in range(owners):
        hopped = jnp.int32(0)
        for n in range(SPILL):
            owner = jnp.where(n < spilled[p], ahead[p * (SPILL + 1) + n], 0)
            entry = counts[owner]
            hops = (n < spilled[p]) & (entry < SPILL)
            counts[owner] = entry + hops.astype(jnp.int32)
            relay[jnp.where(hops, owner * SPILL + entry, owners * SPILL)] = p * SPILL + n
            code[p * (SPILL + 1) + n] = jnp.where(hops, entry, SPILL + n - hopped)
            hopped = hopped + hops.astype(jnp.int32)
        code[p * (SPILL + 1) + SPILL] = SPILL - hopped
        longest = jnp.maximum(longest, spilled[p] - hopped)
    rounds[0] = (longest + SPILL - 1) // SPILL

    def coded(p, n):
        found = code[p * (SPILL + 1) + jnp.clip(n, 0, SPILL)]
        return jnp.where(n < 0, -1, jnp.where(n < SPILL, found, found + n))

    def finish(n, carry):
        coming[n] = coded(source[n], coming[n])
        later[n] = coded(where[1], leaving[n])
        return carry

    lax.fori_loop(0, slots, finish, 0, unroll=4)

    for k, copy in enumerate(copies):
        copy.wait()

        def one(n, carry):
            g = k * chunk + n
            dest, rank = split(placing[g])
            cell = packed_piece(pick, buf[g])

            @pl.when(rank < DIRECT)
            def _():
                out_ref[dest, pl.ds(pl.multiple_of(rank * padded, STRIP), rows), :] = cell

            @pl.when((rank >= DIRECT) & (leaving[g] < SPILL))
            def _():
                at = DIRECT * padded + leaving[g] * STRIP
                for m in range(strips):
                    high = min(STRIP, rows - m * STRIP)
                    out_ref[m, pl.ds(pl.multiple_of(at, STRIP), high), :] = cell[
                        m * STRIP : m * STRIP + high
                    ]

            return carry

        lax.fori_loop(0, chunk, one, 0, unroll=8)


def pack_context(decode_slot, where, prompt_latent, piece, pool_count):
    slots, feature, _ = prompt_latent.shape
    rows = padded_rows(piece, feature)
    return pl.pallas_call(
        pack_context_kernel,
        out_shape=(
            jax.ShapeDtypeStruct((pool_count, DIRECT * rows + SPILL * STRIP, 128), BF16),
            jax.ShapeDtypeStruct((slots,), jnp.int32),
            jax.ShapeDtypeStruct((slots,), jnp.int32),
            jax.ShapeDtypeStruct((slots + 8,), jnp.int32),
            jax.ShapeDtypeStruct((pool_count * SPILL + 8,), jnp.int32),
            jax.ShapeDtypeStruct((1,), jnp.int32),
        ),
        in_specs=[SMEM_SPEC] * 2 + [ANY_SPEC],
        out_specs=(VMEM_SPEC,) + (SMEM_SPEC,) * 5,
        scratch_shapes=[
            pltpu.SMEM((slots,), jnp.int32),
            pltpu.SMEM((pool_count * pool_count,), jnp.int32),
            pltpu.SMEM((pool_count * (SPILL + 1),), jnp.int32),
            pltpu.SMEM((pool_count * (SPILL + 1),), jnp.int32),
            pltpu.SMEM((slots + 8,), jnp.int32),
            pltpu.VMEM((slots, feature, 256), BF16),
            pltpu.SemaphoreType.DMA((4,)),
        ],
        compiler_params=params(63),
        cost_estimate=cost(),
        name="pack_context",
    )(decode_slot, where, prompt_latent)


def pack_spill_kernel(turn, leaving, where, p_ref, spill_ref, buf, sem):
    feature, window = buf.shape
    piece = spill_ref.shape[1] * 128 // feature // 16 * 16
    row = where[0] * piece
    start = window_start(row, piece, window, p_ref.shape[2])
    pick = picker(row, start, piece, window)

    def one(g, carry):
        at = leaving[g] - SPILL - turn[0] * SPILL

        @pl.when((at >= 0) & (at < SPILL))
        def _():
            copy = pltpu.make_async_copy(p_ref.at[g, :, pl.ds(start, window)], buf, sem)
            copy.start()
            copy.wait()
            cell = packed_piece(pick, buf[...])
            spill_ref[at, : cell.shape[0], :] = cell

        return carry

    lax.fori_loop(0, p_ref.shape[0], one, 0)


def pack_spill(turn, leaving, where, prompt_latent, piece):
    slots, feature, _ = prompt_latent.shape
    return pl.pallas_call(
        pack_spill_kernel,
        out_shape=jax.ShapeDtypeStruct((SPILL, padded_rows(piece, feature), 128), BF16),
        in_specs=[SMEM_SPEC] * 3 + [ANY_SPEC],
        out_specs=VMEM_SPEC,
        scratch_shapes=[pltpu.VMEM((feature, 256), BF16), pltpu.SemaphoreType.DMA],
        compiler_params=params(),
        cost_estimate=cost(),
        name="pack_spill",
    )(turn, leaving, where, prompt_latent)


def unpack_piece(out_ref, row, packed, at, start, first_row, length):
    piece, feature = out_ref.shape[1:]
    blocks = feature // 128
    for b in range(blocks):
        out_ref[row, :, 128 * b : 128 * b + 128] = packed[at, pl.ds(start + b * piece, piece), :]
    last = packed[at, pl.ds(start + blocks * piece, piece // 2), :].astype(F32)
    last = jnp.concatenate([last[:, :64], last[:, 64:]], axis=0)
    out_ref[row, :, 128 * blocks :] = last.astype(BF16)

    @pl.when(length < first_row + piece)
    def _():
        whole = out_ref[row].astype(F32)
        position = first_row + lax.broadcasted_iota(jnp.int32, whole.shape, 0)
        out_ref[row] = jnp.where(position < length, whole, 0.0).astype(BF16)


def place_kernel(
    decode_slot, prompt_lengths, arrival, where, direct, out_ref, lengths, outbox, sems
):
    slots, piece, feature = out_ref.shape
    first = where[1] * slots

    def measure(p, carry):
        for k in range(slots):
            inner = decode_slot[p * slots + k] - first
            at = jnp.where((inner >= 0) & (inner < slots), inner, slots)
            lengths[at] = prompt_lengths[p * slots + k]
        return carry

    lax.fori_loop(0, direct.shape[0], measure, 0)
    padded = (direct.shape[1] - SPILL * STRIP) // DIRECT
    chunk = slots // sems.shape[0]

    def copy_out(k):
        part = pl.ds(k * chunk, chunk)
        return pltpu.make_async_copy(outbox.at[part], out_ref.at[part], sems.at[k])

    def one(j, carry):
        owner, rank = split(arrival[j])
        at = pl.multiple_of(jnp.minimum(rank, DIRECT - 1) * padded, STRIP)
        unpack_piece(outbox, j, direct, owner, at, where[0] * piece, lengths[j])
        return carry

    for k in range(sems.shape[0]):
        lax.fori_loop(k * chunk, k * chunk + chunk, one, 0, unroll=2)
        copy_out(k).start()
    for k in range(sems.shape[0]):
        copy_out(k).wait()


def place(decode_slot, prompt_lengths, arrival, where, direct, piece, feature):
    slots = arrival.shape[0] - 8
    return pl.pallas_call(
        place_kernel,
        out_shape=(
            jax.ShapeDtypeStruct((slots, piece, feature), BF16),
            jax.ShapeDtypeStruct((slots + 8,), jnp.int32),
        ),
        in_specs=[SMEM_SPEC] * 4 + [VMEM_SPEC],
        out_specs=(ANY_SPEC, SMEM_SPEC),
        scratch_shapes=[
            pltpu.VMEM((slots, piece, feature), BF16),
            pltpu.SemaphoreType.DMA((4,)),
        ],
        compiler_params=params(),
        cost_estimate=cost(bytes_accessed=12_000_000),
        name="place_context",
    )(decode_slot, prompt_lengths, arrival, where, direct)


def place_strips_kernel(
    coming, lengths, where, back, context, out_ref, inbox, whole, outbox, in_sems, out_sems
):
    slots, piece, feature = out_ref.shape
    strips = inbox.shape[1]

    def copy_in(e):
        source = back.at[pl.ds(0, strips), pl.ds(e * STRIP, STRIP), :]
        return pltpu.make_async_copy(source, inbox.at[e], in_sems.at[e])

    def copy_out(j, e):
        return pltpu.make_async_copy(outbox.at[e], out_ref.at[j], out_sems.at[e])

    for e in range(SPILL):
        copy_in(e).start()
    for e in range(SPILL):
        copy_in(e).wait()
        for m in range(strips):
            whole[e, m * STRIP : m * STRIP + STRIP, :] = inbox[e, m]

    def each(action):
        def step(j, carry):
            for e in range(SPILL):

                @pl.when(coming[j] == e)
                def _():
                    action(j, e)

            return carry

        lax.fori_loop(0, slots, step, 0)

    def work(j, e):
        unpack_piece(outbox, e, whole, e, 0, where[0] * piece, lengths[j])
        copy_out(j, e).start()

    each(work)
    each(lambda j, e: copy_out(j, e).wait())


def place_strips(coming, lengths, where, back, context):
    slots, piece, feature = context.shape
    strips = padded_rows(piece, feature) // STRIP
    return pl.pallas_call(
        place_strips_kernel,
        out_shape=jax.ShapeDtypeStruct(context.shape, BF16),
        in_specs=[SMEM_SPEC] * 3 + [ANY_SPEC] * 2,
        out_specs=ANY_SPEC,
        scratch_shapes=[
            pltpu.VMEM((SPILL, strips, STRIP, 128), BF16),
            pltpu.VMEM((SPILL, strips * STRIP, 128), BF16),
            pltpu.VMEM((SPILL, piece, feature), BF16),
            pltpu.SemaphoreType.DMA((SPILL,)),
            pltpu.SemaphoreType.DMA((SPILL,)),
        ],
        input_output_aliases={4: 0},
        compiler_params=params(),
        cost_estimate=cost(bytes_accessed=6_000_000),
        name="place_strips",
    )(coming, lengths, where, back, context)


def place_spill_kernel(
    turn, arrival, coming, lengths, where, spill, context, out_ref, inbox, outbox, sem
):
    slots, piece, feature = out_ref.shape

    def one(j, carry):
        at = coming[j] - SPILL - turn[0] * SPILL

        @pl.when((at >= 0) & (at < SPILL))
        def _():
            owner = split(arrival[j])[0]
            copy = pltpu.make_async_copy(
                spill.at[owner, jnp.clip(at, 0, SPILL - 1)], inbox.at[0], sem
            )
            copy.start()
            copy.wait()
            unpack_piece(outbox, 0, inbox, 0, 0, where[0] * piece, lengths[j])
            copy = pltpu.make_async_copy(outbox.at[0], out_ref.at[j], sem)
            copy.start()
            copy.wait()

        return carry

    lax.fori_loop(0, slots, one, 0)


def place_spill(turn, arrival, coming, lengths, where, spill, context):
    return pl.pallas_call(
        place_spill_kernel,
        out_shape=jax.ShapeDtypeStruct(context.shape, BF16),
        in_specs=[SMEM_SPEC] * 5 + [ANY_SPEC] * 2,
        out_specs=ANY_SPEC,
        scratch_shapes=[
            pltpu.VMEM((1,) + spill.shape[-2:], BF16),
            pltpu.VMEM((1,) + context.shape[1:], BF16),
            pltpu.SemaphoreType.DMA,
        ],
        input_output_aliases={6: 0},
        compiler_params=params(),
        cost_estimate=cost(),
        name="place_spill",
    )(turn, arrival, coming, lengths, where, spill, context)


def attention_kernel(
    placing, lengths, where, payload_hbm, p_hbm, w_uk_hbm, w_uv_hbm, w_out_hbm,
    given_ref, kept_ref,
    payload, prompt, w_uk, w_uv, w_out,
    q_nope, q_rope, acc, fresh, tails, fresh_score, total, head_out, sems,
):
    steps = 4
    heads, latent, nope = w_uk.shape
    slots, feature, span = prompt.shape
    chunks = latent // 128
    per_step = slots * heads
    many = slots * steps
    scale = 1.0 / math.sqrt(nope + ROPE)
    first = where[1] * slots
    copy_payload = pltpu.make_async_copy(payload_hbm, payload, sems.at[0])
    copy_uk = pltpu.make_async_copy(w_uk_hbm, w_uk, sems.at[1])
    copy_uv = pltpu.make_async_copy(w_uv_hbm, w_uv, sems.at[2])
    copy_out = pltpu.make_async_copy(w_out_hbm, w_out, sems.at[3])

    def copy_prompt(k):
        part = pl.ds(k * GROUP, GROUP)
        return pltpu.make_async_copy(p_hbm.at[part], prompt.at[part], sems.at[4 + k])

    copy_payload.start()
    copy_uk.start()
    for k in range(slots // GROUP):
        copy_prompt(k).start()
    copy_uv.start()
    copy_out.start()

    def spread(ref, i, lead=()):
        return jnp.concatenate(
            [
                ref[(*lead, pl.ds(pl.multiple_of(per_step * s + heads * i, 8), heads), slice(None))]
                for s in range(steps)
            ],
            axis=0,
        )

    def collect(ref, i, value, lead=()):
        for s in range(steps):
            ref[(*lead, pl.ds(pl.multiple_of(per_step * s + heads * i, 8), heads), slice(None))] = (
                value[heads * s : heads * s + heads]
            )

    copy_payload.wait()
    tails[...] = payload[:, 256:264, :].astype(F32).reshape(tails.shape)

    def unpack(i, carry):
        dest, rank = split(placing[i])
        cell = payload[dest, pl.ds(pl.multiple_of(rank * 64, 64), 64), :].astype(F32)
        collect(q_nope, i, cell[:32])
        rope = jnp.concatenate([cell[32:48, :64], cell[32:48, 64:]], axis=0)
        collect(q_rope, i, jnp.concatenate([rope, jnp.zeros_like(rope)], axis=1))
        for b in range(chunks):
            fresh[b, pl.ds(steps * i, steps), :] = cell[48 + 4 * b : 52 + 4 * b]
        last = tails[pl.ds(dest * 8 + rank * 2, 2), :]
        last = jnp.concatenate([last[:, :64], last[:, 64:]], axis=0)
        fresh[chunks, pl.ds(steps * i, steps), :] = jnp.concatenate(
            [last, jnp.zeros_like(last)], axis=1
        )
        return carry

    lax.fori_loop(0, slots, unpack, 0, unroll=8)
    copy_uk.wait()
    for h in range(heads):
        rows = pl.ds(h, many, stride=heads)
        a = lax.dot_general(
            q_nope[rows, :].astype(BF16), w_uk[h], NT, preferred_element_type=F32
        )
        a = a.astype(BF16).astype(F32)
        for c in range(chunks):
            acc[c, rows, :] = a[:, 128 * c : 128 * c + 128]
    keys = jnp.concatenate([fresh[b] for b in range(chunks + 1)], axis=1).astype(BF16)

    def score(k, carry):
        rows = pl.ds(pl.multiple_of(k * 128, 128), 128)
        q = jnp.concatenate(
            [acc[c, rows, :] for c in range(chunks)] + [q_rope[rows, :]], axis=1
        ).astype(BF16)
        fresh_score[rows, :] = scale * lax.dot_general(q, keys, NT, preferred_element_type=F32)
        return carry

    lax.fori_loop(0, per_step * steps // 128, score, 0, unroll=2)

    def one(i):
        q = jnp.concatenate(
            [spread(acc, i, (c,)) for c in range(chunks)] + [spread(q_rope, i)[:, :ROPE]], axis=1
        ).astype(BF16)
        s_prompt = scale * jnp.dot(q, prompt[i], preferred_element_type=F32)
        s_fresh = spread(fresh_score, i)
        column = lax.broadcasted_iota(jnp.int32, s_prompt.shape, 1)
        s_prompt = jnp.where(column < lengths[first + i], s_prompt, FLOOR)
        step_of = lax.broadcasted_iota(jnp.int32, s_fresh.shape, 0) // heads
        column = lax.broadcasted_iota(jnp.int32, s_fresh.shape, 1) - steps * i
        s_fresh = jnp.where((column >= 0) & (column <= step_of), s_fresh, FLOOR)
        peak = jnp.maximum(
            jnp.max(s_prompt, axis=1, keepdims=True), jnp.max(s_fresh, axis=1, keepdims=True)
        )
        w_prompt = jnp.exp(s_prompt - peak)
        w_fresh = jnp.exp(s_fresh - peak)
        sums = jnp.sum(w_prompt, axis=1, keepdims=True) + jnp.sum(w_fresh, axis=1, keepdims=True)
        mixed = lax.dot_general(
            w_prompt.astype(BF16), prompt[i, :latent], NT, preferred_element_type=F32
        )
        for c in range(chunks):
            collect(acc, i, mixed[:, 128 * c : 128 * c + 128], (c,))
        collect(fresh_score, i, w_fresh)
        collect(total, i, jnp.broadcast_to(sums, s_fresh.shape))

    def attend(k, carry):
        copy_prompt(k).wait()
        for n in range(GROUP):
            one(k * GROUP + n)
        return carry

    lax.fori_loop(0, slots // GROUP, attend, 0)

    values = jnp.concatenate([fresh[b] for b in range(chunks)], axis=1).astype(BF16)
    copy_uv.wait()
    for h in range(heads):
        rows = pl.ds(h, many, stride=heads)
        mixed = jnp.dot(fresh_score[rows, :].astype(BF16), values, preferred_element_type=F32)
        mixed = mixed + jnp.concatenate([acc[c, rows, :] for c in range(chunks)], axis=1)
        part = 1.0 / total[rows, :]
        mixed = (mixed * jnp.concatenate([part] * chunks, axis=1)).astype(BF16)
        head_out[:, h * 128 : h * 128 + 128] = jnp.dot(
            mixed, w_uv[h], preferred_element_type=F32
        ).astype(BF16)
    copy_out.wait()
    half = many // 2
    core = where[0] % 2
    mine = head_out[pl.ds(pl.multiple_of(core * half, half), half), :]
    theirs = head_out[pl.ds(pl.multiple_of((1 - core) * half, half), half), :]
    both = jnp.concatenate([theirs, mine], axis=0)
    for b in range(w_out.shape[1] // 512):
        at_b = slice(b * 512, b * 512 + 512)
        summed = jnp.dot(both, w_out[:, at_b], preferred_element_type=F32)
        given_ref[:, at_b] = summed[:half].astype(BF16)
        kept_ref[:, at_b] = summed[half:].astype(BF16)


def attention(placing, lengths, where, payload, prompt_latent, w_uk, w_uv, w_out, steps):
    slots, feature, span = prompt_latent.shape
    heads, latent, nope = w_uk.shape
    width = w_out.shape[1]
    rows = steps * slots * heads
    half = steps * slots // 2
    chunks = latent // 128
    return pl.pallas_call(
        attention_kernel,
        out_shape=(
            jax.ShapeDtypeStruct((half, width), BF16),
            jax.ShapeDtypeStruct((half, width), BF16),
        ),
        in_specs=[SMEM_SPEC] * 3 + [ANY_SPEC] * 5,
        out_specs=(VMEM_SPEC, VMEM_SPEC),
        scratch_shapes=[
            pltpu.VMEM(payload.shape, BF16),
            pltpu.VMEM(prompt_latent.shape, BF16),
            pltpu.VMEM(w_uk.shape, BF16),
            pltpu.VMEM(w_uv.shape, BF16),
            pltpu.VMEM(w_out.shape, BF16),
            pltpu.VMEM((rows, 128), F32),
            pltpu.VMEM((rows, 128), F32),
            pltpu.VMEM((chunks, rows, 128), F32),
            pltpu.VMEM((chunks + 1, steps * slots, 128), F32),
            pltpu.VMEM((payload.shape[0] * 8, 128), F32),
            pltpu.VMEM((rows, 128), F32),
            pltpu.VMEM((rows, 128), F32),
            pltpu.VMEM((steps * slots, heads * 128), BF16),
            pltpu.SemaphoreType.DMA((4 + slots // GROUP,)),
        ],
        compiler_params=params(60),
        cost_estimate=cost(),
        name="attention",
    )(placing, lengths, where, payload, prompt_latent, w_uk, w_uv, w_out)


def share_kernel(where, kept, swapped, mine, *parts):
    block = mine.shape[1]
    z = where[0] >> 1
    for d, part in enumerate((mine,) + parts):
        at = pl.ds(pl.multiple_of((z ^ d) * block, 128), block)
        part[...] = (kept[:, at].astype(F32) + swapped[:, at].astype(F32)).astype(part.dtype)


def share(where, kept, swapped, z_count):
    rows, width = kept.shape
    block = width // z_count
    return pl.pallas_call(
        share_kernel,
        out_shape=(jax.ShapeDtypeStruct((rows, block), F32),)
        + (jax.ShapeDtypeStruct((rows, block), BF16),) * (z_count - 1),
        in_specs=[SMEM_SPEC] + [VMEM_SPEC] * 2,
        out_specs=(VMEM_SPEC,) * z_count,
        compiler_params=params(),
        cost_estimate=cost(),
        name="share",
    )(where, kept, swapped)


def pack_back_kernel(placing, relay, direct, mine, *rest):
    parts, (out_ref, strips, total, rows, sem) = rest[:-5], rest[-5:]
    slots = placing.shape[0]
    blocks = mine.shape[1] // 128
    steps = mine.shape[0] // slots
    hop = SPILL * STRIP
    fetch = pltpu.make_async_copy(
        direct.at[:, pl.ds(direct.shape[1] - hop, hop), :], strips, sem
    )
    fetch.start()
    whole = mine[...]
    for part in parts:
        whole = whole + part[...].astype(F32)
    for b in range(blocks):
        total[b] = whole[:, 128 * b : 128 * b + 128]
    def one(i, carry):
        dest, rank = split(placing[i])
        for s in range(steps):
            for b in range(blocks):
                at = dest * (8 * blocks) + 8 * b + steps * rank + s
                rows[pl.ds(at, 1), :] = total[b, pl.ds(slots * s + i, 1), :]
        return carry

    lax.fori_loop(0, slots, one, 0, unroll=4)
    out_ref[:, hop:, :] = rows[...].reshape(out_ref.shape[0], 8 * blocks, 128).astype(BF16)
    fetch.wait()
    for q in range(out_ref.shape[0]):
        for e in range(SPILL):
            came = relay[q * SPILL + e]
            at = pl.multiple_of((came % SPILL) * STRIP, STRIP)
            out_ref[q, e * STRIP : e * STRIP + STRIP, :] = strips[
                came // SPILL, pl.ds(at, STRIP), :
            ]


def pack_back(placing, relay, direct, mine, parts):
    pool_count = direct.shape[0]
    blocks = mine.shape[1] // 128
    hop = SPILL * STRIP
    return pl.pallas_call(
        pack_back_kernel,
        out_shape=jax.ShapeDtypeStruct((pool_count, hop + 8 * blocks, 128), BF16),
        in_specs=[SMEM_SPEC] * 2 + [ANY_SPEC] + [VMEM_SPEC] * (1 + len(parts)),
        out_specs=VMEM_SPEC,
        scratch_shapes=[
            pltpu.VMEM((pool_count, hop, 128), BF16),
            pltpu.VMEM((blocks, mine.shape[0], 128), F32),
            pltpu.VMEM((pool_count * 8 * blocks, 128), F32),
            pltpu.SemaphoreType.DMA,
        ],
        compiler_params=params(),
        cost_estimate=cost(),
        name="pack_back",
    )(placing, relay, direct, mine, *parts)


def unpack_back_kernel(steps, arrival, packed, out_ref, rows, total):
    slots = out_ref.shape[0] // steps
    blocks = out_ref.shape[1] // 128
    first = packed.shape[1] - 8 * blocks
    rows[...] = packed[:, first:, :].astype(F32).reshape(rows.shape)

    def one(j, carry):
        owner, rank = split(arrival[j])
        for b in range(blocks):
            at = owner * (8 * blocks) + 8 * b + steps * rank
            total[b, pl.ds(steps * j, steps), :] = rows[pl.ds(at, steps), :]
        return carry

    lax.fori_loop(0, slots, one, 0, unroll=4)
    for b in range(blocks):
        out_ref[:, 128 * b : 128 * b + 128] = total[b].astype(BF16)


def unpack_back(arrival, packed, steps, slots, block):
    return pl.pallas_call(
        functools.partial(unpack_back_kernel, steps),
        out_shape=jax.ShapeDtypeStruct((steps * slots, block), BF16),
        in_specs=[SMEM_SPEC, VMEM_SPEC],
        out_specs=VMEM_SPEC,
        scratch_shapes=[
            pltpu.VMEM((packed.shape[0] * 8 * (block // 128), 128), F32),
            pltpu.VMEM((block // 128, steps * slots, 128), F32),
        ],
        compiler_params=params(),
        cost_estimate=cost(),
        name="unpack_back",
    )(arrival, packed)


def assemble_kernel(where, *rest):
    parts, (out_ref, part, whole) = rest[:-3], rest[-3:]
    slots, steps, width = out_ref.shape
    z_count = len(parts) // 2
    block = width // z_count
    core, z = where[0] & 1, where[0] >> 1
    for n, ref in enumerate(parts):
        side = core if n < z_count else 1 - core
        start = (z ^ (n % z_count)) * (block // 128)
        for b in range(block // 128):
            part[...] = ref[:, 128 * b : 128 * b + 128].astype(F32)
            for s in range(steps // 2):
                whole[start + b, pl.ds((steps // 2) * side + s, slots, stride=steps), :] = part[
                    pl.ds(s, slots, stride=steps // 2), :
                ]
    for b in range(width // 128):
        out_ref[:, :, 128 * b : 128 * b + 128] = (
            whole[b].reshape(slots, steps, 128).astype(BF16)
        )


def assemble(where, parts, slots, steps, width):
    return pl.pallas_call(
        assemble_kernel,
        out_shape=jax.ShapeDtypeStruct((slots, steps, width), BF16),
        in_specs=[SMEM_SPEC] + [VMEM_SPEC] * len(parts),
        out_specs=VMEM_SPEC,
        scratch_shapes=[
            pltpu.VMEM((parts[0].shape[0], 128), F32),
            pltpu.VMEM((width // 128, slots * steps, 128), F32),
        ],
        compiler_params=params(),
        cost_estimate=cost(),
        name="assemble",
    )(where, *parts)


def exchange(x):
    return lax.all_to_all(x, "pool", split_axis=0, concat_axis=0, tiled=True)


def body(prompt_latent, prompt_lengths, decode_slot, new_latent, queries, w_uk, w_uv, w_out):
    pool_count = lax.axis_size("pool")
    tp_count = lax.axis_size("tp")
    tp_index = lax.axis_index("tp")
    latent_t = prompt_latent.transpose(0, 2, 1)
    steps, slots, heads, width = queries.shape
    span, feature = prompt_latent.shape[1:]
    piece = span // tp_count
    out_width = w_out.shape[1]
    z_count = tp_count // 2
    where = jnp.stack([tp_index, lax.axis_index("pool")]).astype(jnp.int32)
    swap = [(i, i ^ 1) for i in range(tp_count)]
    hops = [[(i, i ^ (2 * d)) for i in range(tp_count)] for d in range(1, z_count)]

    payload, arrival = pack_queries(decode_slot, where, queries, new_latent, pool_count)
    payload = exchange(payload)
    direct, placing, leaving, coming, relay, rounds = pack_context(
        decode_slot, where, latent_t, piece, pool_count
    )
    payload, direct = lax.optimization_barrier((payload, direct))
    direct = exchange(direct)

    given, kept = attention(
        placing, prompt_lengths, where, payload, latent_t, w_uk, w_uv, w_out, steps
    )

    swapped = lax.ppermute(given, "tp", swap)
    mine, *parts = share(where, kept, swapped, z_count)
    parts = [lax.ppermute(part, "tp", hop) for part, hop in zip(parts, hops)]

    back = exchange(pack_back(placing, relay, direct, mine, parts))
    context, lengths = place(
        decode_slot, prompt_lengths, arrival, where, direct, piece, feature
    )
    back, context = lax.optimization_barrier((back, context))
    own = unpack_back(arrival, back, steps // 2, slots, out_width // z_count)
    parts = [own] + [lax.ppermute(own, "tp", hop) for hop in hops]
    swapped = [lax.ppermute(own, "tp", swap)]
    context = place_strips(coming, lengths, where, back, context)

    def more(state):
        turn, context = state
        spill = pack_spill(turn, leaving, where, latent_t, piece)
        spill = exchange(jnp.broadcast_to(spill[None], (pool_count,) + spill.shape))
        context = place_spill(turn, arrival, coming, lengths, where, spill, context)
        return turn + 1, context

    context = lax.while_loop(
        lambda state: state[0][0] < rounds[0], more, (jnp.zeros((1,), jnp.int32), context)
    )[1]
    context, *parts = lax.optimization_barrier((context, *parts))
    parts = parts + swapped + [lax.ppermute(part, "tp", swap) for part in parts[1:]]
    decoded = assemble(where, parts, slots, steps, out_width)
    return decoded, context


def solution(mesh):
    in_specs = (
        P("pool", None, None),
        P(),
        P(),
        P(None, "pool", None),
        P(None, "pool", "tp", None),
        P("tp", None, None),
        P("tp", None, None),
        P("tp", None),
    )
    out_specs = (P("pool", None, None), P("pool", "tp", None))
    return jax.shard_map(body, mesh=mesh, in_specs=in_specs, out_specs=out_specs, check_vma=False)
```

```python
import functools
import math

import jax
import jax.numpy as jnp
from jax import lax
from jax.experimental import pallas as pl
from jax.experimental.pallas import tpu as pltpu
from jax.sharding import PartitionSpec as P

ROPE = 64
NOPE = 128
CAP = 4
DIRECT = 2
SPILL = 2
STRIP = 16
GROUP = 16
FLOOR = -1e30
BF16 = jnp.bfloat16
F32 = jnp.float32

MIB = 1024 * 1024
SMEM_SPEC = pl.BlockSpec(memory_space=pltpu.SMEM)
VMEM_SPEC = pl.BlockSpec(memory_space=pltpu.VMEM)
ANY_SPEC = pl.BlockSpec(memory_space=pl.ANY)
NT = (((1,), (1,)), ((), ()))


def params(mib=16):
    return pltpu.CompilerParams(vmem_limit_bytes=mib * MIB)


def cost(flops=1000, bytes_accessed=1000):
    return pl.CostEstimate(flops=flops, bytes_accessed=bytes_accessed, transcendentals=0)


def split(cell):
    return cell // CAP, cell % CAP


def pack_queries_kernel(
    decode_slot, where, q_hbm, n_hbm,
    out_ref, arrival,
    q_ref, n_ref, new_rows, tails, sems,
):
    steps, slots, heads, width = q_ref.shape
    rows = steps * heads
    blocks = n_ref.shape[2] // 128
    copy_n = pltpu.make_async_copy(n_hbm, n_ref, sems.at[0])
    copy_q = pltpu.make_async_copy(q_hbm, q_ref, sems.at[1])
    copy_n.start()
    copy_q.start()
    first = where[1] * slots

    def locate(p, carry):
        rank = jnp.int32(0)
        for k in range(slots):
            inner = decode_slot[p * slots + k] - first
            hit = (inner >= 0) & (inner < slots)
            at = jnp.where(hit, inner, slots)
            arrival[at] = p * CAP + rank
            rank = rank + hit.astype(jnp.int32)
        return carry

    lax.fori_loop(0, out_ref.shape[0], locate, 0)
    tails[...] = jnp.zeros(tails.shape, F32)
    copy_n.wait()
    new_rows[...] = n_ref[...].astype(F32)
    copy_q.wait()

    def one(j, carry):
        dest, rank = split(arrival[j])
        x = q_ref[:, j].astype(F32)
        nope = x[:, :, :NOPE].reshape(rows, NOPE)
        rope = x[:, :, NOPE:].reshape(rows, ROPE)
        rope = jnp.concatenate([rope[: rows // 2], rope[rows // 2 :]], axis=1)
        fresh = jnp.concatenate([new_rows[s, pl.ds(j, 1), :] for s in range(steps)], axis=0)
        body = [fresh[:, 128 * b : 128 * b + 128] for b in range(blocks)]
        last = fresh[:, 128 * blocks :]
        cell = jnp.concatenate([nope, rope] + body, axis=0)
        out_ref[dest, pl.ds(pl.multiple_of(rank * 64, 64), 64), :] = cell.astype(BF16)
        tails[pl.ds(dest * 8 + rank * 2, 2), :] = jnp.concatenate(
            [last[: steps // 2], last[steps // 2 :]], axis=1
        )
        return carry

    lax.fori_loop(0, slots, one, 0, unroll=8)
    out_ref[:, 256:264, :] = tails[...].reshape(out_ref.shape[0], 8, 128).astype(BF16)


def pack_queries(decode_slot, where, queries, new_latent, pool_count):
    slots = queries.shape[1]
    return pl.pallas_call(
        pack_queries_kernel,
        out_shape=(
            jax.ShapeDtypeStruct((pool_count, 264, 128), BF16),
            jax.ShapeDtypeStruct((slots + 8,), jnp.int32),
        ),
        in_specs=[SMEM_SPEC] * 2 + [ANY_SPEC] * 2,
        out_specs=(VMEM_SPEC, SMEM_SPEC),
        scratch_shapes=[
            pltpu.VMEM(queries.shape, BF16),
            pltpu.VMEM(new_latent.shape, BF16),
            pltpu.VMEM(new_latent.shape, F32),
            pltpu.VMEM((pool_count * 8, 128), F32),
            pltpu.SemaphoreType.DMA((2,)),
        ],
        compiler_params=params(60),
        cost_estimate=cost(),
        name="pack_queries",
    )(decode_slot, where, queries, new_latent)


def padded_rows(piece, feature):
    return -(-(piece * feature // 128) // STRIP) * STRIP


def window_start(row, piece, window, span):
    return pl.multiple_of(jnp.where(row + piece > window, span - window, 0), 128)


def picker(row, start, piece, window):
    pick = lax.broadcasted_iota(jnp.int32, (piece, window), 1) - (
        row - start + lax.broadcasted_iota(jnp.int32, (piece, window), 0)
    )
    return jnp.where(pick == 0, 1.0, 0.0).astype(BF16)


def packed_piece(pick, latents):
    piece = pick.shape[0]
    blocks = latents.shape[0] // 128
    turned = lax.dot_general(pick, latents, NT, preferred_element_type=F32)
    last = turned[:, 128 * blocks :]
    last = jnp.concatenate([last[: piece // 2], last[piece // 2 :]], axis=1)
    return jnp.concatenate(
        [turned[:, 128 * b : 128 * b + 128] for b in range(blocks)] + [last], axis=0
    ).astype(BF16)


def pack_context_kernel(
    decode_slot, where, p_ref,
    out_ref, placing, later, coming, relay, rounds,
    leaving, counts, ahead, code, source, buf, sems,
):
    slots, feature, window = buf.shape
    owners = out_ref.shape[0]
    padded = (out_ref.shape[1] - SPILL * STRIP) // DIRECT
    piece = padded * 128 // feature // 16 * 16
    rows = piece * feature // 128
    strips = padded // STRIP
    chunk = slots // sems.shape[0]
    row = where[0] * piece
    start = window_start(row, piece, window, p_ref.shape[2])
    copies = [
        pltpu.make_async_copy(
            p_ref.at[pl.ds(k * chunk, chunk), :, pl.ds(start, window)],
            buf.at[pl.ds(k * chunk, chunk)],
            sems.at[k],
        )
        for k in range(sems.shape[0])
    ]
    for copy in copies:
        copy.start()
    bits = slots.bit_length() - 1

    for p in range(owners):
        counts[p] = 0
    spilled = jnp.int32(0)
    for g in range(slots):
        owner = decode_slot[where[1] * slots + g] >> bits
        rank = counts[owner]
        counts[owner] = rank + 1
        placing[g] = owner * CAP + rank
        over = rank >= DIRECT
        leaving[g] = jnp.where(over, spilled, -1)
        spilled = spilled + over.astype(jnp.int32)
    pick = picker(row, start, piece, window)

    def clear(n, carry):
        counts[n] = 0
        return carry

    lax.fori_loop(0, owners * owners, clear, 0, unroll=16)
    first = where[1] * slots

    def look(k, spilled):
        after = []
        for p in range(owners):
            slot = decode_slot[p * slots + k]
            owner = slot >> bits
            rank = counts[p * owners + owner]
            counts[p * owners + owner] = rank + 1
            over = rank >= DIRECT
            ahead[p * (SPILL + 1) + jnp.where(over, jnp.minimum(spilled[p], SPILL), SPILL)] = owner
            inner = slot - first
            at = jnp.where((inner >= 0) & (inner < slots), inner, slots)
            coming[at] = jnp.where(over, spilled[p], -1)
            source[at] = p
            after.append(spilled[p] + over.astype(jnp.int32))
        return tuple(after)

    spilled = lax.fori_loop(0, slots, look, (jnp.int32(0),) * owners)
    for q in range(owners):
        counts[q] = 0
    for n in range(owners * SPILL):
        relay[n] = 0
    longest = jnp.int32(0)
    for p in range(owners):
        hopped = jnp.int32(0)
        for n in range(SPILL):
            owner = jnp.where(n < spilled[p], ahead[p * (SPILL + 1) + n], 0)
            entry = counts[owner]
            hops = (n < spilled[p]) & (entry < SPILL)
            counts[owner] = entry + hops.astype(jnp.int32)
            relay[jnp.where(hops, owner * SPILL + entry, owners * SPILL)] = p * SPILL + n
            code[p * (SPILL + 1) + n] = jnp.where(hops, entry, SPILL + n - hopped)
            hopped = hopped + hops.astype(jnp.int32)
        code[p * (SPILL + 1) + SPILL] = SPILL - hopped
        longest = jnp.maximum(longest, spilled[p] - hopped)
    rounds[0] = (longest + SPILL - 1) // SPILL

    def coded(p, n):
        found = code[p * (SPILL + 1) + jnp.clip(n, 0, SPILL)]
        return jnp.where(n < 0, -1, jnp.where(n < SPILL, found, found + n))

    def finish(n, carry):
        coming[n] = coded(source[n], coming[n])
        later[n] = coded(where[1], leaving[n])
        return carry

    lax.fori_loop(0, slots, finish, 0, unroll=4)

    for k, copy in enumerate(copies):
        copy.wait()

        def one(n, carry):
            g = k * chunk + n
            dest, rank = split(placing[g])
            cell = packed_piece(pick, buf[g])

            @pl.when(rank < DIRECT)
            def _():
                out_ref[dest, pl.ds(pl.multiple_of(rank * padded, STRIP), rows), :] = cell

            @pl.when((rank >= DIRECT) & (leaving[g] < SPILL))
            def _():
                at = DIRECT * padded + leaving[g] * STRIP
                for m in range(strips):
                    high = min(STRIP, rows - m * STRIP)
                    out_ref[m, pl.ds(pl.multiple_of(at, STRIP), high), :] = cell[
                        m * STRIP : m * STRIP + high
                    ]

            return carry

        lax.fori_loop(0, chunk, one, 0, unroll=8)


def pack_context(decode_slot, where, prompt_latent, piece, pool_count):
    slots, feature, _ = prompt_latent.shape
    rows = padded_rows(piece, feature)
    return pl.pallas_call(
        pack_context_kernel,
        out_shape=(
            jax.ShapeDtypeStruct((pool_count, DIRECT * rows + SPILL * STRIP, 128), BF16),
            jax.ShapeDtypeStruct((slots,), jnp.int32),
            jax.ShapeDtypeStruct((slots,), jnp.int32),
            jax.ShapeDtypeStruct((slots + 8,), jnp.int32),
            jax.ShapeDtypeStruct((pool_count * SPILL + 8,), jnp.int32),
            jax.ShapeDtypeStruct((1,), jnp.int32),
        ),
        in_specs=[SMEM_SPEC] * 2 + [ANY_SPEC],
        out_specs=(VMEM_SPEC,) + (SMEM_SPEC,) * 5,
        scratch_shapes=[
            pltpu.SMEM((slots,), jnp.int32),
            pltpu.SMEM((pool_count * pool_count,), jnp.int32),
            pltpu.SMEM((pool_count * (SPILL + 1),), jnp.int32),
            pltpu.SMEM((pool_count * (SPILL + 1),), jnp.int32),
            pltpu.SMEM((slots + 8,), jnp.int32),
            pltpu.VMEM((slots, feature, 256), BF16),
            pltpu.SemaphoreType.DMA((4,)),
        ],
        compiler_params=params(63),
        cost_estimate=cost(),
        name="pack_context",
    )(decode_slot, where, prompt_latent)


def pack_spill_kernel(turn, leaving, where, p_ref, spill_ref, buf, sem):
    feature, window = buf.shape
    piece = spill_ref.shape[1] * 128 // feature // 16 * 16
    row = where[0] * piece
    start = window_start(row, piece, window, p_ref.shape[2])
    pick = picker(row, start, piece, window)

    def one(g, carry):
        at = leaving[g] - SPILL - turn[0] * SPILL

        @pl.when((at >= 0) & (at < SPILL))
        def _():
            copy = pltpu.make_async_copy(p_ref.at[g, :, pl.ds(start, window)], buf, sem)
            copy.start()
            copy.wait()
            cell = packed_piece(pick, buf[...])
            spill_ref[at, : cell.shape[0], :] = cell

        return carry

    lax.fori_loop(0, p_ref.shape[0], one, 0)


def pack_spill(turn, leaving, where, prompt_latent, piece):
    slots, feature, _ = prompt_latent.shape
    return pl.pallas_call(
        pack_spill_kernel,
        out_shape=jax.ShapeDtypeStruct((SPILL, padded_rows(piece, feature), 128), BF16),
        in_specs=[SMEM_SPEC] * 3 + [ANY_SPEC],
        out_specs=VMEM_SPEC,
        scratch_shapes=[pltpu.VMEM((feature, 256), BF16), pltpu.SemaphoreType.DMA],
        compiler_params=params(),
        cost_estimate=cost(),
        name="pack_spill",
    )(turn, leaving, where, prompt_latent)


def unpack_piece(out_ref, row, packed, at, start, first_row, length):
    piece, feature = out_ref.shape[1:]
    blocks = feature // 128
    for b in range(blocks):
        out_ref[row, :, 128 * b : 128 * b + 128] = packed[at, pl.ds(start + b * piece, piece), :]
    last = packed[at, pl.ds(start + blocks * piece, piece // 2), :].astype(F32)
    last = jnp.concatenate([last[:, :64], last[:, 64:]], axis=0)
    out_ref[row, :, 128 * blocks :] = last.astype(BF16)

    @pl.when(length < first_row + piece)
    def _():
        whole = out_ref[row].astype(F32)
        position = first_row + lax.broadcasted_iota(jnp.int32, whole.shape, 0)
        out_ref[row] = jnp.where(position < length, whole, 0.0).astype(BF16)


def place_kernel(
    decode_slot, prompt_lengths, arrival, where, direct, out_ref, lengths, outbox, sems
):
    slots, piece, feature = out_ref.shape
    first = where[1] * slots

    def measure(p, carry):
        for k in range(slots):
            inner = decode_slot[p * slots + k] - first
            at = jnp.where((inner >= 0) & (inner < slots), inner, slots)
            lengths[at] = prompt_lengths[p * slots + k]
        return carry

    lax.fori_loop(0, direct.shape[0], measure, 0)
    padded = (direct.shape[1] - SPILL * STRIP) // DIRECT
    chunk = slots // sems.shape[0]

    def copy_out(k):
        part = pl.ds(k * chunk, chunk)
        return pltpu.make_async_copy(outbox.at[part], out_ref.at[part], sems.at[k])

    def one(j, carry):
        owner, rank = split(arrival[j])
        at = pl.multiple_of(jnp.minimum(rank, DIRECT - 1) * padded, STRIP)
        unpack_piece(outbox, j, direct, owner, at, where[0] * piece, lengths[j])
        return carry

    for k in range(sems.shape[0]):
        lax.fori_loop(k * chunk, k * chunk + chunk, one, 0, unroll=2)
        copy_out(k).start()
    for k in range(sems.shape[0]):
        copy_out(k).wait()


def place(decode_slot, prompt_lengths, arrival, where, direct, piece, feature):
    slots = arrival.shape[0] - 8
    return pl.pallas_call(
        place_kernel,
        out_shape=(
            jax.ShapeDtypeStruct((slots, piece, feature), BF16),
            jax.ShapeDtypeStruct((slots + 8,), jnp.int32),
        ),
        in_specs=[SMEM_SPEC] * 4 + [VMEM_SPEC],
        out_specs=(ANY_SPEC, SMEM_SPEC),
        scratch_shapes=[
            pltpu.VMEM((slots, piece, feature), BF16),
            pltpu.SemaphoreType.DMA((4,)),
        ],
        compiler_params=params(),
        cost_estimate=cost(bytes_accessed=12_000_000),
        name="place_context",
    )(decode_slot, prompt_lengths, arrival, where, direct)


def place_strips_kernel(
    coming, lengths, where, back, context, out_ref, inbox, whole, outbox, in_sems, out_sems
):
    slots, piece, feature = out_ref.shape
    strips = inbox.shape[1]

    def copy_in(e):
        source = back.at[pl.ds(0, strips), pl.ds(e * STRIP, STRIP), :]
        return pltpu.make_async_copy(source, inbox.at[e], in_sems.at[e])

    def copy_out(j, e):
        return pltpu.make_async_copy(outbox.at[e], out_ref.at[j], out_sems.at[e])

    for e in range(SPILL):
        copy_in(e).start()
    for e in range(SPILL):
        copy_in(e).wait()
        for m in range(strips):
            whole[e, m * STRIP : m * STRIP + STRIP, :] = inbox[e, m]

    def each(action):
        def step(j, carry):
            for e in range(SPILL):

                @pl.when(coming[j] == e)
                def _():
                    action(j, e)

            return carry

        lax.fori_loop(0, slots, step, 0)

    def work(j, e):
        unpack_piece(outbox, e, whole, e, 0, where[0] * piece, lengths[j])
        copy_out(j, e).start()

    each(work)
    each(lambda j, e: copy_out(j, e).wait())


def place_strips(coming, lengths, where, back, context):
    slots, piece, feature = context.shape
    strips = padded_rows(piece, feature) // STRIP
    return pl.pallas_call(
        place_strips_kernel,
        out_shape=jax.ShapeDtypeStruct(context.shape, BF16),
        in_specs=[SMEM_SPEC] * 3 + [ANY_SPEC] * 2,
        out_specs=ANY_SPEC,
        scratch_shapes=[
            pltpu.VMEM((SPILL, strips, STRIP, 128), BF16),
            pltpu.VMEM((SPILL, strips * STRIP, 128), BF16),
            pltpu.VMEM((SPILL, piece, feature), BF16),
            pltpu.SemaphoreType.DMA((SPILL,)),
            pltpu.SemaphoreType.DMA((SPILL,)),
        ],
        input_output_aliases={4: 0},
        compiler_params=params(),
        cost_estimate=cost(bytes_accessed=6_000_000),
        name="place_strips",
    )(coming, lengths, where, back, context)


def place_spill_kernel(
    turn, arrival, coming, lengths, where, spill, context, out_ref, inbox, outbox, sem
):
    slots, piece, feature = out_ref.shape

    def one(j, carry):
        at = coming[j] - SPILL - turn[0] * SPILL

        @pl.when((at >= 0) & (at < SPILL))
        def _():
            owner = split(arrival[j])[0]
            copy = pltpu.make_async_copy(
                spill.at[owner, jnp.clip(at, 0, SPILL - 1)], inbox.at[0], sem
            )
            copy.start()
            copy.wait()
            unpack_piece(outbox, 0, inbox, 0, 0, where[0] * piece, lengths[j])
            copy = pltpu.make_async_copy(outbox.at[0], out_ref.at[j], sem)
            copy.start()
            copy.wait()

        return carry

    lax.fori_loop(0, slots, one, 0)


def place_spill(turn, arrival, coming, lengths, where, spill, context):
    return pl.pallas_call(
        place_spill_kernel,
        out_shape=jax.ShapeDtypeStruct(context.shape, BF16),
        in_specs=[SMEM_SPEC] * 5 + [ANY_SPEC] * 2,
        out_specs=ANY_SPEC,
        scratch_shapes=[
            pltpu.VMEM((1,) + spill.shape[-2:], BF16),
            pltpu.VMEM((1,) + context.shape[1:], BF16),
            pltpu.SemaphoreType.DMA,
        ],
        input_output_aliases={6: 0},
        compiler_params=params(),
        cost_estimate=cost(),
        name="place_spill",
    )(turn, arrival, coming, lengths, where, spill, context)


def attention_kernel(
    placing, lengths, where, payload_hbm, p_hbm, w_uk_hbm, w_uv_hbm, w_out_hbm,
    given_ref, kept_ref,
    payload, prompt, w_uk, w_uv, w_out,
    q_nope, q_rope, acc, fresh, tails, fresh_score, total, head_out, sems,
):
    steps = 4
    heads, latent, nope = w_uk.shape
    slots, feature, span = prompt.shape
    chunks = latent // 128
    per_step = slots * heads
    many = slots * steps
    scale = 1.0 / math.sqrt(nope + ROPE)
    first = where[1] * slots
    copy_payload = pltpu.make_async_copy(payload_hbm, payload, sems.at[0])
    copy_uk = pltpu.make_async_copy(w_uk_hbm, w_uk, sems.at[1])
    copy_uv = pltpu.make_async_copy(w_uv_hbm, w_uv, sems.at[2])
    copy_out = pltpu.make_async_copy(w_out_hbm, w_out, sems.at[3])

    def copy_prompt(k):
        part = pl.ds(k * GROUP, GROUP)
        return pltpu.make_async_copy(p_hbm.at[part], prompt.at[part], sems.at[4 + k])

    copy_payload.start()
    copy_uk.start()
    for k in range(slots // GROUP):
        copy_prompt(k).start()
    copy_uv.start()
    copy_out.start()

    def spread(ref, i, lead=()):
        return jnp.concatenate(
            [
                ref[(*lead, pl.ds(pl.multiple_of(per_step * s + heads * i, 8), heads), slice(None))]
                for s in range(steps)
            ],
            axis=0,
        )

    def collect(ref, i, value, lead=()):
        for s in range(steps):
            ref[(*lead, pl.ds(pl.multiple_of(per_step * s + heads * i, 8), heads), slice(None))] = (
                value[heads * s : heads * s + heads]
            )

    copy_payload.wait()
    tails[...] = payload[:, 256:264, :].astype(F32).reshape(tails.shape)

    def unpack(i, carry):
        dest, rank = split(placing[i])
        cell = payload[dest, pl.ds(pl.multiple_of(rank * 64, 64), 64), :].astype(F32)
        collect(q_nope, i, cell[:32])
        rope = jnp.concatenate([cell[32:48, :64], cell[32:48, 64:]], axis=0)
        collect(q_rope, i, jnp.concatenate([rope, jnp.zeros_like(rope)], axis=1))
        for b in range(chunks):
            fresh[b, pl.ds(steps * i, steps), :] = cell[48 + 4 * b : 52 + 4 * b]
        last = tails[pl.ds(dest * 8 + rank * 2, 2), :]
        last = jnp.concatenate([last[:, :64], last[:, 64:]], axis=0)
        fresh[chunks, pl.ds(steps * i, steps), :] = jnp.concatenate(
            [last, jnp.zeros_like(last)], axis=1
        )
        return carry

    lax.fori_loop(0, slots, unpack, 0, unroll=8)
    copy_uk.wait()
    for h in range(heads):
        rows = pl.ds(h, many, stride=heads)
        a = lax.dot_general(
            q_nope[rows, :].astype(BF16), w_uk[h], NT, preferred_element_type=F32
        )
        a = a.astype(BF16).astype(F32)
        for c in range(chunks):
            acc[c, rows, :] = a[:, 128 * c : 128 * c + 128]
    keys = jnp.concatenate([fresh[b] for b in range(chunks + 1)], axis=1).astype(BF16)

    def score(k, carry):
        rows = pl.ds(pl.multiple_of(k * 128, 128), 128)
        q = jnp.concatenate(
            [acc[c, rows, :] for c in range(chunks)] + [q_rope[rows, :]], axis=1
        ).astype(BF16)
        fresh_score[rows, :] = scale * lax.dot_general(q, keys, NT, preferred_element_type=F32)
        return carry

    lax.fori_loop(0, per_step * steps // 128, score, 0, unroll=2)

    def one(i):
        q = jnp.concatenate(
            [spread(acc, i, (c,)) for c in range(chunks)] + [spread(q_rope, i)[:, :ROPE]], axis=1
        ).astype(BF16)
        s_prompt = scale * jnp.dot(q, prompt[i], preferred_element_type=F32)
        s_fresh = spread(fresh_score, i)
        column = lax.broadcasted_iota(jnp.int32, s_prompt.shape, 1)
        s_prompt = jnp.where(column < lengths[first + i], s_prompt, FLOOR)
        step_of = lax.broadcasted_iota(jnp.int32, s_fresh.shape, 0) // heads
        column = lax.broadcasted_iota(jnp.int32, s_fresh.shape, 1) - steps * i
        s_fresh = jnp.where((column >= 0) & (column <= step_of), s_fresh, FLOOR)
        peak = jnp.maximum(
            jnp.max(s_prompt, axis=1, keepdims=True), jnp.max(s_fresh, axis=1, keepdims=True)
        )
        w_prompt = jnp.exp(s_prompt - peak)
        w_fresh = jnp.exp(s_fresh - peak)
        sums = jnp.sum(w_prompt, axis=1, keepdims=True) + jnp.sum(w_fresh, axis=1, keepdims=True)
        mixed = lax.dot_general(
            w_prompt.astype(BF16), prompt[i, :latent], NT, preferred_element_type=F32
        )
        for c in range(chunks):
            collect(acc, i, mixed[:, 128 * c : 128 * c + 128], (c,))
        collect(fresh_score, i, w_fresh)
        collect(total, i, jnp.broadcast_to(sums, s_fresh.shape))

    def attend(k, carry):
        copy_prompt(k).wait()
        for n in range(GROUP):
            one(k * GROUP + n)
        return carry

    lax.fori_loop(0, slots // GROUP, attend, 0)

    values = jnp.concatenate([fresh[b] for b in range(chunks)], axis=1).astype(BF16)
    copy_uv.wait()
    for h in range(heads):
        rows = pl.ds(h, many, stride=heads)
        mixed = jnp.dot(fresh_score[rows, :].astype(BF16), values, preferred_element_type=F32)
        mixed = mixed + jnp.concatenate([acc[c, rows, :] for c in range(chunks)], axis=1)
        part = 1.0 / total[rows, :]
        mixed = (mixed * jnp.concatenate([part] * chunks, axis=1)).astype(BF16)
        head_out[:, h * 128 : h * 128 + 128] = jnp.dot(
            mixed, w_uv[h], preferred_element_type=F32
        ).astype(BF16)
    copy_out.wait()
    half = many // 2
    core = where[0] % 2
    mine = head_out[pl.ds(pl.multiple_of(core * half, half), half), :]
    theirs = head_out[pl.ds(pl.multiple_of((1 - core) * half, half), half), :]
    both = jnp.concatenate([theirs, mine], axis=0)
    for b in range(w_out.shape[1] // 512):
        at_b = slice(b * 512, b * 512 + 512)
        summed = jnp.dot(both, w_out[:, at_b], preferred_element_type=F32)
        given_ref[:, at_b] = summed[:half].astype(BF16)
        kept_ref[:, at_b] = summed[half:].astype(BF16)


def attention(placing, lengths, where, payload, prompt_latent, w_uk, w_uv, w_out, steps):
    slots, feature, span = prompt_latent.shape
    heads, latent, nope = w_uk.shape
    width = w_out.shape[1]
    rows = steps * slots * heads
    half = steps * slots // 2
    chunks = latent // 128
    return pl.pallas_call(
        attention_kernel,
        out_shape=(
            jax.ShapeDtypeStruct((half, width), BF16),
            jax.ShapeDtypeStruct((half, width), BF16),
        ),
        in_specs=[SMEM_SPEC] * 3 + [ANY_SPEC] * 5,
        out_specs=(VMEM_SPEC, VMEM_SPEC),
        scratch_shapes=[
            pltpu.VMEM(payload.shape, BF16),
            pltpu.VMEM(prompt_latent.shape, BF16),
            pltpu.VMEM(w_uk.shape, BF16),
            pltpu.VMEM(w_uv.shape, BF16),
            pltpu.VMEM(w_out.shape, BF16),
            pltpu.VMEM((rows, 128), F32),
            pltpu.VMEM((rows, 128), F32),
            pltpu.VMEM((chunks, rows, 128), F32),
            pltpu.VMEM((chunks + 1, steps * slots, 128), F32),
            pltpu.VMEM((payload.shape[0] * 8, 128), F32),
            pltpu.VMEM((rows, 128), F32),
            pltpu.VMEM((rows, 128), F32),
            pltpu.VMEM((steps * slots, heads * 128), BF16),
            pltpu.SemaphoreType.DMA((4 + slots // GROUP,)),
        ],
        compiler_params=params(60),
        cost_estimate=cost(),
        name="attention",
    )(placing, lengths, where, payload, prompt_latent, w_uk, w_uv, w_out)


def share_kernel(where, kept, swapped, mine, *parts):
    block = mine.shape[1]
    z = where[0] >> 1
    for d, part in enumerate((mine,) + parts):
        at = pl.ds(pl.multiple_of((z ^ d) * block, 128), block)
        part[...] = (kept[:, at].astype(F32) + swapped[:, at].astype(F32)).astype(part.dtype)


def share(where, kept, swapped, z_count):
    rows, width = kept.shape
    block = width // z_count
    return pl.pallas_call(
        share_kernel,
        out_shape=(jax.ShapeDtypeStruct((rows, block), F32),)
        + (jax.ShapeDtypeStruct((rows, block), BF16),) * (z_count - 1),
        in_specs=[SMEM_SPEC] + [VMEM_SPEC] * 2,
        out_specs=(VMEM_SPEC,) * z_count,
        compiler_params=params(),
        cost_estimate=cost(),
        name="share",
    )(where, kept, swapped)


def pack_back_kernel(placing, relay, direct, mine, *rest):
    parts, (out_ref, strips, total, rows, sem) = rest[:-5], rest[-5:]
    slots = placing.shape[0]
    blocks = mine.shape[1] // 128
    steps = mine.shape[0] // slots
    hop = SPILL * STRIP
    fetch = pltpu.make_async_copy(
        direct.at[:, pl.ds(direct.shape[1] - hop, hop), :], strips, sem
    )
    fetch.start()
    whole = mine[...]
    for part in parts:
        whole = whole + part[...].astype(F32)
    for b in range(blocks):
        total[b] = whole[:, 128 * b : 128 * b + 128]
    def one(i, carry):
        dest, rank = split(placing[i])
        for s in range(steps):
            for b in range(blocks):
                at = dest * (8 * blocks) + 8 * b + steps * rank + s
                rows[pl.ds(at, 1), :] = total[b, pl.ds(slots * s + i, 1), :]
        return carry

    lax.fori_loop(0, slots, one, 0, unroll=8)
    out_ref[:, hop:, :] = rows[...].reshape(out_ref.shape[0], 8 * blocks, 128).astype(BF16)
    fetch.wait()
    for q in range(out_ref.shape[0]):
        for e in range(SPILL):
            came = relay[q * SPILL + e]
            at = pl.multiple_of((came % SPILL) * STRIP, STRIP)
            out_ref[q, e * STRIP : e * STRIP + STRIP, :] = strips[
                came // SPILL, pl.ds(at, STRIP), :
            ]


def pack_back(placing, relay, direct, mine, parts):
    pool_count = direct.shape[0]
    blocks = mine.shape[1] // 128
    hop = SPILL * STRIP
    return pl.pallas_call(
        pack_back_kernel,
        out_shape=jax.ShapeDtypeStruct((pool_count, hop + 8 * blocks, 128), BF16),
        in_specs=[SMEM_SPEC] * 2 + [ANY_SPEC] + [VMEM_SPEC] * (1 + len(parts)),
        out_specs=VMEM_SPEC,
        scratch_shapes=[
            pltpu.VMEM((pool_count, hop, 128), BF16),
            pltpu.VMEM((blocks, mine.shape[0], 128), F32),
            pltpu.VMEM((pool_count * 8 * blocks, 128), F32),
            pltpu.SemaphoreType.DMA,
        ],
        compiler_params=params(),
        cost_estimate=cost(),
        name="pack_back",
    )(placing, relay, direct, mine, *parts)


def unpack_back_kernel(steps, arrival, packed, out_ref, rows, total):
    slots = out_ref.shape[0] // steps
    blocks = out_ref.shape[1] // 128
    first = packed.shape[1] - 8 * blocks
    rows[...] = packed[:, first:, :].astype(F32).reshape(rows.shape)

    def one(j, carry):
        owner, rank = split(arrival[j])
        for b in range(blocks):
            at = owner * (8 * blocks) + 8 * b + steps * rank
            total[b, pl.ds(steps * j, steps), :] = rows[pl.ds(at, steps), :]
        return carry

    lax.fori_loop(0, slots, one, 0, unroll=8)
    for b in range(blocks):
        out_ref[:, 128 * b : 128 * b + 128] = total[b].astype(BF16)


def unpack_back(arrival, packed, steps, slots, block):
    return pl.pallas_call(
        functools.partial(unpack_back_kernel, steps),
        out_shape=jax.ShapeDtypeStruct((steps * slots, block), BF16),
        in_specs=[SMEM_SPEC, VMEM_SPEC],
        out_specs=VMEM_SPEC,
        scratch_shapes=[
            pltpu.VMEM((packed.shape[0] * 8 * (block // 128), 128), F32),
            pltpu.VMEM((block // 128, steps * slots, 128), F32),
        ],
        compiler_params=params(),
        cost_estimate=cost(),
        name="unpack_back",
    )(arrival, packed)


def assemble_kernel(where, *rest):
    parts, (out_ref, part, whole) = rest[:-3], rest[-3:]
    slots, steps, width = out_ref.shape
    z_count = len(parts) // 2
    block = width // z_count
    core, z = where[0] & 1, where[0] >> 1
    for n, ref in enumerate(parts):
        side = core if n < z_count else 1 - core
        start = (z ^ (n % z_count)) * (block // 128)
        for b in range(block // 128):
            part[...] = ref[:, 128 * b : 128 * b + 128].astype(F32)
            for s in range(steps // 2):
                whole[start + b, pl.ds((steps // 2) * side + s, slots, stride=steps), :] = part[
                    pl.ds(s, slots, stride=steps // 2), :
                ]
    for b in range(width // 128):
        out_ref[:, :, 128 * b : 128 * b + 128] = (
            whole[b].reshape(slots, steps, 128).astype(BF16)
        )


def assemble(where, parts, slots, steps, width):
    return pl.pallas_call(
        assemble_kernel,
        out_shape=jax.ShapeDtypeStruct((slots, steps, width), BF16),
        in_specs=[SMEM_SPEC] + [VMEM_SPEC] * len(parts),
        out_specs=VMEM_SPEC,
        scratch_shapes=[
            pltpu.VMEM((parts[0].shape[0], 128), F32),
            pltpu.VMEM((width // 128, slots * steps, 128), F32),
        ],
        compiler_params=params(),
        cost_estimate=cost(),
        name="assemble",
    )(where, *parts)


def exchange(x):
    return lax.all_to_all(x, "pool", split_axis=0, concat_axis=0, tiled=True)


def body(prompt_latent, prompt_lengths, decode_slot, new_latent, queries, w_uk, w_uv, w_out):
    pool_count = lax.axis_size("pool")
    tp_count = lax.axis_size("tp")
    tp_index = lax.axis_index("tp")
    latent_t = prompt_latent.transpose(0, 2, 1)
    steps, slots, heads, width = queries.shape
    span, feature = prompt_latent.shape[1:]
    piece = span // tp_count
    out_width = w_out.shape[1]
    z_count = tp_count // 2
    where = jnp.stack([tp_index, lax.axis_index("pool")]).astype(jnp.int32)
    swap = [(i, i ^ 1) for i in range(tp_count)]
    hops = [[(i, i ^ (2 * d)) for i in range(tp_count)] for d in range(1, z_count)]

    payload, arrival = pack_queries(decode_slot, where, queries, new_latent, pool_count)
    payload = exchange(payload)
    direct, placing, leaving, coming, relay, rounds = pack_context(
        decode_slot, where, latent_t, piece, pool_count
    )
    payload, direct = lax.optimization_barrier((payload, direct))
    direct = exchange(direct)

    given, kept = attention(
        placing, prompt_lengths, where, payload, latent_t, w_uk, w_uv, w_out, steps
    )

    swapped = lax.ppermute(given, "tp", swap)
    mine, *parts = share(where, kept, swapped, z_count)
    parts = [lax.ppermute(part, "tp", hop) for part, hop in zip(parts, hops)]

    back = exchange(pack_back(placing, relay, direct, mine, parts))
    context, lengths = place(
        decode_slot, prompt_lengths, arrival, where, direct, piece, feature
    )
    back, context = lax.optimization_barrier((back, context))
    own = unpack_back(arrival, back, steps // 2, slots, out_width // z_count)
    parts = [own] + [lax.ppermute(own, "tp", hop) for hop in hops]
    swapped = [lax.ppermute(own, "tp", swap)]
    context = place_strips(coming, lengths, where, back, context)

    def more(state):
        turn, context = state
        spill = pack_spill(turn, leaving, where, latent_t, piece)
        spill = exchange(jnp.broadcast_to(spill[None], (pool_count,) + spill.shape))
        context = place_spill(turn, arrival, coming, lengths, where, spill, context)
        return turn + 1, context

    context = lax.while_loop(
        lambda state: state[0][0] < rounds[0], more, (jnp.zeros((1,), jnp.int32), context)
    )[1]
    context, *parts = lax.optimization_barrier((context, *parts))
    parts = parts + swapped + [lax.ppermute(part, "tp", swap) for part in parts[1:]]
    decoded = assemble(where, parts, slots, steps, out_width)
    return decoded, context


def solution(mesh):
    in_specs = (
        P("pool", None, None),
        P(),
        P(),
        P(None, "pool", None),
        P(None, "pool", "tp", None),
        P("tp", None, None),
        P("tp", None, None),
        P("tp", None),
    )
    out_specs = (P("pool", None, None), P("pool", "tp", None))
    return jax.shard_map(body, mesh=mesh, in_specs=in_specs, out_specs=out_specs, check_vma=False)
```
